256 devices in a mesh: blk: 4 (over x_lo, core), group: 64 (over x_hi, y, z).
Axes of the slice: x: 4 (x_hi: 2, x_lo: 2; x = x_hi * 2 + x_lo), y: 4, z: 8, core: 2. Of those that a mesh axis runs over, the one named last changes fastest.
Arguments:
- image_feats: bfloat16 [10240, 1152], P('group'), may hold values from -2 to 2
- text_feats: bfloat16 [10240, 1152], P(('blk', 'group')), may hold values from -2 to 2
- image_proj: bfloat16 [1152, 1152], replicated, may hold values from -2 to 2
- text_proj: bfloat16 [1152, 1152], replicated, may hold values from -2 to 2
- logit_scale: float32 [1], replicated, may hold values from 10 to 30
- logit_bias: float32 [1], replicated, may hold values from -9 to -5
Outputs:
- image_grad: float32 [10240, 1152], P('group')
- text_grad: float32 [10240, 1152], P(('blk', 'group'))
- image_proj_grad: float32 [1152, 1152], P('group', 'blk')
- text_proj_grad: float32 [1152, 1152], P('group', 'blk')
The draws below stay inside these ranges and needn't reach their ends.
All inputs are finite; a program needn't handle non-finite values.
Results may differ from the reference program's by a relative error of at most 0.005.
Values may be sent and summed in bfloat16 or wider, within the bound.
A program may use at most 128 MiB of HBM per device.

```python
import math
import jax
import jax.numpy as jnp
from jax import lax

D = 1152
BATCH = 10240


def pair_common(key, spread):
    key = jax.random.fold_in(key, 501)
    key_label, key_center, key_own, key_scale = jax.random.split(key, 4)
    clusters = max(BATCH // 16, 2)
    labels = jax.random.randint(key_label, (BATCH,), 0, clusters)
    centers = jax.random.normal(key_center, (clusters, D), jnp.float32)
    own_part = jax.random.normal(key_own, (BATCH, D), jnp.float32)
    row_scale = jnp.exp(jax.random.uniform(key_scale, (BATCH, 1), jnp.float32, -spread, spread))
    common = 0.65 * centers[labels] + 0.72 * own_part
    return (common, row_scale)


def proj_common(key):
    key = jax.random.fold_in(key, 601)
    key_base, key_cols = jax.random.split(key, 2)
    base = jax.random.normal(key_base, (D, D), jnp.float32)
    col_scale = jnp.exp(jax.random.uniform(key_cols, (1, D), jnp.float32, 0.0, math.log(10.0)))
    return (base, col_scale)


def draw_image_feats(key, part):
    spread = 0.5 * math.log(10.0)
    common, row_scale = pair_common(key, spread)
    key = jax.random.fold_in(key, 11)
    noise = 0.55 * jax.random.normal(key, (BATCH, D), jnp.float32)
    feats = jnp.clip(0.1 * row_scale * (common + noise), -2.0, 2.0)
    return feats.astype(jnp.bfloat16)


def draw_text_feats(key, part):
    spread = 0.5 * math.log(10.0)
    common, row_scale = pair_common(key, spread)
    key = jax.random.fold_in(key, 12)
    noise = 0.55 * jax.random.normal(key, (BATCH, D), jnp.float32)
    feats = jnp.clip(0.1 * row_scale * (common + noise), -2.0, 2.0)
    return feats.astype(jnp.bfloat16)


def draw_image_proj(key, part):
    base, col_scale = proj_common(key)
    key = jax.random.fold_in(key, 21)
    extra = jax.random.normal(key, (D, D), jnp.float32)
    factor = 1.0 / (math.sqrt(99.0 / (2.0 * math.log(10.0))) * math.sqrt(1.25 * D))
    proj = jnp.clip((base + 0.5 * extra) * col_scale * factor, -2.0, 2.0)
    return proj.astype(jnp.bfloat16)


def draw_text_proj(key, part):
    base, col_scale = proj_common(key)
    key = jax.random.fold_in(key, 22)
    extra = jax.random.normal(key, (D, D), jnp.float32)
    factor = 1.0 / (math.sqrt(99.0 / (2.0 * math.log(10.0))) * math.sqrt(1.25 * D))
    proj = jnp.clip((base + 0.5 * extra) * col_scale * factor, -2.0, 2.0)
    return proj.astype(jnp.bfloat16)


def setup_inputs(seed: int = 0) -> dict:
    key_of = jax.random.split(jax.random.key(seed), 7)
    image_feats = draw_image_feats(jax.random.fold_in(key_of[6], 71), 0)
    text_feats = draw_text_feats(jax.random.fold_in(key_of[6], 71), 0)
    image_proj = draw_image_proj(jax.random.fold_in(key_of[6], 71), 0)
    text_proj = draw_text_proj(jax.random.fold_in(key_of[6], 71), 0)
    logit_scale = jnp.clip(jnp.exp(jax.random.uniform(key_of[4], (1,), jnp.float32, math.log(10.0), math.log(30.0))), 10.0, 30.0)
    logit_bias = jnp.clip(jax.random.uniform(key_of[5], (1,), jnp.float32, -9.0, -5.0), -9.0, -5.0)
    return {"image_feats": image_feats, "text_feats": text_feats, "image_proj": image_proj, "text_proj": text_proj, "logit_scale": logit_scale, "logit_bias": logit_bias}


def unit_rows(embed):
    norm = jnp.sqrt(lax.optimization_barrier(jnp.sum(embed * embed, axis=-1, keepdims=True)) + 1e-06)
    return (embed / norm, norm)

def back_rows(embed, upstream):
    unit, norm = unit_rows(embed)
    return (upstream - unit * lax.optimization_barrier(jnp.sum(unit * upstream, axis=-1, keepdims=True))) / norm

def reference(image_feats, text_feats, image_proj, text_proj, logit_scale, logit_bias):
    scale = logit_scale[0]
    shift_bias = logit_bias[0]
    img_emb = jnp.dot(image_feats, image_proj, preferred_element_type=jnp.float32)
    txt_emb = jnp.dot(text_feats, text_proj, preferred_element_type=jnp.float32)
    img_unit = unit_rows(img_emb)[0].astype(jnp.bfloat16)
    txt_unit = unit_rows(txt_emb)[0].astype(jnp.bfloat16)
    logits = scale * jnp.dot(img_unit, txt_unit.T, preferred_element_type=jnp.float32) + shift_bias
    index_rows = jnp.arange(logits.shape[0], dtype=jnp.int32)
    signs = jnp.where(index_rows[:, None] == index_rows[None, :], jnp.float32(1.0), jnp.float32(-1.0))
    coeff = (-signs * jax.nn.sigmoid(-signs * logits)).astype(jnp.bfloat16)
    img_unit_grad = scale * jnp.dot(coeff, txt_unit, preferred_element_type=jnp.float32)
    txt_unit_grad = scale * jnp.dot(coeff.T, img_unit, preferred_element_type=jnp.float32)
    img_emb_grad = back_rows(img_emb, img_unit_grad).astype(jnp.bfloat16)
    txt_emb_grad = back_rows(txt_emb, txt_unit_grad).astype(jnp.bfloat16)
    image_grad = jnp.dot(img_emb_grad, image_proj.T, preferred_element_type=jnp.float32)
    text_grad = jnp.dot(txt_emb_grad, text_proj.T, preferred_element_type=jnp.float32)
    image_proj_grad = jnp.dot(image_feats.T, img_emb_grad, preferred_element_type=jnp.float32)
    text_proj_grad = jnp.dot(text_feats.T, txt_emb_grad, preferred_element_type=jnp.float32)
    return (image_grad, text_grad, image_proj_grad, text_proj_grad)
```

```python
import jax
import jax.numpy as jnp
from jax import lax
from jax.experimental import pallas as pl
from jax.experimental.pallas import tpu as pltpu
from jax.sharding import PartitionSpec as P

D = 1152
MESH = pl.DeviceIdType.MESH
BF = jnp.bfloat16
F32 = jnp.float32
NT = (((1,), (1,)), ((), ()))
TN = (((0,), (0,)), ((), ()))


def dot(a, b):
    return jnp.dot(a, b, preferred_element_type=F32)


def dot_nt(a, b):
    return lax.dot_general(a, b, NT, preferred_element_type=F32)


def dot_tn(a, b):
    return lax.dot_general(a, b, TN, preferred_element_type=F32)


def row_norm(e):
    return jnp.sqrt(jnp.sum(e * e, axis=-1, keepdims=True) + 1e-06)


def back_rows(e, g):
    norm = row_norm(e)
    u = e / norm
    return (g - u * jnp.sum(u * g, axis=-1, keepdims=True)) / norm


def quarters(rows):
    parts = []
    for q in range(4):
        turned = rows if q == 0 else pltpu.roll(rows, D - 288 * q, 1)
        parts.append(turned[:, :384])
    return parts


def kernel(
    scale_ref, bias_ref, ifeat_ref, tfeat_ref, iproj_ref, tproj_ref,
    igrad_ref, tgrad_ref, iw_ref, tw_ref,
    tfbuf, iemb, temb, iset, tset, coeff, ipart, tpart, sib_out, sib_in,
    tsend, trecv, side, side_in, irecv, egath, fsend, frecv, gsend, grecv,
    wsend, wrecv,
    s_tf, r_tf, s_img, r_img, s_txt, r_txt, s_fw, r_fw, s_sib, r_sib, s_tr, r_tr,
    s_sd, r_sd, s_ir, r_ir, s_eg, r_eg, s_fe, r_fe, s_gr, r_gr, s_w, r_w,
):
    bl = lax.axis_index("blk")
    gr = lax.axis_index("group")
    xl, c = bl // 2, bl % 2
    xh, y, z = gr // 32, (gr // 8) % 4, gr % 8
    x = 2 * xh + xl
    sib = 1 - c
    yh, yl = y // 2, y % 2
    scale = scale_ref[0]
    bias = bias_ref[0]

    def dev(x_, y_, z_, c_):
        return ((x_ % 2) * 2 + c_, ((x_ // 2) * 4 + y_) * 8 + z_)

    def rc(src, dst, ss, rs, to):
        return pltpu.make_async_remote_copy(
            src_ref=src, dst_ref=dst, send_sem=ss, recv_sem=rs,
            device_id=to, device_id_type=MESH,
        )

    sibling = dev(x, y, z, sib)

    barrier = pltpu.get_barrier_semaphore()

    def greet(to):
        pl.semaphore_signal(barrier, inc=1, device_id=to, device_id_type=MESH)

    greet(sibling)
    greet(dev(x + 1 - 2 * xl, y, z, sib))

    @pl.loop(1, 8)
    def _(m):
        greet(dev(x, y, (z + m) % 8, c))

    @pl.loop(1, 16)
    def _(k):
        greet(dev((x + k // 4) % 4, (y + k % 4) % 4, z, c))

    @pl.loop(0, 16)
    def _(k):
        y_, z_ = 2 * yh + k // 8, (z + k % 8) % 8

        @pl.when(jnp.logical_not((c == yl) & (k == 8 * yl)))
        def _():
            greet(dev(x, y_, z_, yl))

        @pl.when(jnp.logical_not((c == yl) & (k == 8 * c)))
        def _():
            greet(dev(x, 2 * yh + c, z_, k // 8))

    total = 1 + 1 + 7 + 15 + 32 - 2 * jnp.where(c == yl, 1, 0)

    tfeats = tfeat_ref[...].astype(F32)
    tfbuf[c] = tfeats
    pl.semaphore_wait(barrier, total)

    tf_copy = rc(tfbuf.at[c], tfbuf.at[c], s_tf, r_tf, sibling)
    tf_copy.start()

    emb = dot(ifeat_ref[pl.ds(pl.multiple_of(80 * c, 16), 80), :], iproj_ref[...])
    iemb[...] = emb
    iset[pl.ds(0, 80), :] = (emb / row_norm(emb)).astype(BF)

    def img_copy(j):
        h, dy = j // 4, j % 4
        x_ = x + h * (3 - 2 * x)
        rows = pl.ds(pl.multiple_of(80 * j, 16), 80)
        return rc(
            iset.at[pl.ds(0, 80)], iset.at[rows], s_img.at[j], r_img.at[j],
            dev(x_, (y + dy) % 4, z, c),
        )

    @pl.loop(1, 8)
    def _(j):
        img_copy(j).start()

    rc(tfbuf.at[sib], tfbuf.at[sib], s_tf, r_tf, sibling).wait_recv()
    tboth = tfbuf[...].reshape(80, D).astype(BF)
    emb = dot(tboth, tproj_ref[...])
    temb[...] = emb
    tset[pl.ds(0, 80), :] = (emb / row_norm(emb)).astype(BF)

    def txt_copy(m):
        rows = pl.ds(pl.multiple_of(80 * m, 16), 80)
        return rc(
            tset.at[pl.ds(0, 80)], tset.at[rows], s_txt.at[m], r_txt.at[m],
            dev(x, y, (z + m) % 8, c),
        )

    def fw_copy(m):
        rows = pl.ds(pl.multiple_of(80 * m, 16), 80)
        return rc(tset.at[rows], tset.at[rows], s_fw.at[m], r_fw.at[m], sibling)

    @pl.loop(0, 4)
    def _(i):
        @pl.when((c == 1) | (i > 0))
        def _():
            txt_copy(4 * c + i).start()

    iwin = ifeat_ref[pl.ds(pl.multiple_of(80 * c + 32 * xl, 16), 48), :].astype(F32)
    twin = jnp.concatenate([tfeats, jnp.zeros((8, D), F32)], axis=0)
    for q, (a, b) in enumerate(zip(quarters(iwin), quarters(twin))):
        fsend[q, :, 0:384] = a.astype(BF)
        fsend[q, :, 384:768] = b.astype(BF)
    frecv[0] = fsend[2 * xh + yh]

    def fe_copy(k):
        x_, y_ = (x + k // 4) % 4, (y + k % 4) % 4
        return rc(
            fsend.at[2 * (x_ // 2) + y_ // 2], frecv.at[k], s_fe.at[k], r_fe.at[k],
            dev(x_, y_, z, c),
        )

    @pl.loop(0, 4)
    def _(i):
        @pl.when((c == 1) | (i > 0))
        def _():
            txt_copy(4 * c + i).wait_recv()
            fw_copy(4 * c + i).start()

    @pl.loop(0, 4)
    def _(i):
        @pl.when((c == 0) | (i > 0))
        def _():
            fw_copy(4 * sib + i).wait_recv()

    @pl.loop(1, 8)
    def _(j):
        img_copy(j).wait_recv()

    @pl.loop(1, 16)
    def _(k):
        fe_copy(k).start()

    lane = lax.broadcasted_iota(jnp.int32, (1, 640), 1)
    slot = jnp.zeros((1, 640), jnp.int32)
    for m in range(1, 8):
        slot = slot + jnp.where(lane >= 80 * m, 1, 0)
    rest = lane - 80 * slot
    core = jnp.where(rest >= 40, 1, 0)
    tz = z - slot
    tz = jnp.where(tz < 0, tz + 8, tz)
    tidx = ((2 * xl + core) * 64 + (xh * 4 + y) * 8 + tz) * 40 + rest - 40 * core
    row80 = lax.broadcasted_iota(jnp.int32, (80, 1), 0)
    for h in range(2):
        logits = dot_nt(iset[pl.ds(320 * h, 320), :], tset[...])
        logits = scale * logits + bias
        hi = xh + h * (1 - 2 * xh)
        iidx = jnp.concatenate(
            [
                ((hi * 4 + (y + 4 - dy) % 4) * 8 + z) * 160 + 80 * c + row80
                for dy in range(4)
            ],
            axis=0,
        )
        same = iidx == tidx
        neg = jnp.where(same, logits, -logits)
        sig = 1.0 / (1.0 + jnp.exp(neg))
        coeff[pl.ds(320 * h, 320), :] = jnp.where(same, -sig, sig).astype(BF)

    for n in range(3):
        cols = pl.ds(384 * n, 384)
        tpart[:, cols] = dot_tn(coeff[...], iset[:, cols])
    sib_out[...] = tpart[pl.ds(pl.multiple_of(320 * sib, 16), 320), :].astype(BF)
    sib_copy = rc(sib_out, sib_in, s_sib, r_sib, sibling)
    sib_copy.start()

    for n in range(3):
        cols = pl.ds(384 * n, 384)
        ipart[:, cols] = dot(coeff[...], tset[:, cols]).astype(BF)

    def ir_copy(k):
        x_, dy = (x + k // 4) % 4, (4 - k % 4) % 4
        h = jnp.where(x_ // 2 == xh, 0, 1)
        rows = pl.ds(pl.multiple_of(80 * (4 * h + dy) + 32 * (x_ % 2), 16), 48)
        return rc(
            ipart.at[rows], irecv.at[k], s_ir.at[k], r_ir.at[k],
            dev(x_, (y + k % 4) % 4, z, c),
        )

    @pl.loop(1, 16)
    def _(k):
        ir_copy(k).start()

    sib_copy.wait_recv()

    def tr_copy(i):
        rows = pl.ds(pl.multiple_of(80 * i, 16), 80)
        return rc(
            tsend.at[rows], trecv.at[rows], s_tr.at[i], r_tr.at[i],
            dev(x, y, (z + 8 - (4 * c + i)) % 8, c),
        )

    @pl.loop(0, 4)
    def _(i):
        rows = pl.ds(pl.multiple_of(80 * i, 16), 80)
        mine = tpart[pl.ds(pl.multiple_of(320 * c + 80 * i, 16), 80), :]
        tsend[rows, :] = (mine + sib_in[rows, :].astype(F32)).astype(BF)

        @pl.when((c == 1) | (i > 0))
        def _():
            tr_copy(i).start()

    @pl.when(c == 0)
    def _():
        trecv[pl.ds(0, 80), :] = tsend[pl.ds(0, 80), :]

    @pl.loop(0, 4)
    def _(i):
        @pl.when((c == 1) | (i > 0))
        def _():
            tr_copy(i).wait_recv()

    acc = trecv[pl.ds(0, 80), :].astype(F32)
    for i in range(1, 4):
        acc = acc + trecv[pl.ds(80 * i, 80), :].astype(F32)
    side[...] = acc
    give = pl.ds(pl.multiple_of(40 * sib, 8), 40)
    keep = pl.ds(pl.multiple_of(40 * c, 8), 40)
    sd_copy = rc(side.at[give], side_in, s_sd, r_sd, sibling)
    sd_copy.start()
    sd_copy.wait_recv()
    tg = back_rows(temb[keep, :], scale * (side[keep, :] + side_in[...]))
    tg = jnp.concatenate([tg, jnp.zeros((8, D), F32)], axis=0)

    @pl.loop(1, 16)
    def _(k):
        ir_copy(k).wait_recv()

    acc = ipart[pl.ds(pl.multiple_of(32 * xl, 16), 48), :].astype(F32)
    for k in range(1, 16):
        acc = acc + irecv[k].astype(F32)
    ig = back_rows(iemb[pl.ds(pl.multiple_of(32 * xl, 8), 48), :], scale * acc)
    row48 = lax.broadcasted_iota(jnp.int32, (48, 1), 0)
    ig = jnp.where((row48 >= 8 * xl) & (row48 < 40 + 8 * xl), ig, 0.0)
    place = 2 * c + xl
    egath[place] = ig.astype(BF)

    def eg_copy(k, s):
        xl_, c_ = (xl + k % 2) % 2, (c + k // 2) % 2
        return rc(
            egath.at[s], egath.at[s], s_eg.at[k], r_eg.at[k],
            (2 * xl_ + c_, gr),
        )

    @pl.loop(1, 4)
    def _(k):
        eg_copy(k, place).start()

    for q, (a, b) in enumerate(zip(quarters(ig), quarters(tg))):
        gsend[q, :, 0:384] = a.astype(BF)
        gsend[q, :, 384:768] = b.astype(BF)
    grecv[0] = gsend[2 * xl + yl]

    def gr_copy(k):
        x_, y_ = (x + k // 4) % 4, (y + k % 4) % 4
        return rc(
            gsend.at[2 * (x_ % 2) + y_ % 2], grecv.at[k], s_gr.at[k], r_gr.at[k],
            dev(x_, y_, z, c),
        )

    @pl.loop(1, 16)
    def _(k):
        gr_copy(k).start()

    tgrad_ref[...] = dot_nt(tg.astype(BF), tproj_ref[...])[:40]

    @pl.loop(1, 4)
    def _(k):
        xl_, c_ = (xl + k % 2) % 2, (c + k // 2) % 2
        eg_copy(k, 2 * c_ + xl_).wait_recv()

    parts = []
    for s in range(4):
        rows = egath[s].astype(F32)
        parts.append(rows[0:40] if s % 2 == 0 else rows[8:48])
    igrad_ref[...] = dot_nt(jnp.concatenate(parts, axis=0).astype(BF), iproj_ref[...])

    @pl.loop(1, 16)
    def _(k):
        fe_copy(k).wait_recv()
        gr_copy(k).wait_recv()

    for w in range(2):
        cols = slice(384 * w, 384 * w + 384)
        left = frecv[:, :, cols].reshape(768, 384)
        right = grecv[:, :, cols].reshape(768, 384)
        wsend[:, cols] = dot_tn(left, right).astype(BF)

    def w_rows(k):
        return pl.ds(pl.multiple_of(144 * (k // 8) + 16 * ((z + k % 8) % 8), 16), 32)

    def w_copy(k, s):
        return rc(
            wsend.at[w_rows(k)], wrecv.at[s], s_w.at[k], r_w.at[s],
            dev(x, 2 * yh + k // 8, (z + k % 8) % 8, yl),
        )

    @pl.loop(0, 16)
    def _(k):
        self_ = (c == yl) & (k == 8 * yl)

        @pl.when(jnp.logical_not(self_))
        def _():
            w_copy(k, 8 * c + k % 8).start()

        @pl.when(self_)
        def _():
            wrecv[8 * c] = wsend[w_rows(k), :]

    @pl.loop(0, 16)
    def _(s):
        @pl.when(jnp.logical_not((c == yl) & (s == 8 * c)))
        def _():
            w_copy(s, s).wait_recv()

    acc = wrecv[0].astype(F32)
    for s in range(1, 16):
        acc = acc + wrecv[s].astype(F32)
    for k in range(8):
        @pl.when(z == k)
        def _():
            iw_ref[...] = acc[2 * k:2 * k + 18, 0:288]
            tw_ref[...] = acc[2 * k:2 * k + 18, 384:672]

    tf_copy.wait_send()
    sib_copy.wait_send()
    sd_copy.wait_send()

    @pl.loop(1, 8)
    def _(j):
        img_copy(j).wait_send()

    @pl.loop(0, 4)
    def _(i):
        @pl.when((c == 1) | (i > 0))
        def _():
            txt_copy(4 * c + i).wait_send()
            fw_copy(4 * c + i).wait_send()
            tr_copy(i).wait_send()

    @pl.loop(1, 4)
    def _(k):
        eg_copy(k, place).wait_send()

    @pl.loop(1, 16)
    def _(k):
        ir_copy(k).wait_send()
        fe_copy(k).wait_send()
        gr_copy(k).wait_send()

    @pl.loop(0, 16)
    def _(k):
        @pl.when(jnp.logical_not((c == yl) & (k == 8 * yl)))
        def _():
            w_copy(k, 8 * c + k % 8).wait_send()


def per_device(image_feats, text_feats, image_proj, text_proj, logit_scale, logit_bias):
    vmem = pl.BlockSpec(memory_space=pltpu.VMEM)
    smem = pl.BlockSpec(memory_space=pltpu.SMEM)
    sems = []
    for n in (0, 8, 8, 8, 0, 4, 0, 16, 4, 16, 16, 16):
        for _ in range(2):
            sems.append(pltpu.SemaphoreType.DMA((n,)) if n else pltpu.SemaphoreType.DMA)
    return pl.pallas_call(
        kernel,
        out_shape=(
            jax.ShapeDtypeStruct((160, D), F32),
            jax.ShapeDtypeStruct((40, D), F32),
            jax.ShapeDtypeStruct((18, 288), F32),
            jax.ShapeDtypeStruct((18, 288), F32),
        ),
        in_specs=[smem, smem, vmem, vmem, vmem, vmem],
        out_specs=(vmem, vmem, vmem, vmem),
        scratch_shapes=[
            pltpu.VMEM((2, 40, D), F32),
            pltpu.VMEM((80, D), F32),
            pltpu.VMEM((80, D), F32),
            pltpu.VMEM((640, D), BF),
            pltpu.VMEM((640, D), BF),
            pltpu.VMEM((640, 640), BF),
            pltpu.VMEM((640, D), BF),
            pltpu.VMEM((640, D), F32),
            pltpu.VMEM((320, D), BF),
            pltpu.VMEM((320, D), BF),
            pltpu.VMEM((320, D), BF),
            pltpu.VMEM((320, D), BF),
            pltpu.VMEM((80, D), F32),
            pltpu.VMEM((40, D), F32),
            pltpu.VMEM((16, 48, D), BF),
            pltpu.VMEM((4, 48, D), BF),
            pltpu.VMEM((4, 48, 768), BF),
            pltpu.VMEM((16, 48, 768), BF),
            pltpu.VMEM((4, 48, 768), BF),
            pltpu.VMEM((16, 48, 768), BF),
            pltpu.VMEM((384, 768), BF),
            pltpu.VMEM((16, 32, 768), BF),
            *sems,
        ],
        compiler_params=pltpu.CompilerParams(
            collective_id=0, has_side_effects=True, vmem_limit_bytes=56 * 2**20
        ),
        cost_estimate=pl.CostEstimate(
            flops=4 * 10**9, bytes_accessed=8 * 10**6, transcendentals=409600
        ),
    )(logit_scale, logit_bias, image_feats, text_feats, image_proj, text_proj)


def solution(mesh):
    placed = (P("group", None), P(("blk", "group"), None), P(), P(), P(), P())
    return jax.shard_map(
        per_device,
        mesh=mesh,
        in_specs=placed,
        out_specs=(
            P("group", None),
            P(("blk", "group"), None),
            P("group", "blk"),
            P("group", "blk"),
        ),
        check_vma=False,
    )
```

```python
import jax
import jax.numpy as jnp
from jax import lax
from jax.experimental import pallas as pl
from jax.experimental.pallas import tpu as pltpu
from jax.sharding import PartitionSpec as P

D = 1152
MESH = pl.DeviceIdType.MESH
BF = jnp.bfloat16
F32 = jnp.float32
NT = (((1,), (1,)), ((), ()))
TN = (((0,), (0,)), ((), ()))


def dot(a, b):
    return jnp.dot(a, b, preferred_element_type=F32)


def dot_nt(a, b):
    return lax.dot_general(a, b, NT, preferred_element_type=F32)


def dot_tn(a, b):
    return lax.dot_general(a, b, TN, preferred_element_type=F32)


def row_norm(e):
    return jnp.sqrt(jnp.sum(e * e, axis=-1, keepdims=True) + 1e-06)


def back_rows(e, g):
    norm = row_norm(e)
    u = e / norm
    return (g - u * jnp.sum(u * g, axis=-1, keepdims=True)) / norm


def quarters(left, right):
    lane = lax.broadcasted_iota(jnp.int32, (48, 640), 1)
    parts = []
    for q in range(4):
        a = left if q == 0 else pltpu.roll(left, D - 288 * q, 1)
        b = right if q == 1 else pltpu.roll(right, (D + 288 - 288 * q) % D, 1)
        parts.append(jnp.where(lane < 288, a[:, :640], b[:, :640]).astype(BF))
    return parts


def kernel(
    scale_ref, bias_ref, ifeat_ref, tfeat_ref, iproj_hbm, tproj_hbm,
    igrad_hbm, tgrad_hbm, iw_hbm, tw_hbm,
    iproj_ref, tproj_ref, igrad_ref, tgrad_ref, iw_ref, tw_ref,
    tfbuf, iemb, temb, iset, tset, coeff, ipart, tpart, sib_out, sib_in,
    tsend, trecv, side, side_in, irecv, egath, fsend, frecv, gsend, grecv,
    wpart, wgive, wtake, wsend, wrecv,
    s_tf, r_tf, s_img, r_img, s_txt, r_txt, s_fw, r_fw, s_sib, r_sib, s_tr, r_tr,
    s_sd, r_sd, s_ir, r_ir, s_eg, r_eg, s_fe, r_fe, s_gr, r_gr, s_w, r_w,
    s_ws, r_ws, s_loc,
):
    bl = lax.axis_index("blk")
    gr = lax.axis_index("group")
    xl, c = bl // 2, bl % 2
    xh, y, z = gr // 32, (gr // 8) % 4, gr % 8
    x = 2 * xh + xl
    sib = 1 - c
    yh, yl = y // 2, y % 2
    scale = scale_ref[0]
    bias = bias_ref[0]

    def dev(x_, y_, z_, c_):
        return ((x_ % 2) * 2 + c_, ((x_ // 2) * 4 + y_) * 8 + z_)

    def rc(src, dst, ss, rs, to):
        return pltpu.make_async_remote_copy(
            src_ref=src, dst_ref=dst, send_sem=ss, recv_sem=rs,
            device_id=to, device_id_type=MESH,
        )

    sibling = dev(x, y, z, sib)
    lone = (c == 0) & (yl == 0)

    load_i = pltpu.make_async_copy(iproj_hbm, iproj_ref, s_loc.at[0])
    load_t = pltpu.make_async_copy(tproj_hbm, tproj_ref, s_loc.at[1])
    load_i.start()
    load_t.start()
    barrier = pltpu.get_barrier_semaphore()

    def greet(to):
        pl.semaphore_signal(barrier, inc=1, device_id=to, device_id_type=MESH)

    greet(sibling)
    greet(dev(x + 1 - 2 * xl, y, z, sib))

    @pl.loop(1, 8)
    def _(m):
        greet(dev(x, y, (z + m) % 8, c))

    @pl.loop(1, 16)
    def _(k):
        greet(dev((x + k // 4) % 4, (y + k % 4) % 4, z, c))

    @pl.loop(0, 8)
    def _(k):
        @pl.when(jnp.logical_not(lone & (k == 0)))
        def _():
            greet(dev(x, 2 * yh + k // 4, (z + 4 * c + k % 4) % 8, yl))
            greet(dev(x, 2 * yh + c, (z + 8 - k) % 8, k // 4))

    total = 1 + 1 + 7 + 15 + 16 - 2 * jnp.where(lone, 1, 0)

    tfeats = tfeat_ref[...].astype(F32)
    tfbuf[c] = tfeats

    load_i.wait()
    emb = dot(ifeat_ref[pl.ds(pl.multiple_of(80 * c, 16), 80), :], iproj_ref[...])
    iemb[...] = emb
    iset[pl.ds(0, 80), :] = (emb / row_norm(emb)).astype(BF)

    pl.semaphore_wait(barrier, total)
    tf_copy = rc(tfbuf.at[c], tfbuf.at[c], s_tf, r_tf, sibling)
    tf_copy.start()

    def img_copy(j):
        h, dy = j // 4, j % 4
        x_ = x + h * (3 - 2 * x)
        rows = pl.ds(pl.multiple_of(80 * j, 16), 80)
        return rc(
            iset.at[pl.ds(0, 80)], iset.at[rows], s_img.at[j], r_img.at[j],
            dev(x_, (y + dy) % 4, z, c),
        )

    @pl.loop(1, 8)
    def _(j):
        img_copy(j).start()

    iwin = ifeat_ref[pl.ds(pl.multiple_of(80 * c + 32 * xl, 16), 48), :].astype(F32)
    twin = jnp.concatenate([tfeats, jnp.zeros((8, D), F32)], axis=0)
    for q, part in enumerate(quarters(iwin, twin)):
        fsend[q] = part
    frecv[0] = fsend[2 * xh + yh]

    def fe_copy(k):
        x_, y_ = (x + k // 4) % 4, (y + k % 4) % 4
        return rc(
            fsend.at[2 * (x_ // 2) + y_ // 2], frecv.at[k], s_fe.at[k], r_fe.at[k],
            dev(x_, y_, z, c),
        )

    load_t.wait()
    rc(tfbuf.at[sib], tfbuf.at[sib], s_tf, r_tf, sibling).wait_recv()
    tboth = tfbuf[...].reshape(80, D).astype(BF)
    emb = dot(tboth, tproj_ref[...])
    temb[...] = emb
    tset[pl.ds(0, 80), :] = (emb / row_norm(emb)).astype(BF)

    def txt_copy(m):
        rows = pl.ds(pl.multiple_of(80 * m, 16), 80)
        return rc(
            tset.at[pl.ds(0, 80)], tset.at[rows], s_txt.at[m], r_txt.at[m],
            dev(x, y, (z + m) % 8, c),
        )

    def fw_copy(m):
        rows = pl.ds(pl.multiple_of(80 * m, 16), 80)
        return rc(tset.at[rows], tset.at[rows], s_fw.at[m], r_fw.at[m], sibling)

    @pl.loop(0, 4)
    def _(i):
        @pl.when((c == 1) | (i > 0))
        def _():
            txt_copy(4 * c + i).start()

    @pl.loop(1, 8)
    def _(j):
        img_copy(j).wait_recv()

    @pl.loop(1, 9)
    def _(k):
        fe_copy(k).start()

    @pl.loop(0, 4)
    def _(i):
        @pl.when((c == 1) | (i > 0))
        def _():
            txt_copy(4 * c + i).wait_recv()
            fw_copy(4 * c + i).start()

    @pl.loop(0, 4)
    def _(i):
        @pl.when((c == 0) | (i > 0))
        def _():
            fw_copy(4 * sib + i).wait_recv()

    lane = lax.broadcasted_iota(jnp.int32, (1, 640), 1)
    slot = jnp.zeros((1, 640), jnp.int32)
    for m in range(1, 8):
        slot = slot + jnp.where(lane >= 80 * m, 1, 0)
    rest = lane - 80 * slot
    core = jnp.where(rest >= 40, 1, 0)
    tz = z - slot
    tz = jnp.where(tz < 0, tz + 8, tz)
    tidx = ((2 * xl + core) * 64 + (xh * 4 + y) * 8 + tz) * 40 + rest - 40 * core
    row80 = lax.broadcasted_iota(jnp.int32, (80, 1), 0)
    for h in range(2):
        logits = dot_nt(iset[pl.ds(320 * h, 320), :], tset[...])
        logits = scale * logits + bias
        hi = xh + h * (1 - 2 * xh)
        iidx = jnp.concatenate(
            [
                ((hi * 4 + (y + 4 - dy) % 4) * 8 + z) * 160 + 80 * c + row80
                for dy in range(4)
            ],
            axis=0,
        )
        same = iidx == tidx
        neg = jnp.where(same, logits, -logits)
        sig = 1.0 / (1.0 + jnp.exp(neg))
        coeff[pl.ds(320 * h, 320), :] = jnp.where(same, -sig, sig).astype(BF)

    for n in range(3):
        cols = pl.ds(384 * n, 384)
        ipart[:, cols] = dot(coeff[...], tset[:, cols]).astype(BF)

    def ir_copy(k):
        x_, dy = (x + k // 4) % 4, (4 - k % 4) % 4
        h = jnp.where(x_ // 2 == xh, 0, 1)
        rows = pl.ds(pl.multiple_of(80 * (4 * h + dy) + 32 * (x_ % 2), 16), 48)
        return rc(
            ipart.at[rows], irecv.at[k], s_ir.at[k], r_ir.at[k],
            dev(x_, (y + k % 4) % 4, z, c),
        )

    @pl.loop(1, 16)
    def _(k):
        ir_copy(k).start()

    for n in range(3):
        cols = pl.ds(384 * n, 384)
        tpart[:, cols] = dot_tn(coeff[...], iset[:, cols])
    sib_out[...] = tpart[pl.ds(pl.multiple_of(320 * sib, 16), 320), :].astype(BF)
    sib_copy = rc(sib_out, sib_in, s_sib, r_sib, sibling)
    sib_copy.start()

    @pl.loop(9, 16)
    def _(k):
        fe_copy(k).start()

    sib_copy.wait_recv()

    def tr_copy(i):
        rows = pl.ds(pl.multiple_of(80 * i, 16), 80)
        return rc(
            tsend.at[rows], trecv.at[rows], s_tr.at[i], r_tr.at[i],
            dev(x, y, (z + 8 - (4 * c + i)) % 8, c),
        )

    @pl.loop(0, 4)
    def _(i):
        rows = pl.ds(pl.multiple_of(80 * i, 16), 80)
        mine = tpart[pl.ds(pl.multiple_of(320 * c + 80 * i, 16), 80), :]
        tsend[rows, :] = (mine + sib_in[rows, :].astype(F32)).astype(BF)

        @pl.when((c == 1) | (i > 0))
        def _():
            tr_copy(i).start()

    @pl.when(c == 0)
    def _():
        trecv[pl.ds(0, 80), :] = tsend[pl.ds(0, 80), :]

    @pl.loop(0, 4)
    def _(i):
        @pl.when((c == 1) | (i > 0))
        def _():
            tr_copy(i).wait_recv()

    acc = trecv[pl.ds(0, 80), :].astype(F32)
    for i in range(1, 4):
        acc = acc + trecv[pl.ds(80 * i, 80), :].astype(F32)
    side[...] = acc
    give = pl.ds(pl.multiple_of(40 * sib, 8), 40)
    keep = pl.ds(pl.multiple_of(40 * c, 8), 40)
    sd_copy = rc(side.at[give], side_in, s_sd, r_sd, sibling)
    sd_copy.start()
    sd_copy.wait_recv()
    tg = back_rows(temb[keep, :], scale * (side[keep, :] + side_in[...]))
    tg = jnp.concatenate([tg, jnp.zeros((8, D), F32)], axis=0)
    tgrad_ref[...] = dot_nt(tg.astype(BF), tproj_ref[...])[:40]
    out_t = pltpu.make_async_copy(tgrad_ref, tgrad_hbm, s_loc.at[2])
    out_t.start()

    @pl.loop(1, 16)
    def _(k):
        ir_copy(k).wait_recv()

    acc = ipart[pl.ds(pl.multiple_of(32 * xl, 16), 48), :].astype(F32)
    for k in range(1, 16):
        acc = acc + irecv[k].astype(F32)
    ig = back_rows(iemb[pl.ds(pl.multiple_of(32 * xl, 8), 48), :], scale * acc)
    row48 = lax.broadcasted_iota(jnp.int32, (48, 1), 0)
    ig = jnp.where((row48 >= 8 * xl) & (row48 < 40 + 8 * xl), ig, 0.0)
    for q, part in enumerate(quarters(ig, tg)):
        gsend[q] = part
    grecv[0] = gsend[2 * xl + yl]

    def gr_copy(k):
        x_, y_ = (x + k // 4) % 4, (y + k % 4) % 4
        return rc(
            gsend.at[2 * (x_ % 2) + y_ % 2], grecv.at[k], s_gr.at[k], r_gr.at[k],
            dev(x_, y_, z, c),
        )

    @pl.loop(1, 16)
    def _(k):
        gr_copy(k).start()

    place = 2 * c + xl
    egath[place] = ig.astype(BF)

    def eg_copy(k, s):
        xl_, c_ = (xl + k % 2) % 2, (c + k // 2) % 2
        return rc(
            egath.at[s], egath.at[s], s_eg.at[k], r_eg.at[k],
            (2 * xl_ + c_, gr),
        )

    @pl.loop(1, 4)
    def _(k):
        eg_copy(k, place).start()

    @pl.loop(1, 16)
    def _(k):
        fe_copy(k).wait_recv()

    @pl.loop(1, 16)
    def _(k):
        gr_copy(k).wait_recv()

    both = dot_tn(frecv[...].reshape(768, 640), grecv[...].reshape(768, 640))
    lane = lax.broadcasted_iota(jnp.int32, (288, 640), 1)
    wpart[...] = jnp.where(lane < 288, both[0:288], both[288:576])

    def w_rows(m, u):
        return pl.ds(pl.multiple_of(144 * u + 16 * ((z + m) % 8), 16), 32)

    @pl.loop(0, 8)
    def _(k):
        wgive[k] = wpart[w_rows(4 * sib + k % 4, k // 4), :].astype(BF)

    ws_copy = rc(wgive, wtake, s_ws, r_ws, sibling)
    ws_copy.start()
    ws_copy.wait_recv()

    def w_copy(k, m):
        return rc(
            wsend.at[k], wrecv.at[m], s_w.at[k], r_w.at[m],
            dev(x, 2 * yh + k // 4, (z + 4 * c + k % 4) % 8, yl),
        )

    @pl.loop(0, 8)
    def _(k):
        rows = w_rows(4 * c + k % 4, k // 4)
        wsend[k] = (wpart[rows, :] + wtake[k].astype(F32)).astype(BF)

        @pl.when(jnp.logical_not(lone & (k == 0)))
        def _():
            w_copy(k, 4 * c + k % 4).start()

    @pl.when(lone)
    def _():
        wrecv[0] = wsend[0]

    @pl.loop(1, 4)
    def _(k):
        xl_, c_ = (xl + k % 2) % 2, (c + k // 2) % 2
        eg_copy(k, 2 * c_ + xl_).wait_recv()

    parts = []
    for s in range(4):
        rows = egath[s].astype(F32)
        parts.append(rows[0:40] if s % 2 == 0 else rows[8:48])
    igrad_ref[...] = dot_nt(jnp.concatenate(parts, axis=0).astype(BF), iproj_ref[...])
    out_i = pltpu.make_async_copy(igrad_ref, igrad_hbm, s_loc.at[3])
    out_i.start()

    @pl.loop(0, 8)
    def _(m):
        @pl.when(jnp.logical_not(lone & (m == 0)))
        def _():
            w_copy(m, m).wait_recv()

    acc = wrecv[0].astype(F32)
    for m in range(1, 8):
        acc = acc + wrecv[m].astype(F32)
    for k in range(8):
        @pl.when(z == k)
        def _():
            iw_ref[...] = acc[2 * k:2 * k + 18, 0:288]
            tw_ref[...] = acc[2 * k:2 * k + 18, 288:576]
    out_iw = pltpu.make_async_copy(iw_ref, iw_hbm, s_loc.at[4])
    out_tw = pltpu.make_async_copy(tw_ref, tw_hbm, s_loc.at[5])
    out_iw.start()
    out_tw.start()

    tf_copy.wait_send()
    sib_copy.wait_send()
    sd_copy.wait_send()
    ws_copy.wait_send()

    @pl.loop(1, 8)
    def _(j):
        img_copy(j).wait_send()

    @pl.loop(0, 4)
    def _(i):
        @pl.when((c == 1) | (i > 0))
        def _():
            txt_copy(4 * c + i).wait_send()
            fw_copy(4 * c + i).wait_send()
            tr_copy(i).wait_send()

    @pl.loop(1, 4)
    def _(k):
        eg_copy(k, place).wait_send()

    @pl.loop(1, 16)
    def _(k):
        ir_copy(k).wait_send()
        fe_copy(k).wait_send()
        gr_copy(k).wait_send()

    @pl.loop(0, 8)
    def _(k):
        @pl.when(jnp.logical_not(lone & (k == 0)))
        def _():
            w_copy(k, 4 * c + k % 4).wait_send()

    out_t.wait()
    out_i.wait()
    out_iw.wait()
    out_tw.wait()


def hand_over(*refs):
    held, sems = refs[8:12], refs[12]
    loads = [pltpu.make_async_copy(refs[i], held[i], sems.at[i]) for i in range(4)]
    stores = [
        pltpu.make_async_copy(held[i], refs[4 + i], sems.at[4 + i]) for i in range(4)
    ]
    for load in loads:
        load.start()
    for load, store in zip(loads, stores):
        load.wait()
        store.start()
    for store in stores:
        store.wait()


def per_device(image_feats, text_feats, image_proj, text_proj, logit_scale, logit_bias):
    vmem = pl.BlockSpec(memory_space=pltpu.VMEM)
    smem = pl.BlockSpec(memory_space=pltpu.SMEM)
    hbm = pl.BlockSpec(memory_space=pl.ANY)
    sems = []
    for n in (0, 8, 8, 8, 0, 4, 0, 16, 4, 16, 16, 8, 0):
        for _ in range(2):
            sems.append(pltpu.SemaphoreType.DMA((n,)) if n else pltpu.SemaphoreType.DMA)
    out_shape = (
        jax.ShapeDtypeStruct((160, D), F32),
        jax.ShapeDtypeStruct((40, D), F32),
        jax.ShapeDtypeStruct((18, 288), F32),
        jax.ShapeDtypeStruct((18, 288), F32),
    )
    results = pl.pallas_call(
        kernel,
        out_shape=out_shape,
        in_specs=[smem, smem, vmem, vmem, hbm, hbm],
        out_specs=(hbm, hbm, hbm, hbm),
        scratch_shapes=[
            pltpu.VMEM((D, D), BF),
            pltpu.VMEM((D, D), BF),
            pltpu.VMEM((160, D), F32),
            pltpu.VMEM((40, D), F32),
            pltpu.VMEM((18, 288), F32),
            pltpu.VMEM((18, 288), F32),
            pltpu.VMEM((2, 40, D), F32),
            pltpu.VMEM((80, D), F32),
            pltpu.VMEM((80, D), F32),
            pltpu.VMEM((640, D), BF),
            pltpu.VMEM((640, D), BF),
            pltpu.VMEM((640, 640), BF),
            pltpu.VMEM((640, D), BF),
            pltpu.VMEM((640, D), F32),
            pltpu.VMEM((320, D), BF),
            pltpu.VMEM((320, D), BF),
            pltpu.VMEM((320, D), BF),
            pltpu.VMEM((320, D), BF),
            pltpu.VMEM((80, D), F32),
            pltpu.VMEM((40, D), F32),
            pltpu.VMEM((16, 48, D), BF),
            pltpu.VMEM((4, 48, D), BF),
            pltpu.VMEM((4, 48, 640), BF),
            pltpu.VMEM((16, 48, 640), BF),
            pltpu.VMEM((4, 48, 640), BF),
            pltpu.VMEM((16, 48, 640), BF),
            pltpu.VMEM((288, 640), F32),
            pltpu.VMEM((8, 32, 640), BF),
            pltpu.VMEM((8, 32, 640), BF),
            pltpu.VMEM((8, 32, 640), BF),
            pltpu.VMEM((8, 32, 640), BF),
            *sems,
            pltpu.SemaphoreType.DMA((6,)),
        ],
        compiler_params=pltpu.CompilerParams(
            collective_id=0, has_side_effects=True, vmem_limit_bytes=56 * 2**20
        ),
        cost_estimate=pl.CostEstimate(
            flops=4 * 10**9, bytes_accessed=8 * 10**6, transcendentals=409600
        ),
    )(logit_scale, logit_bias, image_feats, text_feats, image_proj, text_proj)
    return pl.pallas_call(
        hand_over,
        out_shape=out_shape,
        in_specs=[hbm, hbm, hbm, hbm],
        out_specs=(hbm, hbm, hbm, hbm),
        scratch_shapes=[
            *(pltpu.VMEM(shape.shape, F32) for shape in out_shape),
            pltpu.SemaphoreType.DMA((8,)),
        ],
    )(*results)


def solution(mesh):
    placed = (P("group", None), P(("blk", "group"), None), P(), P(), P(), P())
    return jax.shard_map(
        per_device,
        mesh=mesh,
        in_specs=placed,
        out_specs=(
            P("group", None),
            P(("blk", "group"), None),
            P("group", "blk"),
            P("group", "blk"),
        ),
        check_vma=False,
    )
```

```python
import jax
import jax.numpy as jnp
from jax import lax
from jax.experimental import pallas as pl
from jax.experimental.pallas import tpu as pltpu
from jax.sharding import PartitionSpec as P

D = 1152
MESH = pl.DeviceIdType.MESH
BF = jnp.bfloat16
F32 = jnp.float32
NT = (((1,), (1,)), ((), ()))
TN = (((0,), (0,)), ((), ()))


def dot(a, b):
    return jnp.dot(a, b, preferred_element_type=F32)


def dot_nt(a, b):
    return lax.dot_general(a, b, NT, preferred_element_type=F32)


def dot_tn(a, b):
    return lax.dot_general(a, b, TN, preferred_element_type=F32)


def row_norm(e):
    return jnp.sqrt(jnp.sum(e * e, axis=-1, keepdims=True) + 1e-06)


def back_rows(e, g):
    norm = row_norm(e)
    u = e / norm
    return (g - u * jnp.sum(u * g, axis=-1, keepdims=True)) / norm


def pack(rows):
    tiles = [rows[:, 128 * t:128 * t + 128] for t in range(9)]
    return jnp.concatenate(tiles + [jnp.zeros((8, 128), F32)], axis=0).astype(BF)


def unpack(tiles):
    return jnp.concatenate([tiles[40 * t:40 * t + 40] for t in range(9)], axis=1)


def quarters(left, right):
    lane = lax.broadcasted_iota(jnp.int32, (40, 640), 1)
    low = lax.broadcasted_iota(jnp.int32, (24, 128), 1) < 64
    parts = []
    for q in range(4):
        a = left if q == 0 else pltpu.roll(left, D - 288 * q, 1)
        b = right if q == 1 else pltpu.roll(right, (D + 288 - 288 * q) % D, 1)
        both = jnp.where(lane < 288, a[:, :640], b[:, :640])
        tiles = [both[:, 128 * t:128 * t + 128] for t in range(4)]
        half = both[:, 512:640]
        lower = jnp.concatenate([half[24:40], jnp.zeros((8, 128), F32)], axis=0)
        tiles.append(jnp.where(low, half[0:24], pltpu.roll(lower, 64, 1)))
        tiles.append(jnp.zeros((8, 128), F32))
        parts.append(jnp.concatenate(tiles, axis=0).astype(BF))
    return parts


def join(packed):
    packed = packed.astype(F32)
    tiles = [packed[:, 40 * t:40 * t + 40].reshape(640, 128) for t in range(4)]
    top = packed[:, 160:184]
    lower = pltpu.roll(top.reshape(384, 128), 64, 1).reshape(16, 24, 128)[:, 0:16]
    tiles.append(jnp.concatenate([top, lower], axis=1).reshape(640, 128))
    return jnp.concatenate(tiles, axis=1).astype(BF)


def kernel(
    scale_ref, bias_ref, ifeat_ref, tfeat_ref, iproj_hbm, tproj_hbm,
    igrad_hbm, tgrad_hbm, iw_hbm, tw_hbm,
    iproj_ref, tproj_ref, igrad_ref, tgrad_ref, iw_ref, tw_ref,
    tfbuf, iemb, temb, iset, tset, coeff, ipart, tpart, sib_out, sib_in,
    isend, tsum, tsend, trecv, side, side_in, irecv, egath, fsend, frecv, gsend, grecv,
    wpart, wgive, wtake, wsend, wrecv,
    s_tf, r_tf, s_img, r_img, s_txt, r_txt, s_fw, r_fw, s_sib, r_sib, s_tr, r_tr,
    s_sd, r_sd, s_ir, r_ir, s_eg, r_eg, s_fe, r_fe, s_gr, r_gr, s_w, r_w,
    s_ws, r_ws, s_loc,
):
    bl = lax.axis_index("blk")
    gr = lax.axis_index("group")
    xl, c = bl // 2, bl % 2
    xh, y, z = gr // 32, (gr // 8) % 4, gr % 8
    x = 2 * xh + xl
    sib = 1 - c
    yh, yl = y // 2, y % 2
    scale = scale_ref[0]
    bias = bias_ref[0]

    def dev(x_, y_, z_, c_):
        return ((x_ % 2) * 2 + c_, ((x_ // 2) * 4 + y_) * 8 + z_)

    def rc(src, dst, ss, rs, to):
        return pltpu.make_async_remote_copy(
            src_ref=src, dst_ref=dst, send_sem=ss, recv_sem=rs,
            device_id=to, device_id_type=MESH,
        )

    sibling = dev(x, y, z, sib)
    lone = (c == 0) & (yl == 0)

    load_i = pltpu.make_async_copy(iproj_hbm, iproj_ref, s_loc.at[0])
    load_t = pltpu.make_async_copy(tproj_hbm, tproj_ref, s_loc.at[1])
    load_i.start()
    load_t.start()
    barrier = pltpu.get_barrier_semaphore()

    def greet(to):
        pl.semaphore_signal(barrier, inc=1, device_id=to, device_id_type=MESH)

    greet(sibling)
    greet(dev(x + 1 - 2 * xl, y, z, sib))

    greet(dev(x, y, (z + 1) % 8, c))
    greet(dev(x, y, (z + 7) % 8, c))

    @pl.loop(1, 16)
    def _(k):
        greet(dev((x + k // 4) % 4, (y + k % 4) % 4, z, c))

    @pl.loop(0, 8)
    def _(k):
        @pl.when(jnp.logical_not(lone & (k == 0)))
        def _():
            greet(dev(x, 2 * yh + k // 4, (z + 4 * c + k % 4) % 8, yl))
            greet(dev(x, 2 * yh + c, (z + 8 - k) % 8, k // 4))

    total = 1 + 1 + 2 + 15 + 16 - 2 * jnp.where(lone, 1, 0)

    tfeats = tfeat_ref[...].astype(F32)
    tfbuf[c] = tfeats

    load_i.wait()
    emb = dot(ifeat_ref[pl.ds(pl.multiple_of(80 * c, 16), 80), :], iproj_ref[...])
    iemb[...] = emb
    iset[pl.ds(0, 80), :] = (emb / row_norm(emb)).astype(BF)

    pl.semaphore_wait(barrier, total)
    tf_copy = rc(tfbuf.at[c], tfbuf.at[c], s_tf, r_tf, sibling)
    tf_copy.start()

    def img_copy(j, src, x_, y_):
        return rc(
            iset.at[pl.ds(80 * src, 80)], iset.at[pl.ds(80 * j, 80)],
            s_img.at[j], r_img.at[j], dev(x_, y_ % 4, z, c),
        )

    img = {
        1: img_copy(1, 0, x, y + 1), 2: img_copy(2, 0, x, y + 2),
        3: img_copy(3, 0, x, y + 3), 4: img_copy(4, 0, 3 - x, y),
        5: img_copy(5, 4, x, y + 1), 7: img_copy(7, 4, x, y + 3),
        6: img_copy(6, 2, 3 - x, y),
    }
    for j in (4, 2, 1, 3):
        img[j].start()

    load_t.wait()
    rc(tfbuf.at[sib], tfbuf.at[sib], s_tf, r_tf, sibling).wait_recv()
    tboth = tfbuf[...].reshape(80, D).astype(BF)
    emb = dot(tboth, tproj_ref[...])
    temb[...] = emb
    tset[pl.ds(0, 80), :] = (emb / row_norm(emb)).astype(BF)

    def txt_slot(core, i):
        return (i + 1) * (1 - core) + (7 - i) * core

    def txt_copy(i):
        src = (1 - c) * i + c * ((8 - i) % 8)
        return rc(
            tset.at[pl.ds(pl.multiple_of(80 * src, 16), 80)],
            tset.at[pl.ds(pl.multiple_of(80 * txt_slot(c, i), 16), 80)],
            s_txt.at[i], r_txt.at[i], dev(x, y, (z + 1 + 6 * c) % 8, c),
        )

    def fw_copy(i, core):
        rows = pl.ds(pl.multiple_of(80 * txt_slot(core, i), 16), 80)
        return rc(tset.at[rows], tset.at[rows], s_fw.at[i], r_fw.at[i], sibling)

    txt_copy(0).start()

    iwin = ifeat_ref[pl.ds(pl.multiple_of(80 * c, 16), 80), :].astype(F32)
    iwin = jnp.where(xl == 0, iwin[0:40], iwin[40:80])
    for q, part in enumerate(quarters(iwin, tfeats)):
        fsend[q] = part
    frecv[0] = fsend[2 * xh + yh]

    def fe_copy(k):
        x_, y_ = (x + k // 4) % 4, (y + k % 4) % 4
        return rc(
            fsend.at[2 * (x_ // 2) + y_ // 2], frecv.at[k], s_fe.at[k], r_fe.at[k],
            dev(x_, y_, z, c),
        )

    txt_copy(0).wait_recv()
    txt_copy(1).start()
    fw_copy(0, c).start()
    img[4].wait_recv()
    img[5].start()
    img[7].start()
    txt_copy(1).wait_recv()
    txt_copy(2).start()
    fw_copy(1, c).start()
    img[2].wait_recv()
    img[6].start()
    txt_copy(2).wait_recv()

    @pl.when(c == 1)
    def _():
        txt_copy(3).start()

    fw_copy(2, c).start()

    for j in (1, 3, 5, 7, 6):
        img[j].wait_recv()

    @pl.loop(1, 16)
    def _(k):
        fe_copy(k).start()

    @pl.when(c == 1)
    def _():
        txt_copy(3).wait_recv()
        fw_copy(3, c).start()

    for i in range(3):
        fw_copy(i, sib).wait_recv()

    @pl.when(c == 0)
    def _():
        fw_copy(3, sib).wait_recv()

    lane = lax.broadcasted_iota(jnp.int32, (1, 640), 1)
    slot = jnp.zeros((1, 640), jnp.int32)
    for m in range(1, 8):
        slot = slot + jnp.where(lane >= 80 * m, 1, 0)
    rest = lane - 80 * slot
    core = jnp.where(rest >= 40, 1, 0)
    tz = z - slot
    tz = jnp.where(tz < 0, tz + 8, tz)
    tidx = ((2 * xl + core) * 64 + (xh * 4 + y) * 8 + tz) * 40 + rest - 40 * core
    row80 = lax.broadcasted_iota(jnp.int32, (80, 1), 0)
    for h in range(2):
        logits = dot_nt(iset[pl.ds(320 * h, 320), :], tset[...])
        logits = scale * logits + bias
        hi = xh + h * (1 - 2 * xh)
        iidx = jnp.concatenate(
            [
                ((hi * 4 + (y + 4 - dy) % 4) * 8 + z) * 160 + 80 * c + row80
                for dy in range(4)
            ],
            axis=0,
        )
        same = iidx == tidx
        neg = jnp.where(same, logits, -logits)
        sig = 1.0 / (1.0 + jnp.exp(neg))
        coeff[pl.ds(320 * h, 320), :] = jnp.where(same, -sig, sig).astype(BF)

    for n in range(3):
        cols = pl.ds(384 * n, 384)
        tpart[:, cols] = dot_tn(coeff[...], iset[:, cols])
    sib_out[...] = tpart[pl.ds(pl.multiple_of(320 * sib, 16), 320), :].astype(BF)
    sib_copy = rc(sib_out, sib_in, s_sib, r_sib, sibling)
    sib_copy.start()

    for n in range(3):
        cols = pl.ds(384 * n, 384)
        ipart[:, cols] = dot(coeff[...], tset[:, cols])

    def ir_copy(k):
        return rc(
            isend.at[k], irecv.at[k], s_ir.at[k], r_ir.at[k],
            dev((x + k // 4) % 4, (y + k % 4) % 4, z, c),
        )

    @pl.loop(1, 16)
    def _(k):
        x_, dy = (x + k // 4) % 4, (4 - k % 4) % 4
        h = jnp.where(x_ // 2 == xh, 0, 1)
        start = pl.multiple_of(80 * (4 * h + dy) + 40 * (x_ % 2), 8)
        isend[k] = pack(ipart[pl.ds(start, 40), :])
        ir_copy(k).start()

    sib_copy.wait_recv()
    mine = tpart[pl.ds(pl.multiple_of(320 * c, 16), 320), :]
    tsum[...] = mine + sib_in[...].astype(F32)

    def tr_copy(i):
        return rc(
            tsend.at[i], trecv.at[i], s_tr.at[i], r_tr.at[i],
            dev(x, y, (z + 7 + 2 * c) % 8, c),
        )

    def tr_part(i):
        place = (3 - i) * (1 - c) + i * c
        return tsum[pl.ds(pl.multiple_of(80 * place, 16), 80), :]

    tsend[0] = tr_part(0).astype(BF)
    tr_copy(0).start()
    for i in range(1, 3):
        tr_copy(i - 1).wait_recv()
        tsend[i] = (tr_part(i) + trecv[i - 1].astype(F32)).astype(BF)
        tr_copy(i).start()
    tr_copy(2).wait_recv()

    @pl.when(c == 1)
    def _():
        tsend[3] = (tr_part(3) + trecv[2].astype(F32)).astype(BF)
        tr_copy(3).start()
        tr_copy(3).wait_recv()
        side[...] = trecv[3].astype(F32)

    @pl.when(c == 0)
    def _():
        side[...] = tr_part(3) + trecv[2].astype(F32)

    give = pl.ds(pl.multiple_of(40 * sib, 8), 40)
    keep = pl.ds(pl.multiple_of(40 * c, 8), 40)
    sd_copy = rc(side.at[give], side_in, s_sd, r_sd, sibling)
    sd_copy.start()
    sd_copy.wait_recv()
    tg = back_rows(temb[keep, :], scale * (side[keep, :] + side_in[...]))
    tg48 = jnp.concatenate([tg, jnp.zeros((8, D), F32)], axis=0).astype(BF)
    tgrad_ref[...] = dot_nt(tg48, tproj_ref[...])[:40]
    out_t = pltpu.make_async_copy(tgrad_ref, tgrad_hbm, s_loc.at[2])
    out_t.start()

    @pl.loop(1, 16)
    def _(k):
        ir_copy(k).wait_recv()

    acc = irecv[1].astype(F32)
    for k in range(2, 16):
        acc = acc + irecv[k].astype(F32)
    mine = pl.ds(pl.multiple_of(40 * xl, 8), 40)
    ig = back_rows(iemb[mine, :], scale * (unpack(acc) + ipart[mine, :]))
    for q, part in enumerate(quarters(ig, tg)):
        gsend[q] = part
    grecv[0] = gsend[2 * xl + yl]

    def gr_copy(k):
        x_, y_ = (x + k // 4) % 4, (y + k % 4) % 4
        return rc(
            gsend.at[2 * (x_ % 2) + y_ % 2], grecv.at[k], s_gr.at[k], r_gr.at[k],
            dev(x_, y_, z, c),
        )

    @pl.loop(1, 16)
    def _(k):
        gr_copy(k).start()

    place = 2 * c + xl
    egath[place] = pack(ig)

    def eg_copy(k, s):
        xl_, c_ = (xl + k % 2) % 2, (c + k // 2) % 2
        return rc(
            egath.at[s], egath.at[s], s_eg.at[k], r_eg.at[k],
            (2 * xl_ + c_, gr),
        )

    @pl.loop(1, 4)
    def _(k):
        eg_copy(k, place).start()

    @pl.loop(1, 16)
    def _(k):
        fe_copy(k).wait_recv()

    @pl.loop(1, 16)
    def _(k):
        gr_copy(k).wait_recv()

    both = dot_tn(join(frecv[...]), join(grecv[...]))
    lane = lax.broadcasted_iota(jnp.int32, (288, 640), 1)
    wpart[...] = jnp.where(lane < 288, both[0:288], both[288:576])

    def w_rows(m, u):
        return pl.ds(pl.multiple_of(144 * u + 16 * ((z + m) % 8), 16), 32)

    @pl.loop(0, 8)
    def _(k):
        wgive[k] = wpart[w_rows(4 * sib + k % 4, k // 4), :].astype(BF)

    ws_copy = rc(wgive, wtake, s_ws, r_ws, sibling)
    ws_copy.start()
    ws_copy.wait_recv()

    def w_copy(k, m):
        return rc(
            wsend.at[k], wrecv.at[m], s_w.at[k], r_w.at[m],
            dev(x, 2 * yh + k // 4, (z + 4 * c + k % 4) % 8, yl),
        )

    @pl.loop(0, 8)
    def _(k):
        rows = w_rows(4 * c + k % 4, k // 4)
        wsend[k] = (wpart[rows, :] + wtake[k].astype(F32)).astype(BF)

        @pl.when(jnp.logical_not(lone & (k == 0)))
        def _():
            w_copy(k, 4 * c + k % 4).start()

    @pl.when(lone)
    def _():
        wrecv[0] = wsend[0]

    @pl.loop(1, 4)
    def _(k):
        xl_, c_ = (xl + k % 2) % 2, (c + k // 2) % 2
        eg_copy(k, 2 * c_ + xl_).wait_recv()

    parts = [unpack(egath[s].astype(F32)) for s in range(4)]
    igrad_ref[...] = dot_nt(jnp.concatenate(parts, axis=0).astype(BF), iproj_ref[...])
    out_i = pltpu.make_async_copy(igrad_ref, igrad_hbm, s_loc.at[3])
    out_i.start()

    @pl.loop(0, 8)
    def _(m):
        @pl.when(jnp.logical_not(lone & (m == 0)))
        def _():
            w_copy(m, m).wait_recv()

    acc = wrecv[0].astype(F32)
    for m in range(1, 8):
        acc = acc + wrecv[m].astype(F32)
    for k in range(8):
        @pl.when(z == k)
        def _():
            iw_ref[...] = acc[2 * k:2 * k + 18, 0:288]
            tw_ref[...] = acc[2 * k:2 * k + 18, 288:576]
    out_iw = pltpu.make_async_copy(iw_ref, iw_hbm, s_loc.at[4])
    out_tw = pltpu.make_async_copy(tw_ref, tw_hbm, s_loc.at[5])
    out_iw.start()
    out_tw.start()

    tf_copy.wait_send()
    sib_copy.wait_send()
    sd_copy.wait_send()
    ws_copy.wait_send()

    for j in range(1, 8):
        img[j].wait_send()
    for i in range(3):
        txt_copy(i).wait_send()
        fw_copy(i, c).wait_send()
        tr_copy(i).wait_send()

    @pl.when(c == 1)
    def _():
        txt_copy(3).wait_send()
        fw_copy(3, c).wait_send()
        tr_copy(3).wait_send()

    @pl.loop(1, 4)
    def _(k):
        eg_copy(k, place).wait_send()

    @pl.loop(1, 16)
    def _(k):
        ir_copy(k).wait_send()
        fe_copy(k).wait_send()
        gr_copy(k).wait_send()

    @pl.loop(0, 8)
    def _(k):
        @pl.when(jnp.logical_not(lone & (k == 0)))
        def _():
            w_copy(k, 4 * c + k % 4).wait_send()

    out_t.wait()
    out_i.wait()
    out_iw.wait()
    out_tw.wait()


def hand_over(*refs):
    held, sems = refs[8:12], refs[12]
    loads = [pltpu.make_async_copy(refs[i], held[i], sems.at[i]) for i in range(4)]
    stores = [
        pltpu.make_async_copy(held[i], refs[4 + i], sems.at[4 + i]) for i in range(4)
    ]
    for load in loads:
        load.start()
    for load, store in zip(loads, stores):
        load.wait()
        store.start()
    for store in stores:
        store.wait()


def per_device(image_feats, text_feats, image_proj, text_proj, logit_scale, logit_bias):
    vmem = pl.BlockSpec(memory_space=pltpu.VMEM)
    smem = pl.BlockSpec(memory_space=pltpu.SMEM)
    hbm = pl.BlockSpec(memory_space=pl.ANY)
    sems = []
    for n in (0, 8, 8, 8, 0, 4, 0, 16, 4, 16, 16, 8, 0):
        for _ in range(2):
            sems.append(pltpu.SemaphoreType.DMA((n,)) if n else pltpu.SemaphoreType.DMA)
    out_shape = (
        jax.ShapeDtypeStruct((160, D), F32),
        jax.ShapeDtypeStruct((40, D), F32),
        jax.ShapeDtypeStruct((18, 288), F32),
        jax.ShapeDtypeStruct((18, 288), F32),
    )
    results = pl.pallas_call(
        kernel,
        out_shape=out_shape,
        in_specs=[smem, smem, vmem, vmem, hbm, hbm],
        out_specs=(hbm, hbm, hbm, hbm),
        scratch_shapes=[
            pltpu.VMEM((D, D), BF),
            pltpu.VMEM((D, D), BF),
            pltpu.VMEM((160, D), F32),
            pltpu.VMEM((40, D), F32),
            pltpu.VMEM((18, 288), F32),
            pltpu.VMEM((18, 288), F32),
            pltpu.VMEM((2, 40, D), F32),
            pltpu.VMEM((80, D), F32),
            pltpu.VMEM((80, D), F32),
            pltpu.VMEM((640, D), BF),
            pltpu.VMEM((640, D), BF),
            pltpu.VMEM((640, 640), BF),
            pltpu.VMEM((640, D), F32),
            pltpu.VMEM((640, D), F32),
            pltpu.VMEM((320, D), BF),
            pltpu.VMEM((320, D), BF),
            pltpu.VMEM((16, 368, 128), BF),
            pltpu.VMEM((320, D), F32),
            pltpu.VMEM((4, 80, D), BF),
            pltpu.VMEM((4, 80, D), BF),
            pltpu.VMEM((80, D), F32),
            pltpu.VMEM((40, D), F32),
            pltpu.VMEM((16, 368, 128), BF),
            pltpu.VMEM((4, 368, 128), BF),
            pltpu.VMEM((4, 192, 128), BF),
            pltpu.VMEM((16, 192, 128), BF),
            pltpu.VMEM((4, 192, 128), BF),
            pltpu.VMEM((16, 192, 128), BF),
            pltpu.VMEM((288, 640), F32),
            pltpu.VMEM((8, 32, 640), BF),
            pltpu.VMEM((8, 32, 640), BF),
            pltpu.VMEM((8, 32, 640), BF),
            pltpu.VMEM((8, 32, 640), BF),
            *sems,
            pltpu.SemaphoreType.DMA((6,)),
        ],
        compiler_params=pltpu.CompilerParams(
            collective_id=0, has_side_effects=True, vmem_limit_bytes=56 * 2**20
        ),
        cost_estimate=pl.CostEstimate(
            flops=4 * 10**9, bytes_accessed=8 * 10**6, transcendentals=409600
        ),
    )(logit_scale, logit_bias, image_feats, text_feats, image_proj, text_proj)
    return pl.pallas_call(
        hand_over,
        out_shape=out_shape,
        in_specs=[hbm, hbm, hbm, hbm],
        out_specs=(hbm, hbm, hbm, hbm),
        scratch_shapes=[
            *(pltpu.VMEM(shape.shape, F32) for shape in out_shape),
            pltpu.SemaphoreType.DMA((8,)),
        ],
    )(*results)


def solution(mesh):
    placed = (P("group", None), P(("blk", "group"), None), P(), P(), P(), P())
    return jax.shard_map(
        per_device,
        mesh=mesh,
        in_specs=placed,
        out_specs=(
            P("group", None),
            P(("blk", "group"), None),
            P("group", "blk"),
            P("group", "blk"),
        ),
        check_vma=False,
    )
```

```python
import jax
import jax.numpy as jnp
from jax import lax
from jax.experimental import pallas as pl
from jax.experimental.pallas import tpu as pltpu
from jax.sharding import PartitionSpec as P

D = 1152
PIECES = ((0, 48), (48, 32))
MESH = pl.DeviceIdType.MESH
BF = jnp.bfloat16
F32 = jnp.float32
NT = (((1,), (1,)), ((), ()))
TN = (((0,), (0,)), ((), ()))


def dot(a, b):
    return jnp.dot(a, b, preferred_element_type=F32)


def dot_nt(a, b):
    return lax.dot_general(a, b, NT, preferred_element_type=F32)


def dot_tn(a, b):
    return lax.dot_general(a, b, TN, preferred_element_type=F32)


def row_norm(e):
    return jnp.sqrt(jnp.sum(e * e, axis=-1, keepdims=True) + 1e-06)


def back_rows(e, g):
    norm = row_norm(e)
    u = e / norm
    return (g - u * jnp.sum(u * g, axis=-1, keepdims=True)) / norm


def pack(rows):
    tiles = [rows[:, 128 * t:128 * t + 128] for t in range(9)]
    return jnp.concatenate(tiles + [jnp.zeros((8, 128), F32)], axis=0).astype(BF)


def unpack(tiles):
    return jnp.concatenate([tiles[40 * t:40 * t + 40] for t in range(9)], axis=1)


def quarters(left, right):
    lane = lax.broadcasted_iota(jnp.int32, (40, 640), 1)
    low = lax.broadcasted_iota(jnp.int32, (24, 128), 1) < 64
    parts = []
    for q in range(4):
        a = left if q == 0 else pltpu.roll(left, D - 288 * q, 1)
        b = right if q == 1 else pltpu.roll(right, (D + 288 - 288 * q) % D, 1)
        both = jnp.where(lane < 288, a[:, :640], b[:, :640])
        tiles = [both[:, 128 * t:128 * t + 128] for t in range(4)]
        half = both[:, 512:640]
        lower = jnp.concatenate([half[24:40], jnp.zeros((8, 128), F32)], axis=0)
        tiles.append(jnp.where(low, half[0:24], pltpu.roll(lower, 64, 1)))
        tiles.append(jnp.zeros((8, 128), F32))
        parts.append(jnp.concatenate(tiles, axis=0).astype(BF))
    return parts


def join(packed):
    packed = packed.astype(F32)
    tiles = [packed[:, 40 * t:40 * t + 40].reshape(640, 128) for t in range(4)]
    top = packed[:, 160:184]
    lower = pltpu.roll(top.reshape(384, 128), 64, 1).reshape(16, 24, 128)[:, 0:16]
    tiles.append(jnp.concatenate([top, lower], axis=1).reshape(640, 128))
    return jnp.concatenate(tiles, axis=1).astype(BF)


def kernel(
    scale_ref, bias_ref, ifeat_ref, tfeat_ref, iproj_hbm, tproj_hbm,
    igrad_hbm, tgrad_hbm, iw_hbm, tw_hbm,
    iproj_ref, tproj_ref, igrad_ref, tgrad_ref, iw_ref, tw_ref,
    tfbuf, iemb, temb, iset, tset, coeff, ipart, tpart, sib_out, sib_in,
    isend, tsend, trecv, side, side_in, irecv, egath, fsend, frecv, gsend, grecv,
    wpart, wgive, wtake, wsend, wrecv,
    s_tf, r_tf, s_img, r_img, s_txt, r_txt, s_fw, r_fw, s_sib, r_sib, s_tr, r_tr,
    s_sd, r_sd, s_ir, r_ir, s_eg, r_eg, s_fe, r_fe, s_gr, r_gr, s_w, r_w,
    s_ws, r_ws, s_loc,
):
    bl = lax.axis_index("blk")
    gr = lax.axis_index("group")
    xl, c = bl // 2, bl % 2
    xh, y, z = gr // 32, (gr // 8) % 4, gr % 8
    x = 2 * xh + xl
    sib = 1 - c
    yh, yl = y // 2, y % 2
    scale = scale_ref[0]
    bias = bias_ref[0]

    def dev(x_, y_, z_, c_):
        return ((x_ % 2) * 2 + c_, ((x_ // 2) * 4 + y_) * 8 + z_)

    def rc(src, dst, ss, rs, to):
        return pltpu.make_async_remote_copy(
            src_ref=src, dst_ref=dst, send_sem=ss, recv_sem=rs,
            device_id=to, device_id_type=MESH,
        )

    sibling = dev(x, y, z, sib)
    lone = (c == 0) & (yl == 0)

    load_i = pltpu.make_async_copy(iproj_hbm, iproj_ref, s_loc.at[0])
    load_t = pltpu.make_async_copy(tproj_hbm, tproj_ref, s_loc.at[1])
    load_i.start()
    load_t.start()
    barrier = pltpu.get_barrier_semaphore()

    def greet(to):
        pl.semaphore_signal(barrier, inc=1, device_id=to, device_id_type=MESH)

    greet(sibling)
    greet(dev(x + 1 - 2 * xl, y, z, sib))

    greet(dev(x, y, (z + 1) % 8, c))
    greet(dev(x, y, (z + 7) % 8, c))

    @pl.loop(1, 16)
    def _(k):
        greet(dev((x + k // 4) % 4, (y + k % 4) % 4, z, c))

    @pl.loop(0, 8)
    def _(k):
        @pl.when(jnp.logical_not(lone & (k == 0)))
        def _():
            greet(dev(x, 2 * yh + k // 4, (z + 4 * c + k % 4) % 8, yl))
            greet(dev(x, 2 * yh + c, (z + 8 - k) % 8, k // 4))

    total = 1 + 1 + 2 + 15 + 16 - 2 * jnp.where(lone, 1, 0)

    tfeats = tfeat_ref[...].astype(F32)

    load_i.wait()
    emb = dot(ifeat_ref[pl.ds(pl.multiple_of(80 * c, 16), 80), :], iproj_ref[...])
    iemb[...] = emb
    iset[pl.ds(0, 80), :] = (emb / row_norm(emb)).astype(BF)

    load_t.wait()
    tfeats48 = jnp.concatenate([tfeats, jnp.zeros((8, D), F32)], axis=0).astype(BF)
    emb = dot(tfeats48, tproj_ref[...])[:40]
    temb[...] = emb
    tfbuf[c] = emb / row_norm(emb)

    pl.semaphore_wait(barrier, total)
    tf_copy = rc(tfbuf.at[c], tfbuf.at[c], s_tf, r_tf, sibling)
    tf_copy.start()

    def img_copy(j, src, x_, y_):
        return rc(
            iset.at[pl.ds(80 * src, 80)], iset.at[pl.ds(80 * j, 80)],
            s_img.at[j], r_img.at[j], dev(x_, y_ % 4, z, c),
        )

    img = {
        1: img_copy(1, 0, x, y + 1), 2: img_copy(2, 0, x, y + 2),
        3: img_copy(3, 0, x, y + 3), 4: img_copy(4, 0, 3 - x, y),
        5: img_copy(5, 4, x, y + 1), 7: img_copy(7, 4, x, y + 3),
        6: img_copy(6, 2, 3 - x, y),
    }
    for j in (4, 2, 1, 3):
        img[j].start()

    rc(tfbuf.at[sib], tfbuf.at[sib], s_tf, r_tf, sibling).wait_recv()
    tset[pl.ds(0, 80), :] = tfbuf[...].reshape(80, D).astype(BF)

    def txt_slot(core, i):
        return (i + 1) * (1 - core) + (7 - i) * core

    def txt_copy(i, p):
        src = (1 - c) * i + c * ((8 - i) % 8)
        first, rows = PIECES[p]
        return rc(
            tset.at[pl.ds(pl.multiple_of(80 * src + first, 16), rows)],
            tset.at[pl.ds(pl.multiple_of(80 * txt_slot(c, i) + first, 16), rows)],
            s_txt.at[2 * i + p], r_txt.at[2 * i + p],
            dev(x, y, (z + 1 + 6 * c) % 8, c),
        )

    def fw_copy(i, core):
        rows = pl.ds(pl.multiple_of(80 * txt_slot(core, i), 16), 80)
        return rc(tset.at[rows], tset.at[rows], s_fw.at[i], r_fw.at[i], sibling)

    txt_copy(0, 0).start()
    txt_copy(0, 1).start()

    iwin = ifeat_ref[pl.ds(pl.multiple_of(80 * c, 16), 80), :].astype(F32)
    iwin = jnp.where(xl == 0, iwin[0:40], iwin[40:80])
    for q, part in enumerate(quarters(iwin, tfeats)):
        fsend[q] = part
    frecv[0] = fsend[2 * xh + yh]

    def fe_copy(k):
        x_, y_ = (x + k // 4) % 4, (y + k % 4) % 4
        return rc(
            fsend.at[2 * (x_ // 2) + y_ // 2], frecv.at[k], s_fe.at[k], r_fe.at[k],
            dev(x_, y_, z, c),
        )

    def txt_hop(i):
        for p in range(2):
            txt_copy(i, p).wait_recv()
            if i == 2:
                @pl.when(c == 1)
                def _():
                    txt_copy(3, p).start()
            else:
                txt_copy(i + 1, p).start()
        fw_copy(i, c).start()

    txt_hop(0)
    img[4].wait_recv()
    img[5].start()
    img[7].start()
    txt_hop(1)
    img[2].wait_recv()
    img[6].start()
    txt_hop(2)
    img[1].wait_recv()
    img[3].wait_recv()

    @pl.when(c == 1)
    def _():
        txt_copy(3, 0).wait_recv()
        txt_copy(3, 1).wait_recv()
        fw_copy(3, c).start()

    for i in range(3):
        fw_copy(i, sib).wait_recv()

    @pl.when(c == 0)
    def _():
        fw_copy(3, sib).wait_recv()

    lane = lax.broadcasted_iota(jnp.int32, (1, 640), 1)
    slot = jnp.zeros((1, 640), jnp.int32)
    for m in range(1, 8):
        slot = slot + jnp.where(lane >= 80 * m, 1, 0)
    rest = lane - 80 * slot
    core = jnp.where(rest >= 40, 1, 0)
    tz = z - slot
    tz = jnp.where(tz < 0, tz + 8, tz)
    tidx = ((2 * xl + core) * 64 + (xh * 4 + y) * 8 + tz) * 40 + rest - 40 * core
    row80 = lax.broadcasted_iota(jnp.int32, (80, 1), 0)

    def ir_copy(slot_, k):
        return rc(
            isend.at[slot_], irecv.at[k], s_ir.at[slot_], r_ir.at[k],
            dev((x + k // 4) % 4, (y + k % 4) % 4, z, c),
        )

    def ir_place(slot_):
        xh_ = (xh + slot_ // 8) % 2
        dx = (2 * xh_ + slot_ % 2 + 4 - x) % 4
        return 4 * dx + (4 - (slot_ // 2) % 4) % 4

    for h in range(2):
        half = pl.ds(320 * h, 320)
        if h == 1:
            for j in (5, 7, 6):
                img[j].wait_recv()

            @pl.loop(1, 8)
            def _(k):
                fe_copy(k).start()

        logits = dot_nt(iset[half, :], tset[...])
        logits = scale * logits + bias
        hi = xh + h * (1 - 2 * xh)
        iidx = jnp.concatenate(
            [
                ((hi * 4 + (y + 4 - dy) % 4) * 8 + z) * 160 + 80 * c + row80
                for dy in range(4)
            ],
            axis=0,
        )
        same = iidx == tidx
        neg = jnp.where(same, logits, -logits)
        sig = 1.0 / (1.0 + jnp.exp(neg))
        part = jnp.where(same, -sig, sig).astype(BF)
        coeff[half, :] = part
        for n in range(3):
            cols = pl.ds(384 * n, 384)
            ipart[half, cols] = dot(part, tset[:, cols])

        @pl.loop(8 * h, 8 * h + 8)
        def _(slot_):
            k = ir_place(slot_)

            @pl.when(k > 0)
            def _():
                isend[slot_] = pack(ipart[pl.ds(pl.multiple_of(40 * slot_, 8), 40), :])
                ir_copy(slot_, k).start()

    for n in range(3):
        cols = pl.ds(384 * n, 384)
        tpart[:, cols] = dot_tn(coeff[...], iset[:, cols])

    def tr_place(core, i):
        return (3 - i) * (1 - core) + i * core

    def sib_copy(i):
        return rc(sib_out.at[i], sib_in.at[i], s_sib.at[i], r_sib.at[i], sibling)

    for i in range(4):
        rows = pl.ds(pl.multiple_of(320 * sib + 80 * tr_place(sib, i), 16), 80)
        sib_out[i] = tpart[rows, :].astype(BF)
        sib_copy(i).start()

    def tr_copy(i, p):
        rows = pl.ds(*PIECES[p])
        return rc(
            tsend.at[i, rows], trecv.at[i, rows],
            s_tr.at[2 * i + p], r_tr.at[2 * i + p],
            dev(x, y, (z + 7 + 2 * c) % 8, c),
        )

    def tr_hop(i):
        for p, (first, rows) in enumerate(PIECES):
            here = pl.ds(first, rows)
            start = pl.multiple_of(320 * c + 80 * tr_place(c, i) + first, 16)
            part = tpart[pl.ds(start, rows), :] + sib_in[i, here, :].astype(F32)
            if i > 0:
                tr_copy(i - 1, p).wait_recv()
                part = part + trecv[i - 1, here, :].astype(F32)
            tsend[i, here, :] = part.astype(BF)
            tr_copy(i, p).start()

    for i in range(3):
        sib_copy(i).wait_recv()
        tr_hop(i)
    sib_copy(3).wait_recv()

    @pl.loop(8, 16)
    def _(k):
        fe_copy(k).start()

    @pl.when(c == 1)
    def _():
        tr_hop(3)
        tr_copy(3, 0).wait_recv()
        tr_copy(3, 1).wait_recv()
        side[...] = trecv[3].astype(F32)

    @pl.when(c == 0)
    def _():
        part = tpart[pl.ds(0, 80), :] + sib_in[3].astype(F32)
        tr_copy(2, 0).wait_recv()
        tr_copy(2, 1).wait_recv()
        side[...] = part + trecv[2].astype(F32)

    give = pl.ds(pl.multiple_of(40 * sib, 8), 40)
    keep = pl.ds(pl.multiple_of(40 * c, 8), 40)
    sd_copy = rc(side.at[give], side_in, s_sd, r_sd, sibling)
    sd_copy.start()
    sd_copy.wait_recv()
    tg = back_rows(temb[...], scale * (side[keep, :] + side_in[...]))
    tg48 = jnp.concatenate([tg, jnp.zeros((8, D), F32)], axis=0).astype(BF)
    tgrad_ref[...] = dot_nt(tg48, tproj_ref[...])[:40]
    out_t = pltpu.make_async_copy(tgrad_ref, tgrad_hbm, s_loc.at[2])
    out_t.start()

    @pl.loop(1, 16)
    def _(k):
        ir_copy(k, k).wait_recv()

    acc = irecv[1].astype(F32)
    for k in range(2, 16):
        acc = acc + irecv[k].astype(F32)
    mine = pl.ds(pl.multiple_of(40 * xl, 8), 40)
    ig = back_rows(iemb[mine, :], scale * (unpack(acc) + ipart[mine, :]))
    for q, part in enumerate(quarters(ig, tg)):
        gsend[q] = part
    grecv[0] = gsend[2 * xl + yl]

    def gr_copy(k):
        x_, y_ = (x + k // 4) % 4, (y + k % 4) % 4
        return rc(
            gsend.at[2 * (x_ % 2) + y_ % 2], grecv.at[k], s_gr.at[k], r_gr.at[k],
            dev(x_, y_, z, c),
        )

    @pl.loop(1, 16)
    def _(k):
        gr_copy(k).start()

    place = 2 * c + xl
    egath[place] = pack(ig)

    def eg_copy(k, s):
        xl_, c_ = (xl + k % 2) % 2, (c + k // 2) % 2
        return rc(
            egath.at[s], egath.at[s], s_eg.at[k], r_eg.at[k],
            (2 * xl_ + c_, gr),
        )

    @pl.loop(1, 4)
    def _(k):
        eg_copy(k, place).start()

    @pl.loop(1, 16)
    def _(k):
        fe_copy(k).wait_recv()

    @pl.loop(1, 16)
    def _(k):
        gr_copy(k).wait_recv()

    both = dot_tn(join(frecv[...]), join(grecv[...]))
    lane = lax.broadcasted_iota(jnp.int32, (288, 640), 1)
    wpart[...] = jnp.where(lane < 288, both[0:288], both[288:576])

    def w_rows(m, u):
        return pl.ds(pl.multiple_of(144 * u + 16 * ((z + m) % 8), 16), 32)

    @pl.loop(0, 8)
    def _(k):
        wgive[k] = wpart[w_rows(4 * sib + k % 4, k // 4), :].astype(BF)

    ws_copy = rc(wgive, wtake, s_ws, r_ws, sibling)
    ws_copy.start()
    ws_copy.wait_recv()

    def w_copy(k, m):
        return rc(
            wsend.at[k], wrecv.at[m], s_w.at[k], r_w.at[m],
            dev(x, 2 * yh + k // 4, (z + 4 * c + k % 4) % 8, yl),
        )

    @pl.loop(0, 8)
    def _(k):
        rows = w_rows(4 * c + k % 4, k // 4)
        wsend[k] = (wpart[rows, :] + wtake[k].astype(F32)).astype(BF)

        @pl.when(jnp.logical_not(lone & (k == 0)))
        def _():
            w_copy(k, 4 * c + k % 4).start()

    @pl.when(lone)
    def _():
        wrecv[0] = wsend[0]

    @pl.loop(1, 4)
    def _(k):
        xl_, c_ = (xl + k % 2) % 2, (c + k // 2) % 2
        eg_copy(k, 2 * c_ + xl_).wait_recv()

    parts = [unpack(egath[s].astype(F32)) for s in range(4)]
    igrad_ref[...] = dot_nt(jnp.concatenate(parts, axis=0).astype(BF), iproj_ref[...])
    out_i = pltpu.make_async_copy(igrad_ref, igrad_hbm, s_loc.at[3])
    out_i.start()

    @pl.loop(0, 8)
    def _(m):
        @pl.when(jnp.logical_not(lone & (m == 0)))
        def _():
            w_copy(m, m).wait_recv()

    acc = wrecv[0].astype(F32)
    for m in range(1, 8):
        acc = acc + wrecv[m].astype(F32)
    for k in range(8):
        @pl.when(z == k)
        def _():
            iw_ref[...] = acc[2 * k:2 * k + 18, 0:288]
            tw_ref[...] = acc[2 * k:2 * k + 18, 288:576]
    out_iw = pltpu.make_async_copy(iw_ref, iw_hbm, s_loc.at[4])
    out_tw = pltpu.make_async_copy(tw_ref, tw_hbm, s_loc.at[5])
    out_iw.start()
    out_tw.start()

    tf_copy.wait_send()
    for i in range(4):
        sib_copy(i).wait_send()
    sd_copy.wait_send()
    ws_copy.wait_send()

    for j in range(1, 8):
        img[j].wait_send()
    for i in range(3):
        fw_copy(i, c).wait_send()
        for p in range(2):
            txt_copy(i, p).wait_send()
            tr_copy(i, p).wait_send()

    @pl.when(c == 1)
    def _():
        fw_copy(3, c).wait_send()
        for p in range(2):
            txt_copy(3, p).wait_send()
            tr_copy(3, p).wait_send()

    @pl.loop(1, 4)
    def _(k):
        eg_copy(k, place).wait_send()

    @pl.loop(1, 16)
    def _(k):
        fe_copy(k).wait_send()
        gr_copy(k).wait_send()

    @pl.loop(0, 16)
    def _(slot_):
        @pl.when(slot_ != xl)
        def _():
            ir_copy(slot_, 0).wait_send()

    @pl.loop(0, 8)
    def _(k):
        @pl.when(jnp.logical_not(lone & (k == 0)))
        def _():
            w_copy(k, 4 * c + k % 4).wait_send()

    out_t.wait()
    out_i.wait()
    out_iw.wait()
    out_tw.wait()


def hand_over(*refs):
    held, sems = refs[8:12], refs[12]
    loads = [pltpu.make_async_copy(refs[i], held[i], sems.at[i]) for i in range(4)]
    stores = [
        pltpu.make_async_copy(held[i], refs[4 + i], sems.at[4 + i]) for i in range(4)
    ]
    for load in loads:
        load.start()
    for load, store in zip(loads, stores):
        load.wait()
        store.start()
    for store in stores:
        store.wait()


def per_device(image_feats, text_feats, image_proj, text_proj, logit_scale, logit_bias):
    vmem = pl.BlockSpec(memory_space=pltpu.VMEM)
    smem = pl.BlockSpec(memory_space=pltpu.SMEM)
    hbm = pl.BlockSpec(memory_space=pl.ANY)
    sems = []
    for n in (0, 8, 8, 8, 4, 8, 0, 16, 4, 16, 16, 8, 0):
        for _ in range(2):
            sems.append(pltpu.SemaphoreType.DMA((n,)) if n else pltpu.SemaphoreType.DMA)
    out_shape = (
        jax.ShapeDtypeStruct((160, D), F32),
        jax.ShapeDtypeStruct((40, D), F32),
        jax.ShapeDtypeStruct((18, 288), F32),
        jax.ShapeDtypeStruct((18, 288), F32),
    )
    results = pl.pallas_call(
        kernel,
        out_shape=out_shape,
        in_specs=[smem, smem, vmem, vmem, hbm, hbm],
        out_specs=(hbm, hbm, hbm, hbm),
        scratch_shapes=[
            pltpu.VMEM((D, D), BF),
            pltpu.VMEM((D, D), BF),
            pltpu.VMEM((160, D), F32),
            pltpu.VMEM((40, D), F32),
            pltpu.VMEM((18, 288), F32),
            pltpu.VMEM((18, 288), F32),
            pltpu.VMEM((2, 40, D), F32),
            pltpu.VMEM((80, D), F32),
            pltpu.VMEM((40, D), F32),
            pltpu.VMEM((640, D), BF),
            pltpu.VMEM((640, D), BF),
            pltpu.VMEM((640, 640), BF),
            pltpu.VMEM((640, D), F32),
            pltpu.VMEM((640, D), F32),
            pltpu.VMEM((4, 80, D), BF),
            pltpu.VMEM((4, 80, D), BF),
            pltpu.VMEM((16, 368, 128), BF),
            pltpu.VMEM((4, 80, D), BF),
            pltpu.VMEM((4, 80, D), BF),
            pltpu.VMEM((80, D), F32),
            pltpu.VMEM((40, D), F32),
            pltpu.VMEM((16, 368, 128), BF),
            pltpu.VMEM((4, 368, 128), BF),
            pltpu.VMEM((4, 192, 128), BF),
            pltpu.VMEM((16, 192, 128), BF),
            pltpu.VMEM((4, 192, 128), BF),
            pltpu.VMEM((16, 192, 128), BF),
            pltpu.VMEM((288, 640), F32),
            pltpu.VMEM((8, 32, 640), BF),
            pltpu.VMEM((8, 32, 640), BF),
            pltpu.VMEM((8, 32, 640), BF),
            pltpu.VMEM((8, 32, 640), BF),
            *sems,
            pltpu.SemaphoreType.DMA((6,)),
        ],
        compiler_params=pltpu.CompilerParams(
            collective_id=0, has_side_effects=True, vmem_limit_bytes=56 * 2**20
        ),
        cost_estimate=pl.CostEstimate(
            flops=4 * 10**9, bytes_accessed=8 * 10**6, transcendentals=409600
        ),
    )(logit_scale, logit_bias, image_feats, text_feats, image_proj, text_proj)
    return pl.pallas_call(
        hand_over,
        out_shape=out_shape,
        in_specs=[hbm, hbm, hbm, hbm],
        out_specs=(hbm, hbm, hbm, hbm),
        scratch_shapes=[
            *(pltpu.VMEM(shape.shape, F32) for shape in out_shape),
            pltpu.SemaphoreType.DMA((8,)),
        ],
    )(*results)


def solution(mesh):
    placed = (P("group", None), P(("blk", "group"), None), P(), P(), P(), P())
    return jax.shard_map(
        per_device,
        mesh=mesh,
        in_specs=placed,
        out_specs=(
            P("group", None),
            P(("blk", "group"), None),
            P("group", "blk"),
            P("group", "blk"),
        ),
        check_vma=False,
    )
```

```python
import jax
import jax.numpy as jnp
import numpy as np
from jax import lax
from jax.experimental import pallas as pl
from jax.experimental.pallas import tpu as pltpu
from jax.sharding import PartitionSpec as P

D = 1152
PIECES = ((0, 48), (48, 32))
MESH = pl.DeviceIdType.MESH
BF = jnp.bfloat16
F32 = jnp.float32
NT = (((1,), (1,)), ((), ()))
TN = (((0,), (0,)), ((), ()))


def dot(a, b):
    return jnp.dot(a, b, preferred_element_type=F32)


def dot_nt(a, b):
    return lax.dot_general(a, b, NT, preferred_element_type=F32)


def dot_tn(a, b):
    return lax.dot_general(a, b, TN, preferred_element_type=F32)


def row_norm(e):
    return jnp.sqrt(jnp.sum(e * e, axis=-1, keepdims=True) + 1e-06)


def back_rows(e, g):
    norm = row_norm(e)
    u = e / norm
    return (g - u * jnp.sum(u * g, axis=-1, keepdims=True)) / norm


def pack(rows):
    tiles = [rows[:, 128 * t:128 * t + 128] for t in range(9)]
    return jnp.concatenate(tiles + [jnp.zeros((8, 128), F32)], axis=0).astype(BF)


def unpack(tiles):
    return jnp.concatenate([tiles[40 * t:40 * t + 40] for t in range(9)], axis=1)


def fold(tile, step):
    lane = lax.broadcasted_iota(jnp.int32, (step, 128), 1)
    out = tile[0:step]
    for g in range(1, tile.shape[0] // step):
        part = pltpu.roll(tile[g * step:g * step + step], 32 * g, 1)
        out = jnp.where(lane < 32 * g, out, part)
    return out


def quarters(rows):
    parts = []
    for q in range(4):
        a = (rows if q == 0 else pltpu.roll(rows, D - 288 * q, 1))[:, :384]
        last = jnp.concatenate([a[:, 256:384], jnp.zeros((8, 128), F32)], axis=0)
        tiles = [a[:, 0:128], a[:, 128:256], fold(last, 16)]
        parts.append(jnp.concatenate(tiles, axis=0).astype(BF))
    return parts


def join(packed):
    packed = packed.astype(F32)
    last = packed[:, 80:96].reshape(256, 128)
    groups = [last] + [pltpu.roll(last, 128 - 32 * g, 1) for g in (1, 2)]
    groups = [group.reshape(16, 16, 128) for group in groups]
    last = jnp.concatenate([groups[0], groups[1], groups[2][:, 0:8]], axis=1)
    tiles = [packed[:, 0:40], packed[:, 40:80], last]
    return jnp.concatenate([t.reshape(640, 128) for t in tiles], axis=1).astype(BF)


def pack_block(rows):
    last = fold(rows[:, 256:384], 8)
    tiles = [rows[:, 0:128], rows[:, 128:256], last, jnp.zeros((8, 128), F32)]
    return jnp.concatenate(tiles, axis=0)


def unpack_block(tiles):
    last = tiles[48:56]
    last = [last] + [pltpu.roll(last, 128 - 32 * g, 1) for g in (1, 2)]
    parts = [tiles[0:24], tiles[24:48], jnp.concatenate(last, axis=0)]
    return jnp.concatenate(parts, axis=1)


def by_z_pair():
    place = np.arange(D)
    h, s, t = place // 288, place % 288 // 36, place % 36
    order = np.zeros((D, D), np.float32)
    order[144 * s + 36 * h + t, place] = 1.0
    return order


def kernel(
    scale_ref, bias_ref, ifeat_ref, tfeat_ref, iproj_hbm, tproj_hbm, order_hbm,
    igrad_hbm, tgrad_hbm, iw_hbm, tw_hbm,
    iproj_ref, tproj_ref, order_ref, igrad_ref, tgrad_ref, iw_ref, tw_ref,
    tfbuf, iemb, temb, iset, tset, coeff, ipart, tpart, sib_out, sib_in,
    isend, tsend, trecv, side, side_in, irecv, egath, fsend, frecv, gsend, grecv,
    ftsend, ftrecv, gtsend, gtrecv, wipart, wtpart, wgive, wtake, wsend, wrecv,
    wtsend, wtrecv,
    s_tf, r_tf, s_img, r_img, s_txt, r_txt, s_fw, r_fw, s_sib, r_sib, s_tr, r_tr,
    s_sd, r_sd, s_ir, r_ir, s_eg, r_eg, s_fe, r_fe, s_gr, r_gr, s_w, r_w,
    s_ws, r_ws, s_ft, r_ft, s_gt, r_gt, s_wt, r_wt, s_loc,
):
    bl = lax.axis_index("blk")
    gr = lax.axis_index("group")
    xl, c = bl // 2, bl % 2
    xh, y, z = gr // 32, (gr // 8) % 4, gr % 8
    x = 2 * xh + xl
    sib = 1 - c
    yh, yl = y // 2, y % 2
    scale = scale_ref[0]
    bias = bias_ref[0]

    def dev(x_, y_, z_, c_):
        return ((x_ % 2) * 2 + c_, ((x_ // 2) * 4 + y_) * 8 + z_)

    def rc(src, dst, ss, rs, to):
        return pltpu.make_async_remote_copy(
            src_ref=src, dst_ref=dst, send_sem=ss, recv_sem=rs,
            device_id=to, device_id_type=MESH,
        )

    sibling = dev(x, y, z, sib)
    lone = (c == 0) & (yl == 0)
    lone_t = xl == z % 2
    pair = z + 1 - 2 * (z % 2)

    load_i = pltpu.make_async_copy(iproj_hbm, iproj_ref, s_loc.at[0])
    load_t = pltpu.make_async_copy(tproj_hbm, tproj_ref, s_loc.at[1])
    load_i.start()
    load_t.start()
    load_o = pltpu.make_async_copy(order_hbm, order_ref, s_loc.at[6])
    load_o.start()
    barrier = pltpu.get_barrier_semaphore()

    def greet(to):
        pl.semaphore_signal(barrier, inc=1, device_id=to, device_id_type=MESH)

    greet(sibling)
    greet(dev(x + 1 - 2 * xl, y, z, sib))

    @pl.loop(1, 8)
    def _(m):
        greet(dev(x, y, (z + m) % 8, 0))
        greet(dev(x, y, (z + m) % 8, 1))

    @pl.loop(0, 8)
    def _(k):
        greet(dev(2 * (k // 4) + z % 2, k % 4, pair, c))

    @pl.when(jnp.logical_not(lone_t))
    def _():
        @pl.loop(0, 16)
        def _(k):
            greet(dev(k // 4, k % 4, pair, c))

    @pl.loop(1, 16)
    def _(k):
        greet(dev((x + k // 4) % 4, (y + k % 4) % 4, z, c))

    @pl.loop(0, 8)
    def _(k):
        @pl.when(jnp.logical_not(lone & (k == 0)))
        def _():
            greet(dev(x, 2 * yh + k // 4, (z + 4 * c + k % 4) % 8, yl))
            greet(dev(x, 2 * yh + c, (z + 8 - k) % 8, k // 4))

    total = 1 + 1 + 14 + 8 + 15 + 16 - 2 * jnp.where(lone, 1, 0)
    total = total + jnp.where(lone_t, 0, 16)

    tfeats = tfeat_ref[...].astype(F32)

    load_i.wait()
    emb = dot(ifeat_ref[pl.ds(pl.multiple_of(80 * c, 16), 80), :], iproj_ref[...])
    iemb[...] = emb
    iset[pl.ds(0, 80), :] = (emb / row_norm(emb)).astype(BF)

    load_t.wait()
    tfeats48 = jnp.concatenate([tfeats, jnp.zeros((8, D), F32)], axis=0).astype(BF)
    emb = dot(tfeats48, tproj_ref[...])[:40]
    temb[...] = emb
    tfbuf[c] = emb / row_norm(emb)

    pl.semaphore_wait(barrier, total)
    tf_copy = rc(tfbuf.at[c], tfbuf.at[c], s_tf, r_tf, sibling)
    tf_copy.start()

    def img_copy(j, src, x_, y_):
        return rc(
            iset.at[pl.ds(80 * src, 80)], iset.at[pl.ds(80 * j, 80)],
            s_img.at[j], r_img.at[j], dev(x_, y_ % 4, z, c),
        )

    img = {
        1: img_copy(1, 0, x, y + 1), 2: img_copy(2, 0, x, y + 2),
        3: img_copy(3, 0, x, y + 3), 4: img_copy(4, 0, 3 - x, y),
        5: img_copy(5, 4, x, y + 1), 7: img_copy(7, 4, x, y + 3),
        6: img_copy(6, 2, 3 - x, y),
    }
    for j in (4, 2, 1, 3):
        img[j].start()

    rc(tfbuf.at[sib], tfbuf.at[sib], s_tf, r_tf, sibling).wait_recv()
    tset[pl.ds(0, 80), :] = tfbuf[...].reshape(80, D).astype(BF)

    def txt_slot(core, i):
        return (i + 1) * (1 - core) + (7 - i) * core

    def txt_copy(i, p):
        src = (1 - c) * i + c * ((8 - i) % 8)
        first, rows = PIECES[p]
        return rc(
            tset.at[pl.ds(pl.multiple_of(80 * src + first, 16), rows)],
            tset.at[pl.ds(pl.multiple_of(80 * txt_slot(c, i) + first, 16), rows)],
            s_txt.at[2 * i + p], r_txt.at[2 * i + p],
            dev(x, y, (z + 1 + 6 * c) % 8, c),
        )

    def fw_copy(i, core):
        rows = pl.ds(pl.multiple_of(80 * txt_slot(core, i), 16), 80)
        return rc(tset.at[rows], tset.at[rows], s_fw.at[i], r_fw.at[i], sibling)

    txt_copy(0, 0).start()
    txt_copy(0, 1).start()

    iwin = ifeat_ref[pl.ds(pl.multiple_of(80 * c, 16), 80), :].astype(F32)
    iwin = jnp.where(xl == 0, iwin[0:40], iwin[40:80])
    for q, part in enumerate(quarters(iwin)):
        fsend[q] = part
    frecv[0] = fsend[2 * xh + yh]
    load_o.wait()
    for q, part in enumerate(quarters(dot(tfeats48, order_ref[...])[:40])):
        ftsend[q] = part
    ftrecv[0] = ftsend[z // 2]

    def ft_copy(k):
        z_, c_ = (z + k % 8) % 8, (c + k // 8) % 2
        return rc(
            ftsend.at[z_ // 2], ftrecv.at[k], s_ft.at[k], r_ft.at[k], dev(x, y, z_, c_)
        )

    def fe_copy(k):
        x_, y_ = (x + k // 4) % 4, (y + k % 4) % 4
        return rc(
            fsend.at[2 * (x_ // 2) + y_ // 2], frecv.at[k], s_fe.at[k], r_fe.at[k],
            dev(x_, y_, z, c),
        )

    def txt_hop(i):
        for p in range(2):
            txt_copy(i, p).wait_recv()
            if i == 2:
                @pl.when(c == 1)
                def _():
                    txt_copy(3, p).start()
            else:
                txt_copy(i + 1, p).start()
        fw_copy(i, c).start()

    txt_hop(0)
    img[4].wait_recv()
    img[5].start()
    img[7].start()
    txt_hop(1)
    img[2].wait_recv()
    img[6].start()
    txt_hop(2)
    img[1].wait_recv()
    img[3].wait_recv()

    @pl.when(c == 1)
    def _():
        txt_copy(3, 0).wait_recv()
        txt_copy(3, 1).wait_recv()
        fw_copy(3, c).start()

    for i in range(3):
        fw_copy(i, sib).wait_recv()

    @pl.when(c == 0)
    def _():
        fw_copy(3, sib).wait_recv()

    @pl.loop(1, 16)
    def _(k):
        ft_copy(k).start()

    lane = lax.broadcasted_iota(jnp.int32, (1, 640), 1)
    slot = jnp.zeros((1, 640), jnp.int32)
    for m in range(1, 8):
        slot = slot + jnp.where(lane >= 80 * m, 1, 0)
    rest = lane - 80 * slot
    core = jnp.where(rest >= 40, 1, 0)
    tz = z - slot
    tz = jnp.where(tz < 0, tz + 8, tz)
    tidx = ((2 * xl + core) * 64 + (xh * 4 + y) * 8 + tz) * 40 + rest - 40 * core
    row80 = lax.broadcasted_iota(jnp.int32, (80, 1), 0)

    def ir_copy(slot_, k):
        return rc(
            isend.at[slot_], irecv.at[k], s_ir.at[slot_], r_ir.at[k],
            dev((x + k // 4) % 4, (y + k % 4) % 4, z, c),
        )

    def ir_place(slot_):
        xh_ = (xh + slot_ // 8) % 2
        dx = (2 * xh_ + slot_ % 2 + 4 - x) % 4
        return 4 * dx + (4 - (slot_ // 2) % 4) % 4

    for h in range(2):
        half = pl.ds(320 * h, 320)
        if h == 1:
            for j in (5, 7, 6):
                img[j].wait_recv()

            @pl.loop(1, 16)
            def _(k):
                fe_copy(k).start()

        logits = dot_nt(iset[half, :], tset[...])
        logits = scale * logits + bias
        hi = xh + h * (1 - 2 * xh)
        iidx = jnp.concatenate(
            [
                ((hi * 4 + (y + 4 - dy) % 4) * 8 + z) * 160 + 80 * c + row80
                for dy in range(4)
            ],
            axis=0,
        )
        same = iidx == tidx
        neg = jnp.where(same, logits, -logits)
        sig = 1.0 / (1.0 + jnp.exp(neg))
        part = jnp.where(same, -sig, sig).astype(BF)
        coeff[half, :] = part
        for n in range(3):
            cols = pl.ds(384 * n, 384)
            ipart[half, cols] = dot(part, tset[:, cols])

        @pl.loop(8 * h, 8 * h + 8)
        def _(slot_):
            k = ir_place(slot_)

            @pl.when(k > 0)
            def _():
                isend[slot_] = pack(ipart[pl.ds(pl.multiple_of(40 * slot_, 8), 40), :])
                ir_copy(slot_, k).start()

    for n in range(3):
        cols = pl.ds(384 * n, 384)
        tpart[:, cols] = dot_tn(coeff[...], iset[:, cols])

    def tr_place(core, i):
        return (3 - i) * (1 - core) + i * core

    def sib_copy(i):
        return rc(sib_out.at[i], sib_in.at[i], s_sib.at[i], r_sib.at[i], sibling)

    for i in range(4):
        rows = pl.ds(pl.multiple_of(320 * sib + 80 * tr_place(sib, i), 16), 80)
        sib_out[i] = tpart[rows, :].astype(BF)
        sib_copy(i).start()

    def tr_copy(i, p):
        rows = pl.ds(*PIECES[p])
        return rc(
            tsend.at[i, rows], trecv.at[i, rows],
            s_tr.at[2 * i + p], r_tr.at[2 * i + p],
            dev(x, y, (z + 7 + 2 * c) % 8, c),
        )

    def tr_hop(i):
        for p, (first, rows) in enumerate(PIECES):
            here = pl.ds(first, rows)
            start = pl.multiple_of(320 * c + 80 * tr_place(c, i) + first, 16)
            part = tpart[pl.ds(start, rows), :] + sib_in[i, here, :].astype(F32)
            if i > 0:
                tr_copy(i - 1, p).wait_recv()
                part = part + trecv[i - 1, here, :].astype(F32)
            tsend[i, here, :] = part.astype(BF)
            tr_copy(i, p).start()

    for i in range(3):
        sib_copy(i).wait_recv()
        tr_hop(i)
    sib_copy(3).wait_recv()

    @pl.when(c == 1)
    def _():
        tr_hop(3)
        tr_copy(3, 0).wait_recv()
        tr_copy(3, 1).wait_recv()
        side[...] = trecv[3].astype(F32)

    @pl.when(c == 0)
    def _():
        part = tpart[pl.ds(0, 80), :] + sib_in[3].astype(F32)
        tr_copy(2, 0).wait_recv()
        tr_copy(2, 1).wait_recv()
        side[...] = part + trecv[2].astype(F32)

    give = pl.ds(pl.multiple_of(40 * sib, 8), 40)
    keep = pl.ds(pl.multiple_of(40 * c, 8), 40)
    sd_copy = rc(side.at[give], side_in, s_sd, r_sd, sibling)
    sd_copy.start()
    sd_copy.wait_recv()
    tg = back_rows(temb[...], scale * (side[keep, :] + side_in[...]))
    for q, part in enumerate(quarters(tg)):
        gtsend[q] = part
    gtrecv[0] = gtsend[2 * (z % 2) + c]

    def gt_copy(k):
        z_, c_ = (z + k % 8) % 8, (c + k // 8) % 2
        return rc(
            gtsend.at[2 * (z_ % 2) + c_], gtrecv.at[k], s_gt.at[k], r_gt.at[k],
            dev(x, y, z_, c_),
        )

    @pl.loop(1, 16)
    def _(k):
        gt_copy(k).start()

    tg48 = jnp.concatenate([tg, jnp.zeros((8, D), F32)], axis=0).astype(BF)
    tgrad_ref[...] = dot_nt(tg48, tproj_ref[...])[:40]
    out_t = pltpu.make_async_copy(tgrad_ref, tgrad_hbm, s_loc.at[2])
    out_t.start()

    @pl.loop(1, 16)
    def _(k):
        ir_copy(k, k).wait_recv()

    acc = irecv[1].astype(F32)
    for k in range(2, 16):
        acc = acc + irecv[k].astype(F32)
    mine = pl.ds(pl.multiple_of(40 * xl, 8), 40)
    ig = back_rows(iemb[mine, :], scale * (unpack(acc) + ipart[mine, :]))
    for q, part in enumerate(quarters(ig)):
        gsend[q] = part
    grecv[0] = gsend[2 * xl + yl]

    def gr_copy(k):
        x_, y_ = (x + k // 4) % 4, (y + k % 4) % 4
        return rc(
            gsend.at[2 * (x_ % 2) + y_ % 2], grecv.at[k], s_gr.at[k], r_gr.at[k],
            dev(x_, y_, z, c),
        )

    @pl.loop(1, 16)
    def _(k):
        gr_copy(k).start()

    place = 2 * c + xl
    egath[place] = pack(ig)

    def eg_copy(k, s):
        xl_, c_ = (xl + k % 2) % 2, (c + k // 2) % 2
        return rc(
            egath.at[s], egath.at[s], s_eg.at[k], r_eg.at[k],
            (2 * xl_ + c_, gr),
        )

    @pl.loop(1, 4)
    def _(k):
        eg_copy(k, place).start()

    @pl.loop(1, 16)
    def _(k):
        fe_copy(k).wait_recv()

    @pl.loop(1, 16)
    def _(k):
        gr_copy(k).wait_recv()

    wipart[...] = dot_tn(join(frecv[...]), join(grecv[...]))

    def w_block(m, u):
        first = 144 * u + 18 * ((z + m) % 8)
        return pack_block(wipart[pl.ds(pl.multiple_of(8 * (first // 8), 8), 24), :])

    @pl.loop(0, 8)
    def _(k):
        wgive[k] = w_block(4 * sib + k % 4, k // 4).astype(BF)

    ws_copy = rc(wgive, wtake, s_ws, r_ws, sibling)
    ws_copy.start()

    @pl.loop(1, 16)
    def _(k):
        ft_copy(k).wait_recv()
        gt_copy(k).wait_recv()

    wtpart[...] = dot_tn(join(ftrecv[...]), join(gtrecv[...]))

    def wt_copy(k, slot_):
        return rc(
            wtsend.at[k], wtrecv.at[slot_], s_wt.at[k], r_wt.at[slot_],
            dev(2 * (k // 8) + z % 2, (k // 2) % 4, 2 * (z // 2) + k % 2, c),
        )

    def wt_self(k):
        return lone_t & (k == 2 * (4 * xh + y) + z % 2)

    @pl.loop(0, 16)
    def _(k):
        first = pl.multiple_of(8 * ((18 * k) // 8), 8)
        wtsend[k] = pack_block(wtpart[pl.ds(first, 24), :]).astype(BF)
        dx = (2 * (k // 8) + z % 2 + 4 - x) % 4
        dy = ((k // 2) % 4 + 4 - y) % 4

        @pl.when(jnp.logical_not(wt_self(k)))
        def _():
            wt_copy(k, 4 * dx + dy).start()

        @pl.when(wt_self(k))
        def _():
            wtrecv[0] = wtsend[k]

    ws_copy.wait_recv()

    def w_copy(k, m):
        return rc(
            wsend.at[k], wrecv.at[m], s_w.at[k], r_w.at[m],
            dev(x, 2 * yh + k // 4, (z + 4 * c + k % 4) % 8, yl),
        )

    @pl.loop(0, 8)
    def _(k):
        block = w_block(4 * c + k % 4, k // 4)
        wsend[k] = (block + wtake[k].astype(F32)).astype(BF)

        @pl.when(jnp.logical_not(lone & (k == 0)))
        def _():
            w_copy(k, 4 * c + k % 4).start()

    @pl.when(lone)
    def _():
        wrecv[0] = wsend[0]

    @pl.loop(1, 4)
    def _(k):
        xl_, c_ = (xl + k % 2) % 2, (c + k // 2) % 2
        eg_copy(k, 2 * c_ + xl_).wait_recv()

    parts = [unpack(egath[s].astype(F32)) for s in range(4)]
    igrad_ref[...] = dot_nt(jnp.concatenate(parts, axis=0).astype(BF), iproj_ref[...])
    out_i = pltpu.make_async_copy(igrad_ref, igrad_hbm, s_loc.at[3])
    out_i.start()

    @pl.loop(0, 8)
    def _(m):
        @pl.when(jnp.logical_not(lone & (m == 0)))
        def _():
            w_copy(m, m).wait_recv()

    @pl.loop(0, 16)
    def _(k):
        @pl.when(jnp.logical_not(lone_t & (k == 0)))
        def _():
            wt_copy(k, k).wait_recv()

    acc = wrecv[0].astype(F32)
    for m in range(1, 8):
        acc = acc + wrecv[m].astype(F32)
    acc_i = unpack_block(acc)
    acc = wtrecv[0].astype(F32)
    for m in range(1, 16):
        acc = acc + wtrecv[m].astype(F32)
    acc_t = unpack_block(acc)
    for k in range(0, 8, 2):
        @pl.when((18 * z) % 8 == k)
        def _():
            iw_ref[...] = acc_i[k:k + 18, 0:288]

        @pl.when((36 * (4 * xh + y) + 18 * (z % 2)) % 8 == k)
        def _():
            tw_ref[...] = acc_t[k:k + 18, 0:288]
    out_iw = pltpu.make_async_copy(iw_ref, iw_hbm, s_loc.at[4])
    out_tw = pltpu.make_async_copy(tw_ref, tw_hbm, s_loc.at[5])
    out_iw.start()
    out_tw.start()

    tf_copy.wait_send()
    for i in range(4):
        sib_copy(i).wait_send()
    sd_copy.wait_send()
    ws_copy.wait_send()

    for j in range(1, 8):
        img[j].wait_send()
    for i in range(3):
        fw_copy(i, c).wait_send()
        for p in range(2):
            txt_copy(i, p).wait_send()
            tr_copy(i, p).wait_send()

    @pl.when(c == 1)
    def _():
        fw_copy(3, c).wait_send()
        for p in range(2):
            txt_copy(3, p).wait_send()
            tr_copy(3, p).wait_send()

    @pl.loop(1, 4)
    def _(k):
        eg_copy(k, place).wait_send()

    @pl.loop(1, 16)
    def _(k):
        fe_copy(k).wait_send()
        ft_copy(k).wait_send()
        gt_copy(k).wait_send()
        gr_copy(k).wait_send()

    @pl.loop(0, 16)
    def _(slot_):
        @pl.when(slot_ != xl)
        def _():
            ir_copy(slot_, 0).wait_send()

        @pl.when(jnp.logical_not(wt_self(slot_)))
        def _():
            wt_copy(slot_, 0).wait_send()

    @pl.loop(0, 8)
    def _(k):
        @pl.when(jnp.logical_not(lone & (k == 0)))
        def _():
            w_copy(k, 4 * c + k % 4).wait_send()

    out_t.wait()
    out_i.wait()
    out_iw.wait()
    out_tw.wait()


def hand_over(*refs):
    held, sems = refs[8:12], refs[12]
    loads = [pltpu.make_async_copy(refs[i], held[i], sems.at[i]) for i in range(4)]
    stores = [
        pltpu.make_async_copy(held[i], refs[4 + i], sems.at[4 + i]) for i in range(4)
    ]
    for load in loads:
        load.start()
    for load, store in zip(loads, stores):
        load.wait()
        store.start()
    for store in stores:
        store.wait()


def per_device(image_feats, text_feats, image_proj, text_proj, logit_scale, logit_bias):
    order = jnp.asarray(by_z_pair(), BF)
    vmem = pl.BlockSpec(memory_space=pltpu.VMEM)
    smem = pl.BlockSpec(memory_space=pltpu.SMEM)
    hbm = pl.BlockSpec(memory_space=pl.ANY)
    sems = []
    for n in (0, 8, 8, 8, 4, 8, 0, 16, 4, 16, 16, 8, 0, 16, 16, 16):
        for _ in range(2):
            sems.append(pltpu.SemaphoreType.DMA((n,)) if n else pltpu.SemaphoreType.DMA)
    out_shape = (
        jax.ShapeDtypeStruct((160, D), F32),
        jax.ShapeDtypeStruct((40, D), F32),
        jax.ShapeDtypeStruct((18, 288), F32),
        jax.ShapeDtypeStruct((18, 288), F32),
    )
    results = pl.pallas_call(
        kernel,
        out_shape=out_shape,
        in_specs=[smem, smem, vmem, vmem, hbm, hbm, hbm],
        out_specs=(hbm, hbm, hbm, hbm),
        scratch_shapes=[
            pltpu.VMEM((D, D), BF),
            pltpu.VMEM((D, D), BF),
            pltpu.VMEM((D, D), BF),
            pltpu.VMEM((160, D), F32),
            pltpu.VMEM((40, D), F32),
            pltpu.VMEM((18, 288), F32),
            pltpu.VMEM((18, 288), F32),
            pltpu.VMEM((2, 40, D), F32),
            pltpu.VMEM((80, D), F32),
            pltpu.VMEM((40, D), F32),
            pltpu.VMEM((640, D), BF),
            pltpu.VMEM((640, D), BF),
            pltpu.VMEM((640, 640), BF),
            pltpu.VMEM((640, D), F32),
            pltpu.VMEM((640, D), F32),
            pltpu.VMEM((4, 80, D), BF),
            pltpu.VMEM((4, 80, D), BF),
            pltpu.VMEM((16, 368, 128), BF),
            pltpu.VMEM((4, 80, D), BF),
            pltpu.VMEM((4, 80, D), BF),
            pltpu.VMEM((80, D), F32),
            pltpu.VMEM((40, D), F32),
            pltpu.VMEM((16, 368, 128), BF),
            pltpu.VMEM((4, 368, 128), BF),
            pltpu.VMEM((4, 96, 128), BF),
            pltpu.VMEM((16, 96, 128), BF),
            pltpu.VMEM((4, 96, 128), BF),
            pltpu.VMEM((16, 96, 128), BF),
            pltpu.VMEM((4, 96, 128), BF),
            pltpu.VMEM((16, 96, 128), BF),
            pltpu.VMEM((4, 96, 128), BF),
            pltpu.VMEM((16, 96, 128), BF),
            pltpu.VMEM((384, 384), F32),
            pltpu.VMEM((384, 384), F32),
            pltpu.VMEM((8, 64, 128), BF),
            pltpu.VMEM((8, 64, 128), BF),
            pltpu.VMEM((8, 64, 128), BF),
            pltpu.VMEM((8, 64, 128), BF),
            pltpu.VMEM((16, 64, 128), BF),
            pltpu.VMEM((16, 64, 128), BF),
            *sems,
            pltpu.SemaphoreType.DMA((7,)),
        ],
        compiler_params=pltpu.CompilerParams(
            collective_id=0, has_side_effects=True, vmem_limit_bytes=56 * 2**20
        ),
        cost_estimate=pl.CostEstimate(
            flops=4 * 10**9, bytes_accessed=8 * 10**6, transcendentals=409600
        ),
    )(logit_scale, logit_bias, image_feats, text_feats, image_proj, text_proj, order)
    return pl.pallas_call(
        hand_over,
        out_shape=out_shape,
        in_specs=[hbm, hbm, hbm, hbm],
        out_specs=(hbm, hbm, hbm, hbm),
        scratch_shapes=[
            *(pltpu.VMEM(shape.shape, F32) for shape in out_shape),
            pltpu.SemaphoreType.DMA((8,)),
        ],
    )(*results)


def solution(mesh):
    placed = (P("group", None), P(("blk", "group"), None), P(), P(), P(), P())
    return jax.shard_map(
        per_device,
        mesh=mesh,
        in_specs=placed,
        out_specs=(
            P("group", None),
            P(("blk", "group"), None),
            P("group", "blk"),
            P("group", "blk"),
        ),
        check_vma=False,
    )
```

```python
import jax
import jax.numpy as jnp
import numpy as np
from jax import lax
from jax.experimental import pallas as pl
from jax.experimental.pallas import tpu as pltpu
from jax.sharding import PartitionSpec as P

D = 1152
PIECES = ((0, 48), (48, 32))
MESH = pl.DeviceIdType.MESH
BF = jnp.bfloat16
F32 = jnp.float32
NT = (((1,), (1,)), ((), ()))
TN = (((0,), (0,)), ((), ()))


def dot(a, b):
    return jnp.dot(a, b, preferred_element_type=F32)


def dot_nt(a, b):
    return lax.dot_general(a, b, NT, preferred_element_type=F32)


def dot_tn(a, b):
    return lax.dot_general(a, b, TN, preferred_element_type=F32)


def row_norm(e):
    return jnp.sqrt(jnp.sum(e * e, axis=-1, keepdims=True) + 1e-06)


def back_rows(e, g):
    norm = row_norm(e)
    u = e / norm
    return (g - u * jnp.sum(u * g, axis=-1, keepdims=True)) / norm


def pack(rows):
    tiles = [rows[:, 128 * t:128 * t + 128] for t in range(9)]
    return jnp.concatenate(tiles + [jnp.zeros((8, 128), F32)], axis=0).astype(BF)


def unpack(tiles):
    return jnp.concatenate([tiles[40 * t:40 * t + 40] for t in range(9)], axis=1)


def fold(tile, step):
    lane = lax.broadcasted_iota(jnp.int32, (step, 128), 1)
    out = tile[0:step]
    for g in range(1, tile.shape[0] // step):
        part = pltpu.roll(tile[g * step:g * step + step], 32 * g, 1)
        out = jnp.where(lane < 32 * g, out, part)
    return out


def quarters(rows):
    parts = []
    for q in range(4):
        a = (rows if q == 0 else pltpu.roll(rows, D - 288 * q, 1))[:, :384]
        last = jnp.concatenate([a[:, 256:384], jnp.zeros((8, 128), F32)], axis=0)
        tiles = [a[:, 0:128], a[:, 128:256], fold(last, 16)]
        parts.append(jnp.concatenate(tiles, axis=0).astype(BF))
    return parts


def join(packed):
    packed = packed.astype(F32)
    last = packed[:, 80:96].reshape(256, 128)
    groups = [last] + [pltpu.roll(last, 128 - 32 * g, 1) for g in (1, 2)]
    groups = [group.reshape(16, 16, 128) for group in groups]
    last = jnp.concatenate([groups[0], groups[1], groups[2][:, 0:8]], axis=1)
    tiles = [packed[:, 0:40], packed[:, 40:80], last]
    return jnp.concatenate([t.reshape(640, 128) for t in tiles], axis=1).astype(BF)


def pack_block(rows):
    last = fold(rows[:, 256:384], 8)
    tiles = [rows[:, 0:128], rows[:, 128:256], last, jnp.zeros((8, 128), F32)]
    return jnp.concatenate(tiles, axis=0)


def unpack_block(tiles):
    last = tiles[48:56]
    last = [last] + [pltpu.roll(last, 128 - 32 * g, 1) for g in (1, 2)]
    parts = [tiles[0:24], tiles[24:48], jnp.concatenate(last, axis=0)]
    return jnp.concatenate(parts, axis=1)


def by_z_pair():
    place = np.arange(D)
    h, s, t = place // 288, place % 288 // 36, place % 36
    order = np.zeros((D, D), np.float32)
    order[144 * s + 36 * h + t, place] = 1.0
    return order


def kernel(
    scale_ref, bias_ref, ifeat_hbm, tfeat_hbm, iproj_hbm, tproj_hbm, order_hbm,
    igrad_hbm, tgrad_hbm, iw_hbm, tw_hbm,
    ifeat_ref, tfeat_ref, iproj_ref, tproj_ref, order_ref, igrad_ref, tgrad_ref, iw_ref, tw_ref,
    tfbuf, iemb, temb, iset, tset, coeff, ipart, tpart, sib_out, sib_in,
    isend, tsend, trecv, side, side_in, irecv, egath, fsend, frecv, gsend, grecv,
    ftsend, ftrecv, gtsend, gtrecv, wipart, wtpart, wgive, wtake, wsend, wrecv,
    wtsend, wtrecv,
    s_tf, r_tf, s_img, r_img, s_txt, r_txt, s_fw, r_fw, s_sib, r_sib, s_tr, r_tr,
    s_sd, r_sd, s_ir, r_ir, s_eg, r_eg, s_fe, r_fe, s_gr, r_gr, s_w, r_w,
    s_ws, r_ws, s_ft, r_ft, s_gt, r_gt, s_wt, r_wt, s_loc,
):
    bl = lax.axis_index("blk")
    gr = lax.axis_index("group")
    xl, c = bl // 2, bl % 2
    xh, y, z = gr // 32, (gr // 8) % 4, gr % 8
    x = 2 * xh + xl
    sib = 1 - c
    yh, yl = y // 2, y % 2
    scale = scale_ref[0]
    bias = bias_ref[0]

    def dev(x_, y_, z_, c_):
        return ((x_ % 2) * 2 + c_, ((x_ // 2) * 4 + y_) * 8 + z_)

    def rc(src, dst, ss, rs, to):
        return pltpu.make_async_remote_copy(
            src_ref=src, dst_ref=dst, send_sem=ss, recv_sem=rs,
            device_id=to, device_id_type=MESH,
        )

    sibling = dev(x, y, z, sib)
    lone = (c == 0) & (yl == 0)
    lone_t = xl == z % 2
    pair = z + 1 - 2 * (z % 2)

    load_tf = pltpu.make_async_copy(tfeat_hbm, tfeat_ref, s_loc.at[8])
    load_t = pltpu.make_async_copy(tproj_hbm, tproj_ref, s_loc.at[1])
    load_if = pltpu.make_async_copy(ifeat_hbm, ifeat_ref, s_loc.at[7])
    load_i = pltpu.make_async_copy(iproj_hbm, iproj_ref, s_loc.at[0])
    load_tf.start()
    load_t.start()
    load_if.start()
    load_i.start()
    load_o = pltpu.make_async_copy(order_hbm, order_ref, s_loc.at[6])
    load_o.start()
    barrier = pltpu.get_barrier_semaphore()

    def greet(to):
        pl.semaphore_signal(barrier, inc=1, device_id=to, device_id_type=MESH)

    greet(sibling)
    greet(dev(x + 1 - 2 * xl, y, z, sib))

    @pl.loop(1, 8)
    def _(m):
        greet(dev(x, y, (z + m) % 8, 0))
        greet(dev(x, y, (z + m) % 8, 1))

    @pl.loop(0, 8)
    def _(k):
        greet(dev(2 * (k // 4) + z % 2, k % 4, pair, c))

    @pl.when(jnp.logical_not(lone_t))
    def _():
        @pl.loop(0, 16)
        def _(k):
            greet(dev(k // 4, k % 4, pair, c))

    @pl.loop(1, 16)
    def _(k):
        greet(dev((x + k // 4) % 4, (y + k % 4) % 4, z, c))

    @pl.loop(0, 4)
    def _(k):
        greet(dev(x, 2 * yh + 1 - yl, (z + 4 * c + k) % 8, yl))

    @pl.when(c != yl)
    def _():
        @pl.loop(0, 8)
        def _(k):
            greet(dev(x, 2 * yh + c, (z + 8 - k) % 8, k // 4))

    total = 1 + 1 + 14 + 8 + 15 + 4 + jnp.where(c == yl, 0, 8)
    total = total + jnp.where(lone_t, 0, 16)

    load_tf.wait()
    load_t.wait()
    tfeats = tfeat_ref[...].astype(F32)
    tfeats48 = jnp.concatenate([tfeats, jnp.zeros((8, D), F32)], axis=0).astype(BF)
    emb = dot(tfeats48, tproj_ref[...])[:40]
    temb[...] = emb
    tfbuf[c] = emb / row_norm(emb)

    load_if.wait()
    load_i.wait()
    emb = dot(ifeat_ref[pl.ds(pl.multiple_of(80 * c, 16), 80), :], iproj_ref[...])
    iemb[...] = emb
    iset[pl.ds(0, 80), :] = (emb / row_norm(emb)).astype(BF)

    pl.semaphore_wait(barrier, total)
    tf_copy = rc(tfbuf.at[c], tfbuf.at[c], s_tf, r_tf, sibling)
    tf_copy.start()

    def img_copy(j, src, x_, y_):
        return rc(
            iset.at[pl.ds(80 * src, 80)], iset.at[pl.ds(80 * j, 80)],
            s_img.at[j], r_img.at[j], dev(x_, y_ % 4, z, c),
        )

    img = {
        1: img_copy(1, 0, x, y + 1), 2: img_copy(2, 0, x, y + 2),
        3: img_copy(3, 0, x, y + 3), 4: img_copy(4, 0, 3 - x, y),
        5: img_copy(5, 4, x, y + 1), 7: img_copy(7, 4, x, y + 3),
        6: img_copy(6, 2, 3 - x, y),
    }
    for j in (4, 2, 1, 3):
        img[j].start()

    rc(tfbuf.at[sib], tfbuf.at[sib], s_tf, r_tf, sibling).wait_recv()
    tset[pl.ds(0, 80), :] = tfbuf[...].reshape(80, D).astype(BF)

    def txt_slot(core, i):
        return (i + 1) * (1 - core) + (7 - i) * core

    def txt_copy(i, p):
        src = (1 - c) * i + c * ((8 - i) % 8)
        first, rows = PIECES[p]
        return rc(
            tset.at[pl.ds(pl.multiple_of(80 * src + first, 16), rows)],
            tset.at[pl.ds(pl.multiple_of(80 * txt_slot(c, i) + first, 16), rows)],
            s_txt.at[2 * i + p], r_txt.at[2 * i + p],
            dev(x, y, (z + 1 + 6 * c) % 8, c),
        )

    def fw_copy(i, core):
        rows = pl.ds(pl.multiple_of(80 * txt_slot(core, i), 16), 80)
        return rc(tset.at[rows], tset.at[rows], s_fw.at[i], r_fw.at[i], sibling)

    txt_copy(0, 0).start()
    txt_copy(0, 1).start()

    iwin = ifeat_ref[pl.ds(pl.multiple_of(80 * c, 16), 80), :].astype(F32)
    iwin = jnp.where(xl == 0, iwin[0:40], iwin[40:80])
    for q, part in enumerate(quarters(iwin)):
        fsend[q] = part
    frecv[0] = fsend[2 * xh + yh]
    load_o.wait()
    for q, part in enumerate(quarters(dot(tfeats48, order_ref[...])[:40])):
        ftsend[q] = part
    ftrecv[0] = ftsend[z // 2]

    def ft_copy(k):
        z_, c_ = (z + k % 8) % 8, (c + k // 8) % 2
        return rc(
            ftsend.at[z_ // 2], ftrecv.at[k], s_ft, r_ft, dev(x, y, z_, c_)
        )

    def fe_copy(k):
        x_, y_ = (x + k // 4) % 4, (y + k % 4) % 4
        return rc(
            fsend.at[2 * (x_ // 2) + y_ // 2], frecv.at[k], s_fe, r_fe,
            dev(x_, y_, z, c),
        )

    def txt_hop(i):
        for p in range(2):
            txt_copy(i, p).wait_recv()
            if i == 2:
                @pl.when(c == 1)
                def _():
                    txt_copy(3, p).start()
            else:
                txt_copy(i + 1, p).start()
        fw_copy(i, c).start()

    txt_hop(0)
    img[4].wait_recv()
    img[5].start()
    img[7].start()
    txt_hop(1)
    img[2].wait_recv()
    img[6].start()
    txt_hop(2)
    img[1].wait_recv()
    img[3].wait_recv()

    @pl.when(c == 1)
    def _():
        txt_copy(3, 0).wait_recv()
        txt_copy(3, 1).wait_recv()
        fw_copy(3, c).start()

    for i in range(3):
        fw_copy(i, sib).wait_recv()

    @pl.when(c == 0)
    def _():
        fw_copy(3, sib).wait_recv()

    @pl.loop(1, 16)
    def _(k):
        fe_copy(k).start()
        ft_copy(k).start()

    lane = lax.broadcasted_iota(jnp.int32, (1, 640), 1)
    slot = jnp.zeros((1, 640), jnp.int32)
    for m in range(1, 8):
        slot = slot + jnp.where(lane >= 80 * m, 1, 0)
    rest = lane - 80 * slot
    core = jnp.where(rest >= 40, 1, 0)
    tz = z - slot
    tz = jnp.where(tz < 0, tz + 8, tz)
    tidx = ((2 * xl + core) * 64 + (xh * 4 + y) * 8 + tz) * 40 + rest - 40 * core
    row80 = lax.broadcasted_iota(jnp.int32, (80, 1), 0)

    def tr_place(core, i):
        return (3 - i) * (1 - core) + i * core

    def sib_copy(i):
        return rc(sib_out.at[i], sib_in.at[i], s_sib.at[i], r_sib.at[i], sibling)

    def text_terms():
        for n in range(3):
            cols = pl.ds(384 * n, 384)
            tpart[:, cols] = dot_tn(coeff[...], iset[:, cols])
        for i in range(4):
            rows = pl.ds(pl.multiple_of(320 * sib + 80 * tr_place(sib, i), 16), 80)
            sib_out[i] = tpart[rows, :].astype(BF)
            sib_copy(i).start()

    def ir_copy(slot_, k):
        return rc(
            isend.at[slot_], irecv.at[k], s_ir, r_ir,
            dev((x + k // 4) % 4, (y + k % 4) % 4, z, c),
        )

    def ir_place(slot_):
        xh_ = (xh + slot_ // 8) % 2
        dx = (2 * xh_ + slot_ % 2 + 4 - x) % 4
        return 4 * dx + (4 - (slot_ // 2) % 4) % 4

    for h in range(2):
        half = pl.ds(320 * h, 320)
        if h == 1:
            for j in (5, 7, 6):
                img[j].wait_recv()

        logits = dot_nt(iset[half, :], tset[...])
        logits = scale * logits + bias
        hi = xh + h * (1 - 2 * xh)
        iidx = jnp.concatenate(
            [
                ((hi * 4 + (y + 4 - dy) % 4) * 8 + z) * 160 + 80 * c + row80
                for dy in range(4)
            ],
            axis=0,
        )
        same = iidx == tidx
        neg = jnp.where(same, logits, -logits)
        sig = 1.0 / (1.0 + jnp.exp(neg))
        part = jnp.where(same, -sig, sig).astype(BF)
        coeff[half, :] = part
        if h == 1:
            text_terms()
        for n in range(3):
            cols = pl.ds(384 * n, 384)
            ipart[half, cols] = dot(part, tset[:, cols])

        @pl.loop(8 * h, 8 * h + 8)
        def _(slot_):
            k = ir_place(slot_)

            @pl.when(k > 0)
            def _():
                isend[slot_] = pack(ipart[pl.ds(pl.multiple_of(40 * slot_, 8), 40), :])
                ir_copy(slot_, k).start()

    def tr_copy(i, p):
        rows = pl.ds(*PIECES[p])
        return rc(
            tsend.at[i, rows], trecv.at[i, rows],
            s_tr.at[2 * i + p], r_tr.at[2 * i + p],
            dev(x, y, (z + 7 + 2 * c) % 8, c),
        )

    def tr_hop(i):
        for p, (first, rows) in enumerate(PIECES):
            here = pl.ds(first, rows)
            start = pl.multiple_of(320 * c + 80 * tr_place(c, i) + first, 16)
            part = tpart[pl.ds(start, rows), :] + sib_in[i, here, :].astype(F32)
            if i > 0:
                tr_copy(i - 1, p).wait_recv()
                part = part + trecv[i - 1, here, :].astype(F32)
            tsend[i, here, :] = part.astype(BF)
            tr_copy(i, p).start()

    for i in range(3):
        sib_copy(i).wait_recv()
        tr_hop(i)
    sib_copy(3).wait_recv()

    @pl.when(c == 1)
    def _():
        tr_hop(3)
        tr_copy(3, 0).wait_recv()
        tr_copy(3, 1).wait_recv()
        side[...] = trecv[3].astype(F32)

    @pl.when(c == 0)
    def _():
        part = tpart[pl.ds(0, 80), :] + sib_in[3].astype(F32)
        tr_copy(2, 0).wait_recv()
        tr_copy(2, 1).wait_recv()
        side[...] = part + trecv[2].astype(F32)

    give = pl.ds(pl.multiple_of(40 * sib, 8), 40)
    keep = pl.ds(pl.multiple_of(40 * c, 8), 40)
    sd_copy = rc(side.at[give], side_in, s_sd, r_sd, sibling)
    sd_copy.start()
    sd_copy.wait_recv()
    tg = back_rows(temb[...], scale * (side[keep, :] + side_in[...]))
    for q, part in enumerate(quarters(tg)):
        gtsend[q] = part
    gtrecv[0] = gtsend[2 * (z % 2) + c]

    def gt_copy(k):
        z_, c_ = (z + k % 8) % 8, (c + k // 8) % 2
        return rc(
            gtsend.at[2 * (z_ % 2) + c_], gtrecv.at[k], s_gt, r_gt,
            dev(x, y, z_, c_),
        )

    @pl.loop(1, 16)
    def _(k):
        gt_copy(k).start()

    many = pl.ds(1, 15)
    rc(isend.at[many], irecv.at[many], s_ir, r_ir, sibling).wait_recv()

    acc = irecv[1].astype(F32)
    for k in range(2, 16):
        acc = acc + irecv[k].astype(F32)
    mine = pl.ds(pl.multiple_of(40 * xl, 8), 40)
    ig = back_rows(iemb[mine, :], scale * (unpack(acc) + ipart[mine, :]))
    for q, part in enumerate(quarters(ig)):
        gsend[q] = part
    grecv[0] = gsend[2 * xl + yl]

    def gr_copy(k):
        x_, y_ = (x + k // 4) % 4, (y + k % 4) % 4
        return rc(
            gsend.at[2 * (x_ % 2) + y_ % 2], grecv.at[k], s_gr, r_gr,
            dev(x_, y_, z, c),
        )

    @pl.loop(1, 16)
    def _(k):
        gr_copy(k).start()

    place = 2 * c + xl
    egath[place] = pack(ig)

    def eg_copy(k, s):
        xl_, c_ = (xl + k % 2) % 2, (c + k // 2) % 2
        return rc(
            egath.at[s], egath.at[s], s_eg.at[k], r_eg.at[k],
            (2 * xl_ + c_, gr),
        )

    @pl.loop(1, 4)
    def _(k):
        eg_copy(k, place).start()

    tg48 = jnp.concatenate([tg, jnp.zeros((8, D), F32)], axis=0).astype(BF)
    tgrad_ref[...] = dot_nt(tg48, tproj_ref[...])[:40]
    out_t = pltpu.make_async_copy(tgrad_ref, tgrad_hbm, s_loc.at[2])
    out_t.start()

    all_fe = rc(frecv.at[many], frecv.at[many], s_fe, r_fe, sibling)
    all_fe.wait_recv()

    all_gr = rc(grecv.at[many], grecv.at[many], s_gr, r_gr, sibling)
    all_gr.wait_recv()

    wipart[...] = dot_tn(join(frecv[...]), join(grecv[...]))

    def w_block(m, u):
        first = 144 * u + 18 * ((z + m) % 8)
        return pack_block(wipart[pl.ds(pl.multiple_of(8 * (first // 8), 8), 24), :])

    @pl.loop(0, 8)
    def _(k):
        wgive[k] = w_block(4 * sib + k % 4, k // 4).astype(BF)

    ws_copy = rc(wgive, wtake, s_ws, r_ws, sibling)
    ws_copy.start()

    all_ft = rc(ftrecv.at[many], ftrecv.at[many], s_ft, r_ft, sibling)
    all_gt = rc(gtrecv.at[many], gtrecv.at[many], s_gt, r_gt, sibling)
    all_ft.wait_recv()
    all_gt.wait_recv()

    wtpart[...] = dot_tn(join(ftrecv[...]), join(gtrecv[...]))

    def wt_copy(k, slot_):
        return rc(
            wtsend.at[k], wtrecv.at[slot_], s_wt.at[k], r_wt.at[slot_],
            dev(2 * (k // 8) + z % 2, (k // 2) % 4, 2 * (z // 2) + k % 2, c),
        )

    def wt_self(k):
        return lone_t & (k == 2 * (4 * xh + y) + z % 2)

    @pl.loop(0, 16)
    def _(k):
        first = pl.multiple_of(8 * ((18 * k) // 8), 8)
        wtsend[k] = pack_block(wtpart[pl.ds(first, 24), :]).astype(BF)
        dx = (2 * (k // 8) + z % 2 + 4 - x) % 4
        dy = ((k // 2) % 4 + 4 - y) % 4

        @pl.when(jnp.logical_not(wt_self(k)))
        def _():
            wt_copy(k, 4 * dx + dy).start()

        @pl.when(wt_self(k))
        def _():
            wtrecv[0] = wtsend[k]

    ws_copy.wait_recv()

    def w_copy(k, m):
        return rc(
            wsend.at[k], wrecv.at[m], s_w.at[k], r_w.at[m],
            dev(x, 2 * yh + k // 4, (z + 4 * c + k % 4) % 8, yl),
        )

    @pl.loop(0, 8)
    def _(k):
        block = w_block(4 * c + k % 4, k // 4)
        wsend[k] = (block + wtake[k].astype(F32)).astype(BF)

        @pl.when(jnp.logical_not(lone & (k == 0)))
        def _():
            w_copy(k, 4 * c + k % 4).start()

    @pl.when(lone)
    def _():
        wrecv[0] = wsend[0]

    @pl.loop(1, 4)
    def _(k):
        xl_, c_ = (xl + k % 2) % 2, (c + k // 2) % 2
        eg_copy(k, 2 * c_ + xl_).wait_recv()

    parts = [unpack(egath[s].astype(F32)) for s in range(4)]
    igrad_ref[...] = dot_nt(jnp.concatenate(parts, axis=0).astype(BF), iproj_ref[...])
    out_i = pltpu.make_async_copy(igrad_ref, igrad_hbm, s_loc.at[3])
    out_i.start()

    @pl.loop(0, 8)
    def _(m):
        @pl.when(jnp.logical_not(lone & (m == 0)))
        def _():
            w_copy(m, m).wait_recv()

    @pl.loop(0, 16)
    def _(k):
        @pl.when(jnp.logical_not(lone_t & (k == 0)))
        def _():
            wt_copy(k, k).wait_recv()

    acc = wrecv[0].astype(F32)
    for m in range(1, 8):
        acc = acc + wrecv[m].astype(F32)
    acc_i = unpack_block(acc)
    acc = wtrecv[0].astype(F32)
    for m in range(1, 16):
        acc = acc + wtrecv[m].astype(F32)
    acc_t = unpack_block(acc)
    for k in range(0, 8, 2):
        @pl.when((18 * z) % 8 == k)
        def _():
            iw_ref[...] = acc_i[k:k + 18, 0:288]

        @pl.when((36 * (4 * xh + y) + 18 * (z % 2)) % 8 == k)
        def _():
            tw_ref[...] = acc_t[k:k + 18, 0:288]
    out_iw = pltpu.make_async_copy(iw_ref, iw_hbm, s_loc.at[4])
    out_tw = pltpu.make_async_copy(tw_ref, tw_hbm, s_loc.at[5])
    out_iw.start()
    out_tw.start()

    tf_copy.wait_send()
    for i in range(4):
        sib_copy(i).wait_send()
    sd_copy.wait_send()
    ws_copy.wait_send()

    for j in range(1, 8):
        img[j].wait_send()
    for i in range(3):
        fw_copy(i, c).wait_send()
        for p in range(2):
            txt_copy(i, p).wait_send()
            tr_copy(i, p).wait_send()

    @pl.when(c == 1)
    def _():
        fw_copy(3, c).wait_send()
        for p in range(2):
            txt_copy(3, p).wait_send()
            tr_copy(3, p).wait_send()

    @pl.loop(1, 4)
    def _(k):
        eg_copy(k, place).wait_send()

    rc(isend.at[many], irecv.at[many], s_ir, r_ir, sibling).wait_send()
    for group in (all_fe, all_ft, all_gr, all_gt):
        group.wait_send()

    @pl.loop(0, 16)
    def _(slot_):
        @pl.when(jnp.logical_not(wt_self(slot_)))
        def _():
            wt_copy(slot_, 0).wait_send()

    @pl.loop(0, 8)
    def _(k):
        @pl.when(jnp.logical_not(lone & (k == 0)))
        def _():
            w_copy(k, 4 * c + k % 4).wait_send()

    out_t.wait()
    out_i.wait()
    out_iw.wait()
    out_tw.wait()


def hand_over(*refs):
    held, sems = refs[8:12], refs[12]
    loads = [pltpu.make_async_copy(refs[i], held[i], sems.at[i]) for i in range(4)]
    stores = [
        pltpu.make_async_copy(held[i], refs[4 + i], sems.at[4 + i]) for i in range(4)
    ]
    for load in loads:
        load.start()
    for load, store in zip(loads, stores):
        load.wait()
        store.start()
    for store in stores:
        store.wait()


def per_device(image_feats, text_feats, image_proj, text_proj, logit_scale, logit_bias):
    order = jnp.asarray(by_z_pair(), BF)
    smem = pl.BlockSpec(memory_space=pltpu.SMEM)
    hbm = pl.BlockSpec(memory_space=pl.ANY)
    sems = []
    for n in (0, 8, 8, 8, 4, 8, 0, 0, 4, 0, 0, 8, 0, 0, 0, 16):
        for _ in range(2):
            sems.append(pltpu.SemaphoreType.DMA((n,)) if n else pltpu.SemaphoreType.DMA)
    out_shape = (
        jax.ShapeDtypeStruct((160, D), F32),
        jax.ShapeDtypeStruct((40, D), F32),
        jax.ShapeDtypeStruct((18, 288), F32),
        jax.ShapeDtypeStruct((18, 288), F32),
    )
    results = pl.pallas_call(
        kernel,
        out_shape=out_shape,
        in_specs=[smem, smem, hbm, hbm, hbm, hbm, hbm],
        out_specs=(hbm, hbm, hbm, hbm),
        scratch_shapes=[
            pltpu.VMEM((160, D), BF),
            pltpu.VMEM((40, D), BF),
            pltpu.VMEM((D, D), BF),
            pltpu.VMEM((D, D), BF),
            pltpu.VMEM((D, D), BF),
            pltpu.VMEM((160, D), F32),
            pltpu.VMEM((40, D), F32),
            pltpu.VMEM((18, 288), F32),
            pltpu.VMEM((18, 288), F32),
            pltpu.VMEM((2, 40, D), F32),
            pltpu.VMEM((80, D), F32),
            pltpu.VMEM((40, D), F32),
            pltpu.VMEM((640, D), BF),
            pltpu.VMEM((640, D), BF),
            pltpu.VMEM((640, 640), BF),
            pltpu.VMEM((640, D), F32),
            pltpu.VMEM((640, D), F32),
            pltpu.VMEM((4, 80, D), BF),
            pltpu.VMEM((4, 80, D), BF),
            pltpu.VMEM((16, 368, 128), BF),
            pltpu.VMEM((4, 80, D), BF),
            pltpu.VMEM((4, 80, D), BF),
            pltpu.VMEM((80, D), F32),
            pltpu.VMEM((40, D), F32),
            pltpu.VMEM((16, 368, 128), BF),
            pltpu.VMEM((4, 368, 128), BF),
            pltpu.VMEM((4, 96, 128), BF),
            pltpu.VMEM((16, 96, 128), BF),
            pltpu.VMEM((4, 96, 128), BF),
            pltpu.VMEM((16, 96, 128), BF),
            pltpu.VMEM((4, 96, 128), BF),
            pltpu.VMEM((16, 96, 128), BF),
            pltpu.VMEM((4, 96, 128), BF),
            pltpu.VMEM((16, 96, 128), BF),
            pltpu.VMEM((384, 384), F32),
            pltpu.VMEM((384, 384), F32),
            pltpu.VMEM((8, 64, 128), BF),
            pltpu.VMEM((8, 64, 128), BF),
            pltpu.VMEM((8, 64, 128), BF),
            pltpu.VMEM((8, 64, 128), BF),
            pltpu.VMEM((16, 64, 128), BF),
            pltpu.VMEM((16, 64, 128), BF),
            *sems,
            pltpu.SemaphoreType.DMA((9,)),
        ],
        compiler_params=pltpu.CompilerParams(
            collective_id=0, has_side_effects=True, vmem_limit_bytes=56 * 2**20
        ),
        cost_estimate=pl.CostEstimate(
            flops=4 * 10**9, bytes_accessed=8 * 10**6, transcendentals=409600
        ),
    )(logit_scale, logit_bias, image_feats, text_feats, image_proj, text_proj, order)
    return pl.pallas_call(
        hand_over,
        out_shape=out_shape,
        in_specs=[hbm, hbm, hbm, hbm],
        out_specs=(hbm, hbm, hbm, hbm),
        scratch_shapes=[
            *(pltpu.VMEM(shape.shape, F32) for shape in out_shape),
            pltpu.SemaphoreType.DMA((8,)),
        ],
    )(*results)


def solution(mesh):
    placed = (P("group", None), P(("blk", "group"), None), P(), P(), P(), P())
    return jax.shard_map(
        per_device,
        mesh=mesh,
        in_specs=placed,
        out_specs=(
            P("group", None),
            P(("blk", "group"), None),
            P("group", "blk"),
            P("group", "blk"),
        ),
        check_vma=False,
    )
```

```python
import jax
import jax.numpy as jnp
import numpy as np
from jax import lax
from jax.experimental import pallas as pl
from jax.experimental.pallas import tpu as pltpu
from jax.sharding import PartitionSpec as P

D = 1152
PIECES = ((0, 48), (48, 32))
MESH = pl.DeviceIdType.MESH
BF = jnp.bfloat16
F32 = jnp.float32
NT = (((1,), (1,)), ((), ()))
TN = (((0,), (0,)), ((), ()))


def dot(a, b):
    return jnp.dot(a, b, preferred_element_type=F32)


def dot_nt(a, b):
    return lax.dot_general(a, b, NT, preferred_element_type=F32)


def dot_tn(a, b):
    return lax.dot_general(a, b, TN, preferred_element_type=F32)


def row_norm(e):
    return jnp.sqrt(jnp.sum(e * e, axis=-1, keepdims=True) + 1e-06)


def back_rows(e, g):
    norm = row_norm(e)
    u = e / norm
    return (g - u * jnp.sum(u * g, axis=-1, keepdims=True)) / norm


def pack(rows):
    tiles = [rows[:, 128 * t:128 * t + 128] for t in range(9)]
    return jnp.concatenate(tiles + [jnp.zeros((8, 128), F32)], axis=0).astype(BF)


def unpack(tiles):
    return jnp.concatenate([tiles[40 * t:40 * t + 40] for t in range(9)], axis=1)


def fold(tile, step):
    lane = lax.broadcasted_iota(jnp.int32, (step, 128), 1)
    out = tile[0:step]
    for g in range(1, tile.shape[0] // step):
        part = pltpu.roll(tile[g * step:g * step + step], 32 * g, 1)
        out = jnp.where(lane < 32 * g, out, part)
    return out


def quarters(rows):
    parts = []
    for q in range(4):
        a = (rows if q == 0 else pltpu.roll(rows, D - 288 * q, 1))[:, :384]
        last = jnp.concatenate([a[:, 256:384], jnp.zeros((8, 128), F32)], axis=0)
        tiles = [a[:, 0:128], a[:, 128:256], fold(last, 16)]
        parts.append(jnp.concatenate(tiles, axis=0).astype(BF))
    return parts


def join(packed):
    packed = packed.astype(F32)
    last = packed[:, 80:96].reshape(256, 128)
    groups = [last] + [pltpu.roll(last, 128 - 32 * g, 1) for g in (1, 2)]
    groups = [group.reshape(16, 16, 128) for group in groups]
    last = jnp.concatenate([groups[0], groups[1], groups[2][:, 0:8]], axis=1)
    tiles = [packed[:, 0:40], packed[:, 40:80], last]
    return jnp.concatenate([t.reshape(640, 128) for t in tiles], axis=1).astype(BF)


def pack_block(rows):
    last = fold(rows[:, 256:384], 8)
    tiles = [rows[:, 0:128], rows[:, 128:256], last, jnp.zeros((8, 128), F32)]
    return jnp.concatenate(tiles, axis=0)


def unpack_block(tiles):
    last = tiles[48:56]
    last = [last] + [pltpu.roll(last, 128 - 32 * g, 1) for g in (1, 2)]
    parts = [tiles[0:24], tiles[24:48], jnp.concatenate(last, axis=0)]
    return jnp.concatenate(parts, axis=1)


def by_z_pair():
    place = np.arange(D)
    h, s, t = place // 288, place % 288 // 36, place % 36
    order = np.zeros((D, D), np.float32)
    order[144 * s + 36 * h + t, place] = 1.0
    return order


def kernel(
    scale_ref, bias_ref, ifeat_hbm, tfeat_hbm, iproj_hbm, tproj_hbm, order_hbm,
    igrad_hbm, tgrad_hbm, iw_hbm, tw_hbm,
    ifeat_ref, tfeat_ref, iproj_ref, tproj_ref, order_ref, igrad_ref, tgrad_ref, iw_ref, tw_ref,
    tfbuf, iemb, temb, iset, tset, coeff, ipart, tpart, sib_out, sib_in,
    isend, tsend, trecv, side, side_in, irecv, egath, fsend, frecv, gsend, grecv,
    ftsend, ftrecv, gtsend, gtrecv, wipart, wtpart, wgive, wtake, wsend, wrecv,
    wtsend, wtrecv,
    s_tf, r_tf, s_img, r_img, s_txt, r_txt, s_fw, r_fw, s_sib, r_sib, s_tr, r_tr,
    s_sd, r_sd, s_ir, r_ir, s_eg, r_eg, s_fe, r_fe, s_gr, r_gr, s_w, r_w,
    s_ws, r_ws, s_ft, r_ft, s_gt, r_gt, s_wt, r_wt, s_ff, r_ff, s_loc,
):
    bl = lax.axis_index("blk")
    gr = lax.axis_index("group")
    xl, c = bl // 2, bl % 2
    xh, y, z = gr // 32, (gr // 8) % 4, gr % 8
    x = 2 * xh + xl
    sib = 1 - c
    yh, yl = y // 2, y % 2
    scale = scale_ref[0]
    bias = bias_ref[0]

    def dev(x_, y_, z_, c_):
        return ((x_ % 2) * 2 + c_, ((x_ // 2) * 4 + y_) * 8 + z_)

    def rc(src, dst, ss, rs, to):
        return pltpu.make_async_remote_copy(
            src_ref=src, dst_ref=dst, send_sem=ss, recv_sem=rs,
            device_id=to, device_id_type=MESH,
        )

    sibling = dev(x, y, z, sib)
    lone = (c == 0) & (yl == 0)
    lone_t = xl == z % 2
    pair = z + 1 - 2 * (z % 2)

    load_tf = pltpu.make_async_copy(tfeat_hbm, tfeat_ref, s_loc.at[8])
    load_t = pltpu.make_async_copy(tproj_hbm, tproj_ref, s_loc.at[1])
    load_if = pltpu.make_async_copy(ifeat_hbm, ifeat_ref, s_loc.at[7])
    load_i = pltpu.make_async_copy(iproj_hbm, iproj_ref, s_loc.at[0])
    load_tf.start()
    load_t.start()
    load_if.start()
    load_i.start()
    load_o = pltpu.make_async_copy(order_hbm, order_ref, s_loc.at[6])
    load_o.start()
    barrier = pltpu.get_barrier_semaphore()

    def greet(to):
        pl.semaphore_signal(barrier, inc=1, device_id=to, device_id_type=MESH)

    greet(sibling)
    greet(dev(x + 1 - 2 * xl, y, z, sib))

    @pl.loop(1, 8)
    def _(m):
        greet(dev(x, y, (z + m) % 8, 0))
        greet(dev(x, y, (z + m) % 8, 1))

    @pl.loop(0, 8)
    def _(k):
        greet(dev(2 * (k // 4) + z % 2, k % 4, pair, c))

    @pl.when(jnp.logical_not(lone_t))
    def _():
        @pl.loop(0, 16)
        def _(k):
            greet(dev(k // 4, k % 4, pair, c))

    @pl.loop(1, 16)
    def _(k):
        greet(dev((x + k // 4) % 4, (y + k % 4) % 4, z, c))

    @pl.loop(0, 4)
    def _(k):
        greet(dev(x, 2 * yh + 1 - yl, (z + 4 * c + k) % 8, yl))

    @pl.when(c != yl)
    def _():
        @pl.loop(0, 8)
        def _(k):
            greet(dev(x, 2 * yh + c, (z + 8 - k) % 8, k // 4))

    total = 1 + 1 + 14 + 8 + 15 + 4 + jnp.where(c == yl, 0, 8)
    total = total + jnp.where(lone_t, 0, 16)

    load_tf.wait()
    load_t.wait()
    tfeats = tfeat_ref[...].astype(F32)
    tfeats48 = jnp.concatenate([tfeats, jnp.zeros((8, D), F32)], axis=0).astype(BF)
    emb = dot(tfeats48, tproj_ref[...])[:40]
    temb[...] = emb
    tfbuf[c] = emb / row_norm(emb)

    load_if.wait()
    load_i.wait()
    emb = dot(ifeat_ref[pl.ds(pl.multiple_of(80 * c, 16), 80), :], iproj_ref[...])
    iemb[...] = emb
    iset[pl.ds(0, 80), :] = (emb / row_norm(emb)).astype(BF)

    pl.semaphore_wait(barrier, total)
    tf_copy = rc(tfbuf.at[c], tfbuf.at[c], s_tf, r_tf, sibling)
    tf_copy.start()

    def img_copy(j, src, x_, y_):
        return rc(
            iset.at[pl.ds(80 * src, 80)], iset.at[pl.ds(80 * j, 80)],
            s_img.at[j], r_img.at[j], dev(x_, y_ % 4, z, c),
        )

    img = {
        1: img_copy(1, 0, x, y + 1), 2: img_copy(2, 0, x, y + 2),
        3: img_copy(3, 0, x, y + 3), 4: img_copy(4, 0, 3 - x, y),
        5: img_copy(5, 4, x, y + 1), 7: img_copy(7, 4, x, y + 3),
        6: img_copy(6, 2, 3 - x, y),
    }
    for j in (4, 2, 1, 3):
        img[j].start()

    rc(tfbuf.at[sib], tfbuf.at[sib], s_tf, r_tf, sibling).wait_recv()
    tset[pl.ds(0, 80), :] = tfbuf[...].reshape(80, D).astype(BF)

    def txt_slot(core, i):
        return (i + 1) * (1 - core) + (7 - i) * core

    def txt_copy(i, p):
        src = (1 - c) * i + c * ((8 - i) % 8)
        first, rows = PIECES[p]
        return rc(
            tset.at[pl.ds(pl.multiple_of(80 * src + first, 16), rows)],
            tset.at[pl.ds(pl.multiple_of(80 * txt_slot(c, i) + first, 16), rows)],
            s_txt.at[2 * i + p], r_txt.at[2 * i + p],
            dev(x, y, (z + 1 + 6 * c) % 8, c),
        )

    def fw_copy(i, core):
        rows = pl.ds(pl.multiple_of(80 * txt_slot(core, i), 16), 80)
        return rc(tset.at[rows], tset.at[rows], s_fw.at[i], r_fw.at[i], sibling)

    txt_copy(0, 0).start()
    txt_copy(0, 1).start()

    iwin = ifeat_ref[pl.ds(pl.multiple_of(80 * c, 16), 80), :].astype(F32)
    iwin = jnp.where(xl == 0, iwin[0:40], iwin[40:80])
    for q, part in enumerate(quarters(iwin)):
        fsend[q] = part
    frecv[0] = fsend[2 * xh + yh]
    load_o.wait()
    for q, part in enumerate(quarters(dot(tfeats48, order_ref[...])[:40])):
        ftsend[q] = part
    ftrecv[0] = ftsend[z // 2]

    def ft_copy(k):
        z_, c_ = (z + k % 8) % 8, (c + k // 8) % 2
        return rc(
            ftsend.at[z_ // 2], ftrecv.at[k], s_ft, r_ft, dev(x, y, z_, c_)
        )

    def fe_copy(k):
        x_, y_ = (x + k // 4) % 4, (y + k % 4) % 4
        return rc(
            fsend.at[2 * (x_ // 2) + y_ // 2], frecv.at[k], s_fe, r_fe,
            dev(x_, y_, z, c),
        )

    def txt_hop(i):
        for p in range(2):
            txt_copy(i, p).wait_recv()
            if i == 2:
                @pl.when(c == 1)
                def _():
                    txt_copy(3, p).start()
            else:
                txt_copy(i + 1, p).start()
        fw_copy(i, c).start()

    txt_hop(0)
    img[4].wait_recv()
    img[5].start()
    img[7].start()
    txt_hop(1)
    img[2].wait_recv()
    img[6].start()
    txt_hop(2)
    img[1].wait_recv()
    img[3].wait_recv()

    @pl.loop(1, 16)
    def _(k):
        fe_copy(k).start()

    @pl.when(c == 1)
    def _():
        txt_copy(3, 0).wait_recv()
        txt_copy(3, 1).wait_recv()
        fw_copy(3, c).start()

    for i in range(3):
        fw_copy(i, sib).wait_recv()

    @pl.when(c == 0)
    def _():
        fw_copy(3, sib).wait_recv()

    @pl.loop(1, 8)
    def _(k):
        ft_copy(k).start()

    lane = lax.broadcasted_iota(jnp.int32, (1, 640), 1)
    slot = jnp.zeros((1, 640), jnp.int32)
    for m in range(1, 8):
        slot = slot + jnp.where(lane >= 80 * m, 1, 0)
    rest = lane - 80 * slot
    core = jnp.where(rest >= 40, 1, 0)
    tz = z - slot
    tz = jnp.where(tz < 0, tz + 8, tz)
    tidx = ((2 * xl + core) * 64 + (xh * 4 + y) * 8 + tz) * 40 + rest - 40 * core
    row80 = lax.broadcasted_iota(jnp.int32, (80, 1), 0)

    def tr_place(core, i):
        return (3 - i) * (1 - core) + i * core

    def sib_copy(i):
        return rc(sib_out.at[i], sib_in.at[i], s_sib.at[i], r_sib.at[i], sibling)

    def text_terms():
        for n in range(3):
            cols = pl.ds(384 * n, 384)
            tpart[:, cols] = dot_tn(coeff[...], iset[:, cols])
        for i in range(4):
            rows = pl.ds(pl.multiple_of(320 * sib + 80 * tr_place(sib, i), 16), 80)
            sib_out[i] = tpart[rows, :].astype(BF)
            sib_copy(i).start()

    def ir_copy(slot_, k):
        return rc(
            isend.at[slot_], irecv.at[k], s_ir, r_ir,
            dev((x + k // 4) % 4, (y + k % 4) % 4, z, c),
        )

    def ir_place(slot_):
        xh_ = (xh + slot_ // 8) % 2
        dx = (2 * xh_ + slot_ % 2 + 4 - x) % 4
        return 4 * dx + (4 - (slot_ // 2) % 4) % 4

    for h in range(2):
        half = pl.ds(320 * h, 320)
        if h == 1:
            for j in (5, 7, 6):
                img[j].wait_recv()

        logits = dot_nt(iset[half, :], tset[...])
        logits = scale * logits + bias
        hi = xh + h * (1 - 2 * xh)
        iidx = jnp.concatenate(
            [
                ((hi * 4 + (y + 4 - dy) % 4) * 8 + z) * 160 + 80 * c + row80
                for dy in range(4)
            ],
            axis=0,
        )
        same = iidx == tidx
        neg = jnp.where(same, logits, -logits)
        sig = 1.0 / (1.0 + jnp.exp(neg))
        part = jnp.where(same, -sig, sig).astype(BF)
        coeff[half, :] = part
        if h == 1:
            text_terms()
        for n in range(3):
            cols = pl.ds(384 * n, 384)
            ipart[half, cols] = dot(part, tset[:, cols])

        @pl.loop(8 * h, 8 * h + 8)
        def _(slot_):
            k = ir_place(slot_)

            @pl.when(k > 0)
            def _():
                isend[slot_] = pack(ipart[pl.ds(pl.multiple_of(40 * slot_, 8), 40), :])
                ir_copy(slot_, k).start()

    def tr_copy(i, p):
        rows = pl.ds(*PIECES[p])
        return rc(
            tsend.at[i, rows], trecv.at[i, rows],
            s_tr.at[2 * i + p], r_tr.at[2 * i + p],
            dev(x, y, (z + 7 + 2 * c) % 8, c),
        )

    def tr_hop(i):
        for p, (first, rows) in enumerate(PIECES):
            here = pl.ds(first, rows)
            start = pl.multiple_of(320 * c + 80 * tr_place(c, i) + first, 16)
            part = tpart[pl.ds(start, rows), :] + sib_in[i, here, :].astype(F32)
            if i > 0:
                tr_copy(i - 1, p).wait_recv()
                part = part + trecv[i - 1, here, :].astype(F32)
            tsend[i, here, :] = part.astype(BF)
            tr_copy(i, p).start()

    for i in range(3):
        sib_copy(i).wait_recv()
        tr_hop(i)
    sib_copy(3).wait_recv()

    @pl.when(c == 1)
    def _():
        tr_hop(3)
        tr_copy(3, 0).wait_recv()
        tr_copy(3, 1).wait_recv()
        side[...] = trecv[3].astype(F32)

    @pl.when(c == 0)
    def _():
        part = tpart[pl.ds(0, 80), :] + sib_in[3].astype(F32)
        tr_copy(2, 0).wait_recv()
        tr_copy(2, 1).wait_recv()
        side[...] = part + trecv[2].astype(F32)

    give = pl.ds(pl.multiple_of(40 * sib, 8), 40)
    keep = pl.ds(pl.multiple_of(40 * c, 8), 40)
    sd_copy = rc(side.at[give], side_in, s_sd, r_sd, sibling)
    sd_copy.start()
    sd_copy.wait_recv()
    tg = back_rows(temb[...], scale * (side[keep, :] + side_in[...]))
    for q, part in enumerate(quarters(tg)):
        gtsend[q] = part
    gtrecv[0] = gtsend[2 * (z % 2) + c]

    def gt_copy(k):
        z_, c_ = (z + k % 8) % 8, (c + k // 8) % 2
        return rc(
            gtsend.at[2 * (z_ % 2) + c_], gtrecv.at[k], s_gt, r_gt,
            dev(x, y, z_, c_),
        )

    @pl.loop(1, 16)
    def _(k):
        gt_copy(k).start()

    line = pl.ds(1, 7)
    all_ft = rc(ftrecv.at[line], ftrecv.at[line], s_ft, r_ft, sibling)
    all_ft.wait_recv()
    ff_copy = rc(
        ftrecv.at[pl.ds(0, 8)], ftrecv.at[pl.ds(8, 8)], s_ff, r_ff, sibling
    )
    ff_copy.start()

    many = pl.ds(1, 15)
    rc(isend.at[many], irecv.at[many], s_ir, r_ir, sibling).wait_recv()

    acc = irecv[1].astype(F32)
    for k in range(2, 16):
        acc = acc + irecv[k].astype(F32)
    mine = pl.ds(pl.multiple_of(40 * xl, 8), 40)
    ig = back_rows(iemb[mine, :], scale * (unpack(acc) + ipart[mine, :]))
    for q, part in enumerate(quarters(ig)):
        gsend[q] = part
    grecv[0] = gsend[2 * xl + yl]

    def gr_copy(k):
        x_, y_ = (x + k // 4) % 4, (y + k % 4) % 4
        return rc(
            gsend.at[2 * (x_ % 2) + y_ % 2], grecv.at[k], s_gr, r_gr,
            dev(x_, y_, z, c),
        )

    @pl.loop(1, 16)
    def _(k):
        gr_copy(k).start()

    place = 2 * c + xl
    egath[place] = pack(ig)

    def eg_copy(k, s):
        xl_, c_ = (xl + k % 2) % 2, (c + k // 2) % 2
        return rc(
            egath.at[s], egath.at[s], s_eg.at[k], r_eg.at[k],
            (2 * xl_ + c_, gr),
        )

    @pl.loop(1, 4)
    def _(k):
        eg_copy(k, place).start()

    tg48 = jnp.concatenate([tg, jnp.zeros((8, D), F32)], axis=0).astype(BF)
    tgrad_ref[...] = dot_nt(tg48, tproj_ref[...])[:40]
    out_t = pltpu.make_async_copy(tgrad_ref, tgrad_hbm, s_loc.at[2])
    out_t.start()

    all_fe = rc(frecv.at[many], frecv.at[many], s_fe, r_fe, sibling)
    all_fe.wait_recv()

    all_gr = rc(grecv.at[many], grecv.at[many], s_gr, r_gr, sibling)
    all_gr.wait_recv()

    wipart[...] = dot_tn(join(frecv[...]), join(grecv[...]))

    def w_block(m, u):
        first = 144 * u + 18 * ((z + m) % 8)
        return pack_block(wipart[pl.ds(pl.multiple_of(8 * (first // 8), 8), 24), :])

    @pl.loop(0, 8)
    def _(k):
        wgive[k] = w_block(4 * sib + k % 4, k // 4).astype(BF)

    ws_copy = rc(wgive, wtake, s_ws, r_ws, sibling)
    ws_copy.start()

    all_gt = rc(gtrecv.at[many], gtrecv.at[many], s_gt, r_gt, sibling)
    ff_copy.wait_recv()
    all_gt.wait_recv()

    wtpart[...] = dot_tn(join(ftrecv[...]), join(gtrecv[...]))

    def wt_copy(k, slot_):
        return rc(
            wtsend.at[k], wtrecv.at[slot_], s_wt.at[k], r_wt.at[slot_],
            dev(2 * (k // 8) + z % 2, (k // 2) % 4, 2 * (z // 2) + k % 2, c),
        )

    def wt_self(k):
        return lone_t & (k == 2 * (4 * xh + y) + z % 2)

    @pl.loop(0, 16)
    def _(k):
        first = pl.multiple_of(8 * ((18 * k) // 8), 8)
        wtsend[k] = pack_block(wtpart[pl.ds(first, 24), :]).astype(BF)
        dx = (2 * (k // 8) + z % 2 + 4 - x) % 4
        dy = ((k // 2) % 4 + 4 - y) % 4

        @pl.when(jnp.logical_not(wt_self(k)))
        def _():
            wt_copy(k, 4 * dx + dy).start()

        @pl.when(wt_self(k))
        def _():
            wtrecv[0] = wtsend[k]

    ws_copy.wait_recv()

    def w_copy(k, m):
        return rc(
            wsend.at[k], wrecv.at[m], s_w.at[k], r_w.at[m],
            dev(x, 2 * yh + k // 4, (z + 4 * c + k % 4) % 8, yl),
        )

    @pl.loop(0, 8)
    def _(k):
        block = w_block(4 * c + k % 4, k // 4)
        wsend[k] = (block + wtake[k].astype(F32)).astype(BF)

        @pl.when(jnp.logical_not(lone & (k == 0)))
        def _():
            w_copy(k, 4 * c + k % 4).start()

    @pl.when(lone)
    def _():
        wrecv[0] = wsend[0]

    @pl.loop(1, 4)
    def _(k):
        xl_, c_ = (xl + k % 2) % 2, (c + k // 2) % 2
        eg_copy(k, 2 * c_ + xl_).wait_recv()

    parts = [unpack(egath[s].astype(F32)) for s in range(4)]
    igrad_ref[...] = dot_nt(jnp.concatenate(parts, axis=0).astype(BF), iproj_ref[...])
    out_i = pltpu.make_async_copy(igrad_ref, igrad_hbm, s_loc.at[3])
    out_i.start()

    @pl.loop(0, 8)
    def _(m):
        @pl.when(jnp.logical_not(lone & (m == 0)))
        def _():
            w_copy(m, m).wait_recv()

    @pl.loop(0, 16)
    def _(k):
        @pl.when(jnp.logical_not(lone_t & (k == 0)))
        def _():
            wt_copy(k, k).wait_recv()

    acc = wrecv[0].astype(F32)
    for m in range(1, 8):
        acc = acc + wrecv[m].astype(F32)
    acc_i = unpack_block(acc)
    acc = wtrecv[0].astype(F32)
    for m in range(1, 16):
        acc = acc + wtrecv[m].astype(F32)
    acc_t = unpack_block(acc)
    for k in range(0, 8, 2):
        @pl.when((18 * z) % 8 == k)
        def _():
            iw_ref[...] = acc_i[k:k + 18, 0:288]

        @pl.when((36 * (4 * xh + y) + 18 * (z % 2)) % 8 == k)
        def _():
            tw_ref[...] = acc_t[k:k + 18, 0:288]
    out_iw = pltpu.make_async_copy(iw_ref, iw_hbm, s_loc.at[4])
    out_tw = pltpu.make_async_copy(tw_ref, tw_hbm, s_loc.at[5])
    out_iw.start()
    out_tw.start()

    tf_copy.wait_send()
    for i in range(4):
        sib_copy(i).wait_send()
    sd_copy.wait_send()
    ws_copy.wait_send()
    ff_copy.wait_send()

    for j in range(1, 8):
        img[j].wait_send()
    for i in range(3):
        fw_copy(i, c).wait_send()
        for p in range(2):
            txt_copy(i, p).wait_send()
            tr_copy(i, p).wait_send()

    @pl.when(c == 1)
    def _():
        fw_copy(3, c).wait_send()
        for p in range(2):
            txt_copy(3, p).wait_send()
            tr_copy(3, p).wait_send()

    @pl.loop(1, 4)
    def _(k):
        eg_copy(k, place).wait_send()

    rc(isend.at[many], irecv.at[many], s_ir, r_ir, sibling).wait_send()
    for group in (all_fe, all_ft, all_gr, all_gt):
        group.wait_send()

    @pl.loop(0, 16)
    def _(slot_):
        @pl.when(jnp.logical_not(wt_self(slot_)))
        def _():
            wt_copy(slot_, 0).wait_send()

    @pl.loop(0, 8)
    def _(k):
        @pl.when(jnp.logical_not(lone & (k == 0)))
        def _():
            w_copy(k, 4 * c + k % 4).wait_send()

    out_t.wait()
    out_i.wait()
    out_iw.wait()
    out_tw.wait()


def hand_over(*refs):
    held, sems = refs[8:12], refs[12]
    loads = [pltpu.make_async_copy(refs[i], held[i], sems.at[i]) for i in range(4)]
    stores = [
        pltpu.make_async_copy(held[i], refs[4 + i], sems.at[4 + i]) for i in range(4)
    ]
    for load in loads:
        load.start()
    for load, store in zip(loads, stores):
        load.wait()
        store.start()
    for store in stores:
        store.wait()


def per_device(image_feats, text_feats, image_proj, text_proj, logit_scale, logit_bias):
    order = jnp.asarray(by_z_pair(), BF)
    smem = pl.BlockSpec(memory_space=pltpu.SMEM)
    hbm = pl.BlockSpec(memory_space=pl.ANY)
    sems = []
    for n in (0, 8, 8, 8, 4, 8, 0, 0, 4, 0, 0, 8, 0, 0, 0, 16, 0):
        for _ in range(2):
            sems.append(pltpu.SemaphoreType.DMA((n,)) if n else pltpu.SemaphoreType.DMA)
    out_shape = (
        jax.ShapeDtypeStruct((160, D), F32),
        jax.ShapeDtypeStruct((40, D), F32),
        jax.ShapeDtypeStruct((18, 288), F32),
        jax.ShapeDtypeStruct((18, 288), F32),
    )
    results = pl.pallas_call(
        kernel,
        out_shape=out_shape,
        in_specs=[smem, smem, hbm, hbm, hbm, hbm, hbm],
        out_specs=(hbm, hbm, hbm, hbm),
        scratch_shapes=[
            pltpu.VMEM((160, D), BF),
            pltpu.VMEM((40, D), BF),
            pltpu.VMEM((D, D), BF),
            pltpu.VMEM((D, D), BF),
            pltpu.VMEM((D, D), BF),
            pltpu.VMEM((160, D), F32),
            pltpu.VMEM((40, D), F32),
            pltpu.VMEM((18, 288), F32),
            pltpu.VMEM((18, 288), F32),
            pltpu.VMEM((2, 40, D), F32),
            pltpu.VMEM((80, D), F32),
            pltpu.VMEM((40, D), F32),
            pltpu.VMEM((640, D), BF),
            pltpu.VMEM((640, D), BF),
            pltpu.VMEM((640, 640), BF),
            pltpu.VMEM((640, D), F32),
            pltpu.VMEM((640, D), F32),
            pltpu.VMEM((4, 80, D), BF),
            pltpu.VMEM((4, 80, D), BF),
            pltpu.VMEM((16, 368, 128), BF),
            pltpu.VMEM((4, 80, D), BF),
            pltpu.VMEM((4, 80, D), BF),
            pltpu.VMEM((80, D), F32),
            pltpu.VMEM((40, D), F32),
            pltpu.VMEM((16, 368, 128), BF),
            pltpu.VMEM((4, 368, 128), BF),
            pltpu.VMEM((4, 96, 128), BF),
            pltpu.VMEM((16, 96, 128), BF),
            pltpu.VMEM((4, 96, 128), BF),
            pltpu.VMEM((16, 96, 128), BF),
            pltpu.VMEM((4, 96, 128), BF),
            pltpu.VMEM((16, 96, 128), BF),
            pltpu.VMEM((4, 96, 128), BF),
            pltpu.VMEM((16, 96, 128), BF),
            pltpu.VMEM((384, 384), F32),
            pltpu.VMEM((384, 384), F32),
            pltpu.VMEM((8, 64, 128), BF),
            pltpu.VMEM((8, 64, 128), BF),
            pltpu.VMEM((8, 64, 128), BF),
            pltpu.VMEM((8, 64, 128), BF),
            pltpu.VMEM((16, 64, 128), BF),
            pltpu.VMEM((16, 64, 128), BF),
            *sems,
            pltpu.SemaphoreType.DMA((9,)),
        ],
        compiler_params=pltpu.CompilerParams(
            collective_id=0, has_side_effects=True, vmem_limit_bytes=56 * 2**20
        ),
        cost_estimate=pl.CostEstimate(
            flops=4 * 10**9, bytes_accessed=8 * 10**6, transcendentals=409600
        ),
    )(logit_scale, logit_bias, image_feats, text_feats, image_proj, text_proj, order)
    return pl.pallas_call(
        hand_over,
        out_shape=out_shape,
        in_specs=[hbm, hbm, hbm, hbm],
        out_specs=(hbm, hbm, hbm, hbm),
        scratch_shapes=[
            *(pltpu.VMEM(shape.shape, F32) for shape in out_shape),
            pltpu.SemaphoreType.DMA((8,)),
        ],
    )(*results)


def solution(mesh):
    placed = (P("group", None), P(("blk", "group"), None), P(), P(), P(), P())
    return jax.shard_map(
        per_device,
        mesh=mesh,
        in_specs=placed,
        out_specs=(
            P("group", None),
            P(("blk", "group"), None),
            P("group", "blk"),
            P("group", "blk"),
        ),
        check_vma=False,
    )
```

```python
import jax
import jax.numpy as jnp
import numpy as np
from jax import lax
from jax.experimental import pallas as pl
from jax.experimental.pallas import tpu as pltpu
from jax.sharding import PartitionSpec as P

D = 1152
PIECES = ((0, 48), (48, 32))
MESH = pl.DeviceIdType.MESH
BF = jnp.bfloat16
F32 = jnp.float32
NT = (((1,), (1,)), ((), ()))
TN = (((0,), (0,)), ((), ()))


def dot(a, b):
    return jnp.dot(a, b, preferred_element_type=F32)


def dot_nt(a, b):
    return lax.dot_general(a, b, NT, preferred_element_type=F32)


def dot_tn(a, b):
    return lax.dot_general(a, b, TN, preferred_element_type=F32)


def row_norm(e):
    return jnp.sqrt(jnp.sum(e * e, axis=-1, keepdims=True) + 1e-06)


def back_rows(e, g):
    norm = row_norm(e)
    u = e / norm
    return (g - u * jnp.sum(u * g, axis=-1, keepdims=True)) / norm


def pack(rows):
    tiles = [rows[:, 128 * t:128 * t + 128] for t in range(9)]
    return jnp.concatenate(tiles + [jnp.zeros((8, 128), F32)], axis=0).astype(BF)


def unpack(tiles):
    return jnp.concatenate([tiles[40 * t:40 * t + 40] for t in range(9)], axis=1)


def fold(tile, step):
    lane = lax.broadcasted_iota(jnp.int32, (step, 128), 1)
    out = tile[0:step]
    for g in range(1, tile.shape[0] // step):
        part = pltpu.roll(tile[g * step:g * step + step], 32 * g, 1)
        out = jnp.where(lane < 32 * g, out, part)
    return out


def quarters(rows):
    parts = []
    for q in range(4):
        a = (rows if q == 0 else pltpu.roll(rows, D - 288 * q, 1))[:, :384]
        last = jnp.concatenate([a[:, 256:384], jnp.zeros((8, 128), F32)], axis=0)
        tiles = [a[:, 0:128], a[:, 128:256], fold(last, 16)]
        parts.append(jnp.concatenate(tiles, axis=0).astype(BF))
    return parts


def join(packed):
    packed = packed.astype(F32)
    last = packed[:, 80:96].reshape(256, 128)
    groups = [last] + [pltpu.roll(last, 128 - 32 * g, 1) for g in (1, 2)]
    groups = [group.reshape(16, 16, 128) for group in groups]
    last = jnp.concatenate([groups[0], groups[1], groups[2][:, 0:8]], axis=1)
    tiles = [packed[:, 0:40], packed[:, 40:80], last]
    return jnp.concatenate([t.reshape(640, 128) for t in tiles], axis=1).astype(BF)


def pack_block(rows):
    last = fold(rows[:, 256:384], 8)
    tiles = [rows[:, 0:128], rows[:, 128:256], last, jnp.zeros((8, 128), F32)]
    return jnp.concatenate(tiles, axis=0)


def unpack_block(tiles):
    last = tiles[48:56]
    last = [last] + [pltpu.roll(last, 128 - 32 * g, 1) for g in (1, 2)]
    parts = [tiles[0:24], tiles[24:48], jnp.concatenate(last, axis=0)]
    return jnp.concatenate(parts, axis=1)


def by_z_pair():
    place = np.arange(D)
    h, s, t = place // 288, place % 288 // 36, place % 36
    order = np.zeros((D, D), np.float32)
    order[144 * s + 36 * h + t, place] = 1.0
    return order


def kernel(
    scale_ref, bias_ref, ifeat_hbm, tfeat_hbm, iproj_hbm, tproj_hbm, order_hbm,
    igrad_hbm, tgrad_hbm, iw_hbm, tw_hbm,
    ifeat_ref, tfeat_ref, iproj_ref, tproj_ref, order_ref, igrad_ref, tgrad_ref, iw_ref, tw_ref,
    tfbuf, iemb, temb, iset, tset, coeff, ipart, tpart, sib_out, sib_in,
    isend, tsend, trecv, side, side_in, irecv, egath, fsend, frecv, gsend, grecv,
    ftsend, ftrecv, gtsend, gtrecv, wipart, wtpart, wgive, wtake, wsend, wrecv,
    wtsend, wtrecv,
    s_tf, r_tf, s_img, r_img, s_txt, r_txt, s_fw, r_fw, s_sib, r_sib, s_tr, r_tr,
    s_sd, r_sd, s_ir, r_ir, s_eg, r_eg, s_fe, r_fe, s_gr, r_gr, s_w, r_w,
    s_ws, r_ws, s_ft, r_ft, s_gt, r_gt, s_wt, r_wt, s_ff, r_ff, s_loc,
):
    bl = lax.axis_index("blk")
    gr = lax.axis_index("group")
    xl, c = bl // 2, bl % 2
    xh, y, z = gr // 32, (gr // 8) % 4, gr % 8
    x = 2 * xh + xl
    sib = 1 - c
    yh, yl = y // 2, y % 2
    scale = scale_ref[0]
    bias = bias_ref[0]

    def dev(x_, y_, z_, c_):
        return ((x_ % 2) * 2 + c_, ((x_ // 2) * 4 + y_) * 8 + z_)

    def rc(src, dst, ss, rs, to):
        return pltpu.make_async_remote_copy(
            src_ref=src, dst_ref=dst, send_sem=ss, recv_sem=rs,
            device_id=to, device_id_type=MESH,
        )

    sibling = dev(x, y, z, sib)
    lone = (c == 0) & (yl == 0)
    lone_t = xl == z % 2
    pair = z + 1 - 2 * (z % 2)

    load_tf = pltpu.make_async_copy(tfeat_hbm, tfeat_ref, s_loc.at[8])
    load_t = pltpu.make_async_copy(tproj_hbm, tproj_ref, s_loc.at[1])
    load_if = pltpu.make_async_copy(ifeat_hbm, ifeat_ref, s_loc.at[7])
    load_i = pltpu.make_async_copy(iproj_hbm, iproj_ref, s_loc.at[0])
    load_tf.start()
    load_t.start()
    load_if.start()
    load_i.start()
    load_o = pltpu.make_async_copy(order_hbm, order_ref, s_loc.at[6])
    load_o.start()
    barrier = pltpu.get_barrier_semaphore()

    def greet(to):
        pl.semaphore_signal(barrier, inc=1, device_id=to, device_id_type=MESH)

    greet(sibling)
    greet(dev(x + 1 - 2 * xl, y, z, sib))

    @pl.loop(1, 8)
    def _(m):
        greet(dev(x, y, (z + m) % 8, 0))
        greet(dev(x, y, (z + m) % 8, 1))

    @pl.loop(0, 8)
    def _(k):
        greet(dev(2 * (k // 4) + z % 2, k % 4, pair, c))

    @pl.when(jnp.logical_not(lone_t))
    def _():
        @pl.loop(0, 16)
        def _(k):
            greet(dev(k // 4, k % 4, pair, c))

    @pl.loop(1, 16)
    def _(k):
        greet(dev((x + k // 4) % 4, (y + k % 4) % 4, z, c))

    @pl.loop(0, 4)
    def _(k):
        greet(dev(x, 2 * yh + 1 - yl, (z + 4 * c + k) % 8, yl))

    @pl.when(c != yl)
    def _():
        @pl.loop(0, 8)
        def _(k):
            greet(dev(x, 2 * yh + c, (z + 8 - k) % 8, k // 4))

    total = 1 + 1 + 14 + 8 + 15 + 4 + jnp.where(c == yl, 0, 8)
    total = total + jnp.where(lone_t, 0, 16)

    load_tf.wait()
    load_t.wait()
    tfeats = tfeat_ref[...].astype(F32)
    tfeats48 = jnp.concatenate([tfeats, jnp.zeros((8, D), F32)], axis=0).astype(BF)
    emb = dot(tfeats48, tproj_ref[...])[:40]
    temb[...] = emb
    tfbuf[c] = emb / row_norm(emb)

    load_if.wait()
    load_i.wait()
    emb = dot(ifeat_ref[pl.ds(pl.multiple_of(80 * c, 16), 80), :], iproj_ref[...])
    iemb[...] = emb
    iset[pl.ds(0, 80), :] = (emb / row_norm(emb)).astype(BF)

    pl.semaphore_wait(barrier, total)
    tf_copy = rc(tfbuf.at[c], tfbuf.at[c], s_tf, r_tf, sibling)
    tf_copy.start()

    def img_copy(j, src, x_, y_):
        return rc(
            iset.at[pl.ds(80 * src, 80)], iset.at[pl.ds(80 * j, 80)],
            s_img.at[j], r_img.at[j], dev(x_, y_ % 4, z, c),
        )

    img = {
        1: img_copy(1, 0, x, y + 1), 2: img_copy(2, 0, x, y + 2),
        3: img_copy(3, 0, x, y + 3), 4: img_copy(4, 0, 3 - x, y),
        5: img_copy(5, 4, x, y + 1), 7: img_copy(7, 4, x, y + 3),
        6: img_copy(6, 2, 3 - x, y),
    }
    for j in (4, 2, 1, 3):
        img[j].start()

    rc(tfbuf.at[sib], tfbuf.at[sib], s_tf, r_tf, sibling).wait_recv()
    tset[pl.ds(0, 80), :] = tfbuf[...].reshape(80, D).astype(BF)

    def txt_slot(core, i):
        return (i + 1) * (1 - core) + (7 - i) * core

    def txt_copy(i, p):
        src = (1 - c) * i + c * ((8 - i) % 8)
        first, rows = PIECES[p]
        return rc(
            tset.at[pl.ds(pl.multiple_of(80 * src + first, 16), rows)],
            tset.at[pl.ds(pl.multiple_of(80 * txt_slot(c, i) + first, 16), rows)],
            s_txt.at[2 * i + p], r_txt.at[2 * i + p],
            dev(x, y, (z + 1 + 6 * c) % 8, c),
        )

    def fw_copy(i, core):
        rows = pl.ds(pl.multiple_of(80 * txt_slot(core, i), 16), 80)
        return rc(tset.at[rows], tset.at[rows], s_fw.at[i], r_fw.at[i], sibling)

    txt_copy(0, 0).start()
    txt_copy(0, 1).start()

    iwin = ifeat_ref[pl.ds(pl.multiple_of(80 * c, 16), 80), :].astype(F32)
    iwin = jnp.where(xl == 0, iwin[0:40], iwin[40:80])
    for q, part in enumerate(quarters(iwin)):
        fsend[q] = part
    frecv[0] = fsend[2 * xh + yh]
    load_o.wait()
    for q, part in enumerate(quarters(dot(tfeats48, order_ref[...])[:40])):
        ftsend[q] = part
    ftrecv[0] = ftsend[z // 2]

    def ft_copy(k):
        z_, c_ = (z + k % 8) % 8, (c + k // 8) % 2
        return rc(
            ftsend.at[z_ // 2], ftrecv.at[k], s_ft, r_ft, dev(x, y, z_, c_)
        )

    def fe_copy(k):
        x_, y_ = (x + k // 4) % 4, (y + k % 4) % 4
        return rc(
            fsend.at[2 * (x_ // 2) + y_ // 2], frecv.at[k], s_fe, r_fe,
            dev(x_, y_, z, c),
        )

    def txt_hop(i):
        for p in range(2):
            txt_copy(i, p).wait_recv()
            if i == 2:
                @pl.when(c == 1)
                def _():
                    txt_copy(3, p).start()
            else:
                txt_copy(i + 1, p).start()
        fw_copy(i, c).start()

    txt_hop(0)
    img[4].wait_recv()
    img[5].start()
    img[7].start()
    txt_hop(1)
    img[2].wait_recv()
    img[6].start()
    txt_hop(2)
    img[1].wait_recv()
    img[3].wait_recv()

    @pl.loop(1, 16)
    def _(k):
        fe_copy(k).start()

    @pl.when(c == 1)
    def _():
        txt_copy(3, 0).wait_recv()
        txt_copy(3, 1).wait_recv()
        fw_copy(3, c).start()

    for i in range(3):
        fw_copy(i, sib).wait_recv()

    @pl.when(c == 0)
    def _():
        fw_copy(3, sib).wait_recv()

    @pl.loop(1, 8)
    def _(k):
        ft_copy(k).start()

    lane = lax.broadcasted_iota(jnp.int32, (1, 640), 1)
    slot = jnp.zeros((1, 640), jnp.int32)
    for m in range(1, 8):
        slot = slot + jnp.where(lane >= 80 * m, 1, 0)
    rest = lane - 80 * slot
    core = jnp.where(rest >= 40, 1, 0)
    tz = z - slot
    tz = jnp.where(tz < 0, tz + 8, tz)
    tidx = ((2 * xl + core) * 64 + (xh * 4 + y) * 8 + tz) * 40 + rest - 40 * core
    row80 = lax.broadcasted_iota(jnp.int32, (80, 1), 0)

    def tr_place(core, i):
        return (3 - i) * (1 - core) + i * core

    def sib_copy(i):
        return rc(sib_out.at[i], sib_in.at[i], s_sib.at[i], r_sib.at[i], sibling)

    def text_terms():
        for n in range(3):
            cols = pl.ds(384 * n, 384)
            tpart[:, cols] = dot_tn(coeff[...], iset[:, cols])
        for i in range(4):
            rows = pl.ds(pl.multiple_of(320 * sib + 80 * tr_place(sib, i), 16), 80)
            sib_out[i] = tpart[rows, :].astype(BF)
            sib_copy(i).start()

    def ir_copy(slot_, k):
        return rc(
            isend.at[slot_], irecv.at[k], s_ir, r_ir,
            dev((x + k // 4) % 4, (y + k % 4) % 4, z, c),
        )

    def ir_place(slot_):
        xh_ = (xh + slot_ // 8) % 2
        dx = (2 * xh_ + slot_ % 2 + 4 - x) % 4
        return 4 * dx + (4 - (slot_ // 2) % 4) % 4

    for h in range(2):
        half = pl.ds(320 * h, 320)
        if h == 1:
            for j in (5, 7, 6):
                img[j].wait_recv()

        logits = dot_nt(iset[half, :], tset[...])
        logits = scale * logits + bias
        hi = xh + h * (1 - 2 * xh)
        iidx = jnp.concatenate(
            [
                ((hi * 4 + (y + 4 - dy) % 4) * 8 + z) * 160 + 80 * c + row80
                for dy in range(4)
            ],
            axis=0,
        )
        same = iidx == tidx
        neg = jnp.where(same, logits, -logits)
        sig = 1.0 / (1.0 + jnp.exp(neg))
        part = jnp.where(same, -sig, sig).astype(BF)
        coeff[half, :] = part
        if h == 1:
            text_terms()
        for n in range(3):
            cols = pl.ds(384 * n, 384)
            ipart[half, cols] = dot(part, tset[:, cols])

        @pl.loop(8 * h, 8 * h + 8)
        def _(slot_):
            k = ir_place(slot_)

            @pl.when(k > 0)
            def _():
                isend[slot_] = pack(ipart[pl.ds(pl.multiple_of(40 * slot_, 8), 40), :])
                ir_copy(slot_, k).start()

    def tr_copy(i, p):
        rows = pl.ds(*PIECES[p])
        return rc(
            tsend.at[i, rows], trecv.at[i, rows],
            s_tr.at[2 * i + p], r_tr.at[2 * i + p],
            dev(x, y, (z + 7 + 2 * c) % 8, c),
        )

    def tr_hop(i):
        for p, (first, rows) in enumerate(PIECES):
            here = pl.ds(first, rows)
            start = pl.multiple_of(320 * c + 80 * tr_place(c, i) + first, 16)
            part = tpart[pl.ds(start, rows), :] + sib_in[i, here, :].astype(F32)
            if i > 0:
                tr_copy(i - 1, p).wait_recv()
                part = part + trecv[i - 1, here, :].astype(F32)
            tsend[i, here, :] = part.astype(BF)
            tr_copy(i, p).start()

    for i in range(3):
        sib_copy(i).wait_recv()
        tr_hop(i)
    sib_copy(3).wait_recv()

    @pl.when(c == 1)
    def _():
        tr_hop(3)
        tr_copy(3, 0).wait_recv()
        tr_copy(3, 1).wait_recv()
        side[...] = trecv[3].astype(F32)

    @pl.when(c == 0)
    def _():
        part = tpart[pl.ds(0, 80), :] + sib_in[3].astype(F32)
        tr_copy(2, 0).wait_recv()
        tr_copy(2, 1).wait_recv()
        side[...] = part + trecv[2].astype(F32)

    give = pl.ds(pl.multiple_of(40 * sib, 8), 40)
    keep = pl.ds(pl.multiple_of(40 * c, 8), 40)
    sd_copy = rc(side.at[give], side_in, s_sd, r_sd, sibling)
    sd_copy.start()
    sd_copy.wait_recv()
    tg = back_rows(temb[...], scale * (side[keep, :] + side_in[...]))
    for q, part in enumerate(quarters(tg)):
        gtsend[q] = part
    gtrecv[0] = gtsend[2 * (z % 2) + c]

    def gt_copy(k):
        z_, c_ = (z + k % 8) % 8, (c + k // 8) % 2
        return rc(
            gtsend.at[2 * (z_ % 2) + c_], gtrecv.at[k], s_gt, r_gt,
            dev(x, y, z_, c_),
        )

    @pl.loop(1, 16)
    def _(k):
        gt_copy(k).start()

    line = pl.ds(1, 7)
    all_ft = rc(ftrecv.at[line], ftrecv.at[line], s_ft, r_ft, sibling)
    all_ft.wait_recv()
    ff_copy = rc(
        ftrecv.at[pl.ds(0, 8)], ftrecv.at[pl.ds(8, 8)], s_ff, r_ff, sibling
    )
    ff_copy.start()

    many = pl.ds(1, 15)
    rc(isend.at[many], irecv.at[many], s_ir, r_ir, sibling).wait_recv()

    acc = irecv[1].astype(F32)
    for k in range(2, 16):
        acc = acc + irecv[k].astype(F32)
    mine = pl.ds(pl.multiple_of(40 * xl, 8), 40)
    ig = back_rows(iemb[mine, :], scale * (unpack(acc) + ipart[mine, :]))
    for q, part in enumerate(quarters(ig)):
        gsend[q] = part
    grecv[0] = gsend[2 * xl + yl]

    def gr_copy(k):
        x_, y_ = (x + k // 4) % 4, (y + k % 4) % 4
        return rc(
            gsend.at[2 * (x_ % 2) + y_ % 2], grecv.at[k], s_gr, r_gr,
            dev(x_, y_, z, c),
        )

    @pl.loop(1, 16)
    def _(k):
        gr_copy(k).start()

    place = 2 * c + xl
    egath[place] = pack(ig)

    def eg_copy(k, s):
        xl_, c_ = (xl + k % 2) % 2, (c + k // 2) % 2
        return rc(
            egath.at[s], egath.at[s], s_eg.at[k], r_eg.at[k],
            (2 * xl_ + c_, gr),
        )

    @pl.loop(1, 4)
    def _(k):
        eg_copy(k, place).start()

    tg48 = jnp.concatenate([tg, jnp.zeros((8, D), F32)], axis=0).astype(BF)
    tgrad_ref[...] = dot_nt(tg48, tproj_ref[...])[:40]
    out_t = pltpu.make_async_copy(tgrad_ref, tgrad_hbm, s_loc.at[2])
    out_t.start()

    all_fe = rc(frecv.at[many], frecv.at[many], s_fe, r_fe, sibling)
    all_fe.wait_recv()

    all_gr = rc(grecv.at[many], grecv.at[many], s_gr, r_gr, sibling)
    all_gr.wait_recv()

    wipart[...] = dot_tn(join(frecv[...]), join(grecv[...]))

    def w_block(m, u):
        first = 144 * u + 18 * ((z + m) % 8)
        return pack_block(wipart[pl.ds(pl.multiple_of(8 * (first // 8), 8), 24), :])

    @pl.loop(0, 8)
    def _(k):
        wgive[k] = w_block(4 * sib + k % 4, k // 4).astype(BF)

    ws_copy = rc(wgive, wtake, s_ws, r_ws, sibling)
    ws_copy.start()

    all_gt = rc(gtrecv.at[many], gtrecv.at[many], s_gt, r_gt, sibling)
    ff_copy.wait_recv()
    all_gt.wait_recv()

    wtpart[...] = dot_tn(join(ftrecv[...]), join(gtrecv[...]))

    def wt_copy(k, slot_):
        return rc(
            wtsend.at[k], wtrecv.at[slot_], s_wt.at[k], r_wt.at[slot_],
            dev(2 * (k // 8) + z % 2, (k // 2) % 4, 2 * (z // 2) + k % 2, c),
        )

    def wt_self(k):
        return lone_t & (k == 2 * (4 * xh + y) + z % 2)

    ws_copy.wait_recv()

    def w_copy(k, m):
        return rc(
            wsend.at[k], wrecv.at[m], s_w.at[k], r_w.at[m],
            dev(x, 2 * yh + k // 4, (z + 4 * c + k % 4) % 8, yl),
        )

    @pl.loop(0, 8)
    def _(k):
        block = w_block(4 * c + k % 4, k // 4)
        wsend[k] = (block + wtake[k].astype(F32)).astype(BF)

        @pl.when(jnp.logical_not(lone & (k == 0)))
        def _():
            w_copy(k, 4 * c + k % 4).start()

    @pl.when(lone)
    def _():
        wrecv[0] = wsend[0]

    @pl.loop(0, 16)
    def _(k):
        first = pl.multiple_of(8 * ((18 * k) // 8), 8)
        wtsend[k] = pack_block(wtpart[pl.ds(first, 24), :]).astype(BF)
        dx = (2 * (k // 8) + z % 2 + 4 - x) % 4
        dy = ((k // 2) % 4 + 4 - y) % 4

        @pl.when(jnp.logical_not(wt_self(k)))
        def _():
            wt_copy(k, 4 * dx + dy).start()

        @pl.when(wt_self(k))
        def _():
            wtrecv[0] = wtsend[k]

    @pl.loop(1, 4)
    def _(k):
        xl_, c_ = (xl + k % 2) % 2, (c + k // 2) % 2
        eg_copy(k, 2 * c_ + xl_).wait_recv()

    parts = [unpack(egath[s].astype(F32)) for s in range(4)]
    igrad_ref[...] = dot_nt(jnp.concatenate(parts, axis=0).astype(BF), iproj_ref[...])
    out_i = pltpu.make_async_copy(igrad_ref, igrad_hbm, s_loc.at[3])
    out_i.start()

    @pl.loop(0, 8)
    def _(m):
        @pl.when(jnp.logical_not(lone & (m == 0)))
        def _():
            w_copy(m, m).wait_recv()

    @pl.loop(0, 16)
    def _(k):
        @pl.when(jnp.logical_not(lone_t & (k == 0)))
        def _():
            wt_copy(k, k).wait_recv()

    acc = wrecv[0].astype(F32)
    for m in range(1, 8):
        acc = acc + wrecv[m].astype(F32)
    acc_i = unpack_block(acc)
    acc = wtrecv[0].astype(F32)
    for m in range(1, 16):
        acc = acc + wtrecv[m].astype(F32)
    acc_t = unpack_block(acc)
    for k in range(0, 8, 2):
        @pl.when((18 * z) % 8 == k)
        def _():
            iw_ref[...] = acc_i[k:k + 18, 0:288]

        @pl.when((36 * (4 * xh + y) + 18 * (z % 2)) % 8 == k)
        def _():
            tw_ref[...] = acc_t[k:k + 18, 0:288]
    out_iw = pltpu.make_async_copy(iw_ref, iw_hbm, s_loc.at[4])
    out_tw = pltpu.make_async_copy(tw_ref, tw_hbm, s_loc.at[5])
    out_iw.start()
    out_tw.start()

    tf_copy.wait_send()
    for i in range(4):
        sib_copy(i).wait_send()
    sd_copy.wait_send()
    ws_copy.wait_send()
    ff_copy.wait_send()

    for j in range(1, 8):
        img[j].wait_send()
    for i in range(3):
        fw_copy(i, c).wait_send()
        for p in range(2):
            txt_copy(i, p).wait_send()
            tr_copy(i, p).wait_send()

    @pl.when(c == 1)
    def _():
        fw_copy(3, c).wait_send()
        for p in range(2):
            txt_copy(3, p).wait_send()
            tr_copy(3, p).wait_send()

    @pl.loop(1, 4)
    def _(k):
        eg_copy(k, place).wait_send()

    rc(isend.at[many], irecv.at[many], s_ir, r_ir, sibling).wait_send()
    for group in (all_fe, all_ft, all_gr, all_gt):
        group.wait_send()

    @pl.loop(0, 16)
    def _(slot_):
        @pl.when(jnp.logical_not(wt_self(slot_)))
        def _():
            wt_copy(slot_, 0).wait_send()

    @pl.loop(0, 8)
    def _(k):
        @pl.when(jnp.logical_not(lone & (k == 0)))
        def _():
            w_copy(k, 4 * c + k % 4).wait_send()

    out_t.wait()
    out_i.wait()
    out_iw.wait()
    out_tw.wait()


def hand_over(*refs):
    held, sems = refs[8:12], refs[12]
    loads = [pltpu.make_async_copy(refs[i], held[i], sems.at[i]) for i in range(4)]
    stores = [
        pltpu.make_async_copy(held[i], refs[4 + i], sems.at[4 + i]) for i in range(4)
    ]
    for load in loads:
        load.start()
    for load, store in zip(loads, stores):
        load.wait()
        store.start()
    for store in stores:
        store.wait()


def per_device(image_feats, text_feats, image_proj, text_proj, logit_scale, logit_bias):
    order = jnp.asarray(by_z_pair(), BF)
    smem = pl.BlockSpec(memory_space=pltpu.SMEM)
    hbm = pl.BlockSpec(memory_space=pl.ANY)
    sems = []
    for n in (0, 8, 8, 8, 4, 8, 0, 0, 4, 0, 0, 8, 0, 0, 0, 16, 0):
        for _ in range(2):
            sems.append(pltpu.SemaphoreType.DMA((n,)) if n else pltpu.SemaphoreType.DMA)
    out_shape = (
        jax.ShapeDtypeStruct((160, D), F32),
        jax.ShapeDtypeStruct((40, D), F32),
        jax.ShapeDtypeStruct((18, 288), F32),
        jax.ShapeDtypeStruct((18, 288), F32),
    )
    results = pl.pallas_call(
        kernel,
        out_shape=out_shape,
        in_specs=[smem, smem, hbm, hbm, hbm, hbm, hbm],
        out_specs=(hbm, hbm, hbm, hbm),
        scratch_shapes=[
            pltpu.VMEM((160, D), BF),
            pltpu.VMEM((40, D), BF),
            pltpu.VMEM((D, D), BF),
            pltpu.VMEM((D, D), BF),
            pltpu.VMEM((D, D), BF),
            pltpu.VMEM((160, D), F32),
            pltpu.VMEM((40, D), F32),
            pltpu.VMEM((18, 288), F32),
            pltpu.VMEM((18, 288), F32),
            pltpu.VMEM((2, 40, D), F32),
            pltpu.VMEM((80, D), F32),
            pltpu.VMEM((40, D), F32),
            pltpu.VMEM((640, D), BF),
            pltpu.VMEM((640, D), BF),
            pltpu.VMEM((640, 640), BF),
            pltpu.VMEM((640, D), F32),
            pltpu.VMEM((640, D), F32),
            pltpu.VMEM((4, 80, D), BF),
            pltpu.VMEM((4, 80, D), BF),
            pltpu.VMEM((16, 368, 128), BF),
            pltpu.VMEM((4, 80, D), BF),
            pltpu.VMEM((4, 80, D), BF),
            pltpu.VMEM((80, D), F32),
            pltpu.VMEM((40, D), F32),
            pltpu.VMEM((16, 368, 128), BF),
            pltpu.VMEM((4, 368, 128), BF),
            pltpu.VMEM((4, 96, 128), BF),
            pltpu.VMEM((16, 96, 128), BF),
            pltpu.VMEM((4, 96, 128), BF),
            pltpu.VMEM((16, 96, 128), BF),
            pltpu.VMEM((4, 96, 128), BF),
            pltpu.VMEM((16, 96, 128), BF),
            pltpu.VMEM((4, 96, 128), BF),
            pltpu.VMEM((16, 96, 128), BF),
            pltpu.VMEM((384, 384), F32),
            pltpu.VMEM((384, 384), F32),
            pltpu.VMEM((8, 64, 128), BF),
            pltpu.VMEM((8, 64, 128), BF),
            pltpu.VMEM((8, 64, 128), BF),
            pltpu.VMEM((8, 64, 128), BF),
            pltpu.VMEM((16, 64, 128), BF),
            pltpu.VMEM((16, 64, 128), BF),
            *sems,
            pltpu.SemaphoreType.DMA((9,)),
        ],
        compiler_params=pltpu.CompilerParams(
            collective_id=0, has_side_effects=True, vmem_limit_bytes=56 * 2**20
        ),
        cost_estimate=pl.CostEstimate(
            flops=4 * 10**9, bytes_accessed=8 * 10**6, transcendentals=409600
        ),
    )(logit_scale, logit_bias, image_feats, text_feats, image_proj, text_proj, order)
    return pl.pallas_call(
        hand_over,
        out_shape=out_shape,
        in_specs=[hbm, hbm, hbm, hbm],
        out_specs=(hbm, hbm, hbm, hbm),
        scratch_shapes=[
            *(pltpu.VMEM(shape.shape, F32) for shape in out_shape),
            pltpu.SemaphoreType.DMA((8,)),
        ],
    )(*results)


def solution(mesh):
    placed = (P("group", None), P(("blk", "group"), None), P(), P(), P(), P())
    return jax.shard_map(
        per_device,
        mesh=mesh,
        in_specs=placed,
        out_specs=(
            P("group", None),
            P(("blk", "group"), None),
            P("group", "blk"),
            P("group", "blk"),
        ),
        check_vma=False,
    )
```
